32 devices in a mesh: dp: 8 (over z, x), tensor: 4 (over y, core).
Axes of the slice: x: 2, y: 2, z: 4, core: 2. Of those that a mesh axis runs over, the one named last changes fastest.
Arguments:
- tokens: bfloat16 [16, 1024, 768], P('dp', 'tensor'), may hold values from -6 to 6
- w_qkv: bfloat16 [2, 768, 3, 768], P(None, 'dp', None, 'tensor'), may hold values from -0.21875 to 0.21875
- w_out: bfloat16 [2, 768, 768], P(None, 'tensor', 'dp'), may hold values from -0.875 to 0.875
- w_up: bfloat16 [2, 768, 3072], P(None, 'dp', 'tensor'), may hold values from -0.21875 to 0.21875
- w_down: bfloat16 [2, 3072, 768], P(None, 'tensor', 'dp'), may hold values from -0.109375 to 0.109375
- norm_gain: bfloat16 [2, 2, 768], P(None, None, 'dp'), may hold values from 0.5 to 1.5
- norm_bias: bfloat16 [2, 2, 768], P(None, None, 'dp'), may hold values from -1.5 to 1.5
- seg_table: bfloat16 [8, 768], P(None, 'dp'), may hold values from -4 to 4
- seg_ids: int32 [16, 8], P('dp', 'tensor'), may hold values from 0 to 7
- cotangent: bfloat16 [16, 1024, 768], P('dp', 'tensor'), may hold values from -6 to 6
Outputs:
- result: bfloat16 [16, 1024, 768], P('dp', 'tensor')
- grad_tokens: float32 [16, 1024, 768], P('dp', 'tensor')
- grad_qkv: float32 [2, 768, 3, 768], P(None, 'dp', None, 'tensor')
- grad_out: float32 [2, 768, 768], P(None, 'tensor', 'dp')
- grad_up: float32 [2, 768, 3072], P(None, 'dp', 'tensor')
- grad_down: float32 [2, 3072, 768], P(None, 'tensor', 'dp')
- grad_gain: float32 [2, 2, 768], P(None, None, 'dp')
- grad_bias: float32 [2, 2, 768], P(None, None, 'dp')
- grad_table: float32 [8, 768], P(None, 'dp')
The draws below stay inside these ranges and needn't reach their ends.
Inputs may be any that keep to these rules, and one draw needn't show every extreme that they name: `seg_ids`: one table row for each segment.
All inputs are finite; a program needn't handle non-finite values.
Results may differ from the reference program's by a relative error of at most 0.025.
Values may be sent and summed in bfloat16 or wider, within the bound.
No kernel may reach another device: no remote copies, remote signals or barrier semaphores. Data moves between devices by JAX's collectives and lax.ppermute only.
A program may use at most 128 MiB of HBM per device.

```python
import math
import jax
import jax.numpy as jnp
from jax import lax

D = 768
HEADS = 12
FF = 3072
SEG = 128
NSEG = 8
NPOS = 8
LEN = 1024
SEQS = 16


def place_ends(values, rng, low, largest):
    longest = values.shape.index(max(values.shape))
    spots = []
    for shift in (0, 1):
        where = [jax.random.randint(jax.random.fold_in(rng, axis), (), 0, length) for axis, length in enumerate(values.shape)]
        where[longest] = (where[longest] + shift) % values.shape[longest]
        spots.append(tuple(where))
    return values.at[spots[0]].set(low).at[spots[1]].set(largest)


def levels(rng, extent, pieces, smallest, high):
    gain, own = 1.0, jax.random.fold_in(rng, 6)
    for axis_at, blocks in pieces:
        heights = jnp.exp(jax.random.uniform(jax.random.fold_in(own, axis_at), (blocks,), jnp.float32, smallest / len(pieces), high / len(pieces)))
        gain = gain * jnp.repeat(heights, extent[axis_at] // blocks).reshape([-1 if axis == axis_at else 1 for axis in range(len(extent))])
    return gain


def noise(own_key, extent, scale, limit, cuts=(), held_as=jnp.bfloat16):
    drawn = jax.random.normal(own_key, extent, jnp.float32) * scale
    if len(cuts) > 0:
        drawn = levels(own_key, extent, cuts, -0.22, 0.18) * drawn
    return jnp.clip(drawn, min=-limit, max=limit).astype(held_as)


def setup_inputs(seed: int = 0) -> dict:
    key_of = jax.random.split(jax.random.key(seed), 11)
    return {
        "tokens": noise(key_of[0], (SEQS, LEN, D), 1.0, 6.0, ((0, 8), (1, 4))),
        "w_qkv": noise(key_of[1], (2, D, 3, D), D ** -0.5, 0.21875, ((1, 8), (3, 4))),
        "w_out": noise(key_of[2], (2, D, D), (D // 16) ** -0.5, 0.875, ((1, 4), (2, 8))),
        "w_up": noise(key_of[3], (2, D, FF), D ** -0.5, 0.21875, ((1, 8), (2, 4))),
        "w_down": noise(key_of[4], (2, FF, D), FF ** -0.5, 0.109375, ((1, 4), (2, 8))),
        "norm_gain": jnp.clip(1.0 + 0.1 * jax.random.normal(key_of[5], (2, 2, D), jnp.float32), 0.5, 1.5).astype(jnp.bfloat16),
        "norm_bias": noise(key_of[6], (2, 2, D), 0.3, 1.5, ((2, 8),)),
        "seg_table": noise(key_of[7], (NPOS, D), 1.0, 4.0, ((1, 8),)),
        "seg_ids": place_ends(jax.random.randint(key_of[8], (SEQS, NSEG), 0, NPOS), jax.random.fold_in(key_of[8], 1), 0, NPOS - 1).astype(jnp.int32),
        "cotangent": noise(key_of[9], (SEQS, LEN, D), 1.0, 6.0, ((0, 8), (1, 4))),
    }


@jax.custom_vjp
def low(v):
    return lax.optimization_barrier(v.astype(jnp.bfloat16)).astype(jnp.float32)

@jax.custom_vjp
def low_back(v):
    return v

def low_keep(v):
    return (low(v), None)

def low_pass(kept, grad):
    return (grad,)

def back_keep(v):
    return (v, None)

def back_low(kept, grad):
    return (low(grad),)
low.defvjp(low_keep, low_pass)
low_back.defvjp(back_keep, back_low)
highest = lax.Precision.HIGHEST

def layer_norm(hidden, gain_row, offset):
    center = hidden - lax.optimization_barrier(jnp.mean(hidden, axis=-1, keepdims=True))
    spread = lax.optimization_barrier(jnp.mean(center * center, axis=-1, keepdims=True))
    return center * lax.rsqrt(spread + 1e-05) * gain_row + offset

def attend(queries, key_rows, values, group_len):
    batch_count, row_count, head_count, head_width = queries.shape
    grouped = (batch_count, row_count // group_len, group_len, head_count, head_width)
    scores = jnp.einsum('bnqhe,bnkhe->bnhqk', queries.reshape(grouped), key_rows.reshape(grouped), precision=highest) * head_width ** (-0.5)
    scores = low_back(scores)
    probs = jax.nn.softmax(scores, axis=-1)
    weighted = jnp.einsum('bnhqk,bnkhe->bnqhe', low(probs), values.reshape(grouped), precision=highest)
    return weighted.reshape(batch_count, row_count, head_count * head_width)

def block(hidden_in, w_qkv, w_out, w_up, w_down, gains, offsets, group_len):
    batch_count, row_count = (hidden_in.shape[0], hidden_in.shape[1])
    sent = low(hidden_in)
    project = jnp.einsum('btd,dch->btch', sent, w_qkv, precision=highest)
    project = low(low_back(project))
    split = project.reshape(batch_count, row_count, 3, HEADS, D // HEADS)
    context = attend(split[:, :, 0], split[:, :, 1], split[:, :, 2], group_len)
    context = low(low_back(context))
    branch = low_back(jnp.einsum('btk,kd->btd', context, w_out, precision=highest))
    normed = layer_norm(hidden_in + branch, gains[0], offsets[0])
    upward = low_back(jnp.einsum('btd,df->btf', low(normed), w_up, precision=highest))
    activated = low(jax.nn.gelu(upward, approximate=False))
    mlp_out = low_back(jnp.einsum('btf,fd->btd', activated, w_down, precision=highest))
    return layer_norm(normed + mlp_out, gains[1], offsets[1])

def whole_layer(tokens32, w_qkv, w_out, w_up, w_down, gains, offsets, table, segment_ids):
    segment_out = block(tokens32, w_qkv[0], w_out[0], w_up[0], w_down[0], gains[0], offsets[0], SEG)
    leaders = segment_out[:, ::SEG]
    onehot = (segment_ids[..., None] == jnp.arange(NPOS, dtype=jnp.int32)).astype(jnp.float32)
    placed = leaders + jnp.einsum('bsp,pd->bsd', onehot, table, precision=highest)
    cross = block(placed, w_qkv[1], w_out[1], w_up[1], w_down[1], gains[1], offsets[1], NSEG)
    return segment_out.at[:, ::SEG].set(cross)

def reference(tokens, w_qkv, w_out, w_up, w_down, norm_gain, norm_bias, seg_table, seg_ids, cotangent):
    params = tuple((item.astype(jnp.float32) for item in (w_qkv, w_out, w_up, w_down, norm_gain, norm_bias, seg_table)))
    group_size = math.gcd(SEQS, 4)
    group_count = SEQS // group_size
    token_groups = tokens.reshape(group_count, group_size, LEN, D)
    cot_groups = cotangent.reshape(group_count, group_size, LEN, D)
    id_groups = seg_ids.reshape(group_count, group_size, NSEG)

    def one_group(totals, items):
        token_part, cot_part, id_part = items

        def forward(token_float, *weights):
            return whole_layer(token_float, *weights, id_part)
        output, pullback = jax.vjp(forward, token_part.astype(jnp.float32), *params)
        grads = pullback(cot_part.astype(jnp.float32))
        totals = tuple((total + part for total, part in zip(totals, grads[1:])))
        return (totals, (output.astype(jnp.bfloat16), grads[0]))
    zeros = tuple((jnp.zeros(item.shape, jnp.float32) for item in params))
    totals, (outputs, grad_parts) = lax.scan(one_group, zeros, (token_groups, cot_groups, id_groups))
    return (outputs.reshape(SEQS, LEN, D), grad_parts.reshape(SEQS, LEN, D), totals[0], totals[1], totals[2], totals[3], totals[4], totals[5], totals[6])
```

```python
import functools
import math

import jax
import jax.numpy as jnp
from jax import lax
from jax.experimental import pallas as pl
from jax.experimental.pallas import tpu as pltpu
from jax.sharding import PartitionSpec as P

HEAD = 64
SEG = 128
GROUP = 8
F32, BF16 = jnp.float32, jnp.bfloat16
VMEM = pltpu.VMEM
ANY = pl.BlockSpec(memory_space=pl.ANY)
WHOLE = pl.BlockSpec(memory_space=pltpu.VMEM)
SMEM = pl.BlockSpec(memory_space=pltpu.SMEM)
PARAMS = pltpu.CompilerParams(vmem_limit_bytes=60 << 20)
EPS = 1e-05
SCALE = HEAD ** (-0.5)
RSQRT2 = 1.0 / math.sqrt(2.0)
RSQRT2PI = 1.0 / math.sqrt(2.0 * math.pi)


def nn(a, b):
    return lax.dot_general(a, b, (((1,), (0,)), ((), ())), preferred_element_type=F32)


def nt(a, b):
    return lax.dot_general(a, b, (((1,), (1,)), ((), ())), preferred_element_type=F32)


def tn(a, b):
    return lax.dot_general(a, b, (((0,), (0,)), ((), ())), preferred_element_type=F32)


def norm_parts(h):
    center = h - jnp.mean(h, axis=-1, keepdims=True)
    rstd = lax.rsqrt(jnp.mean(center * center, axis=-1, keepdims=True) + EPS)
    return center * rstd, rstd


def norm_back(grad, normed, rstd, gain):
    dn = grad * gain
    return rstd * (
        dn
        - jnp.mean(dn, axis=-1, keepdims=True)
        - normed * jnp.mean(dn * normed, axis=-1, keepdims=True)
    )


def gelu_both(u):
    cdf = 0.5 + 0.5 * lax.erf(u * RSQRT2)
    return u * cdf, cdf + u * (jnp.exp(-0.5 * u * u) * RSQRT2PI)


def halves(pair):
    lane = lax.broadcasted_iota(jnp.int32, pair.shape, 1)
    zero = jnp.zeros_like(pair)
    return jnp.concatenate(
        [jnp.where(lane < HEAD, pair, zero), jnp.where(lane < HEAD, zero, pair)], axis=0
    )


def unhalve(stacked):
    lane = lax.broadcasted_iota(jnp.int32, (SEG, 2 * HEAD), 1)
    return jnp.where(lane < HEAD, stacked[:SEG], stacked[SEG:])


def half_softmax(s):
    top = jnp.concatenate(
        [
            jnp.broadcast_to(jnp.max(s[:, :SEG], axis=-1, keepdims=True), (SEG, SEG)),
            jnp.broadcast_to(jnp.max(s[:, SEG:], axis=-1, keepdims=True), (SEG, SEG)),
        ],
        axis=1,
    )
    ex = jnp.exp(s - top)
    inv = jnp.concatenate(
        [
            jnp.broadcast_to(1.0 / jnp.sum(ex[:, :SEG], axis=-1, keepdims=True), (SEG, SEG)),
            jnp.broadcast_to(1.0 / jnp.sum(ex[:, SEG:], axis=-1, keepdims=True), (SEG, SEG)),
        ],
        axis=1,
    )
    return ex * inv


def call(body, outs, out_specs, in_specs, scratch=(), flops=0, nbytes=0):
    return pl.pallas_call(
        body,
        out_shape=outs,
        in_specs=in_specs,
        out_specs=out_specs,
        scratch_shapes=list(scratch),
        compiler_params=PARAMS,
        cost_estimate=pl.CostEstimate(
            flops=int(flops), bytes_accessed=int(nbytes), transcendentals=0
        ),
    )


def sds(shape, dtype):
    return jax.ShapeDtypeStruct(shape, dtype)


def fetch(plan, pieces, packs, blk_ref, dst, sems):
    by_j = [[], [], [], []]
    n = 0
    for which, lead, j, slot in plan:
        for p in range(packs):
            src = pieces[which]
            if slot is None:
                src, to = src.at[j, p], dst.at[p, j]
            else:
                src = src.at[(*lead, p)]
                rows = src.shape[0]
                to = dst.at[p, j, pl.ds(pl.multiple_of(blk_ref[slot] * rows, 16), rows)]
            copy = pltpu.make_async_copy(src, to, sems.at[n])
            copy.start()
            by_j[j].append(copy)
            n += 1
    return by_j


def n_copies(plan, packs):
    return len(plan) * packs


def attn_forward(plan, n_pieces, blk, x, nv, pieces):
    rows, d = x.shape
    segs, quarter = rows // SEG, d // 4

    def body(blk_ref, x_ref, nv_ref, *refs):
        ins, refs = refs[:n_pieces], refs[n_pieces:]
        (w_out, q_ref, k_ref, v_ref, o_ref, p_ref, xt_ref, y_ref, n_ref, r_ref, yl_ref) = refs[:11]
        raw, w, sems, wsem = refs[11:]
        copies = fetch(plan, ins, 1, blk_ref, raw, sems)
        xt_ref[...] = x_ref[...].T
        for j in range(4):
            for c in copies[j]:
                c.wait()
        for t in range(4):
            for half in range(2):
                a = raw[0, 2 * half, :, t * quarter : (t + 1) * quarter]
                b = raw[0, 2 * half + 1, :, t * quarter : (t + 1) * quarter]
                w[t, :, 2 * half * quarter : 2 * (half + 1) * quarter] = jnp.concatenate(
                    [a, b], axis=1
                )
        save = pltpu.make_async_copy(w, w_out, wsem)
        save.start()
        q_ref[...] = nn(x_ref[...], w[0]).astype(BF16)
        k_ref[...] = nn(x_ref[...], w[1]).astype(BF16)
        v_ref[...] = nn(x_ref[...], w[2]).astype(BF16)

        def seg(t, _):
            at = pl.ds(pl.multiple_of(t * SEG, SEG), SEG)
            for pair in range(d // SEG):
                cols = slice(pair * SEG, (pair + 1) * SEG)
                s = nt(q_ref[at, cols], halves(k_ref[at, cols])) * SCALE
                p = half_softmax(s).astype(BF16)
                p_ref[t, pair] = p
                o_ref[at, cols] = nn(p, halves(v_ref[at, cols])).astype(BF16)
            return 0

        lax.fori_loop(0, segs, seg, 0)
        y_ref[...] = nt(o_ref[...], w[3])

        def ln(t, _):
            at = pl.ds(pl.multiple_of(t * SEG, SEG), SEG)
            n, r = norm_parts(x_ref[at].astype(F32) + y_ref[at])
            y = n * nv_ref[0:1] + nv_ref[4:5]
            y_ref[at] = y
            n_ref[at] = n.astype(BF16)
            r_ref[at] = r
            yl_ref[t] = y[0:8]
            return 0

        lax.fori_loop(0, segs, ln, 0)
        save.wait()

    outs = (
        sds((4, d, d), BF16),
        *(sds((rows, d), BF16) for _ in range(4)),
        sds((segs, d // SEG, SEG, 2 * SEG), BF16),
        sds((d, rows), BF16),
        sds((rows, d), F32),
        sds((rows, d), BF16),
        sds((rows, 1), F32),
        sds((segs, 8, d), F32),
    )
    return call(
        body,
        outs,
        (ANY,) + (WHOLE,) * 10,
        [SMEM, WHOLE, WHOLE] + [ANY] * n_pieces,
        [
            VMEM((1, 4, d, d), BF16),
            VMEM((4, d, d), BF16),
            pltpu.SemaphoreType.DMA((n_copies(plan, 1),)),
            pltpu.SemaphoreType.DMA,
        ],
        flops=2 * rows * d * d * 4,
        nbytes=20e6,
    )(blk, x, nv, *pieces)


def mlp_forward(plan, n_pieces, blk, y, lead_y, cot, nv, pieces):
    rows, d = y.shape
    leads = lead_y.shape[0]
    total = rows + leads
    tile = total if total <= 640 else 512
    assert total % tile == 0

    def body(blk_ref, y_ref, yl_ref, cot_ref, nv_ref, *refs):
        ins, refs = refs[:n_pieces], refs[n_pieces:]
        (w_out, gb_out, gp_out, ybt_ref, dmt_ref, dm_ref, dh_ref, res_ref, sums_ref) = refs[:9]
        zl_ref, nl_ref, rl_ref, ybl_ref = refs[9:13]
        w, yb, m, gb, gp, sems, wsem, gsem = refs[13:]
        copies = fetch(plan, ins, 2, blk_ref, w, sems)
        yb[0:rows] = y_ref[...].astype(BF16)
        yb[rows:total] = yl_ref[...].astype(BF16)
        ybl_ref[...] = yb[rows:total]
        ybt_ref[...] = yb[0:rows].T
        saves = []
        for j in range(4):
            for c in copies[j]:
                c.wait()
            if j >= 2:
                saves[2 * (j - 2)].wait()
                saves[2 * (j - 2) + 1].wait()

            def up(t, _, j=j):
                at = pl.ds(pl.multiple_of(t * tile, 16), tile)
                g, gd = gelu_both(nn(yb[at], w[0, j]))
                gb[j % 2, at] = g.astype(BF16)
                gp[j % 2, at] = gd.astype(BF16)
                part = nt(gb[j % 2, at], w[1, j])
                m[at] = part if j == 0 else m[at] + part
                return 0

            if total == tile:
                up(0, 0)
            else:
                lax.fori_loop(0, total // tile, up, 0)
            for buf, out, at in ((gb, gb_out, 0), (gp, gp_out, 1)):
                saves.append(
                    pltpu.make_async_copy(buf.at[j % 2], out.at[j], gsem.at[2 * j + at])
                )
                saves[-1].start()
        save = pltpu.make_async_copy(w, w_out, wsem)
        save.start()
        gain, bias = nv_ref[1:2], nv_ref[5:6]
        sums_ref[...] = jnp.zeros_like(sums_ref)

        def main(t, _):
            at = pl.ds(pl.multiple_of(t * SEG, SEG), SEG)
            n, r = norm_parts(y_ref[at] + m[at])
            res_ref[at] = (n * gain + bias).astype(BF16)
            row = lax.broadcasted_iota(jnp.int32, (SEG, d), 0)
            grad = jnp.where(row == 0, 0.0, cot_ref[at].astype(F32))
            sums_ref[0:1] += jnp.sum(grad * n, axis=0, keepdims=True)
            sums_ref[1:2] += jnp.sum(grad, axis=0, keepdims=True)
            dh = norm_back(grad, n, r, gain)
            dh_ref[at] = dh
            dm_ref[at] = dh.astype(BF16)
            return 0

        lax.fori_loop(0, rows // SEG, main, 0)

        def lead(t, _):
            at = pl.ds(pl.multiple_of(t * SEG, SEG), SEG)
            n, r = norm_parts(
                yl_ref[at].astype(F32) + m[pl.ds(pl.multiple_of(rows + t * SEG, SEG), SEG)]
            )
            zl_ref[at] = n * gain + bias
            nl_ref[at] = n
            rl_ref[at] = r
            return 0

        lax.fori_loop(0, leads // SEG, lead, 0)
        dmt_ref[...] = dm_ref[...].T
        for s in saves[4:]:
            s.wait()
        save.wait()

    outs = (
        sds((2, 4, d, d), BF16),
        sds((4, total, d), BF16),
        sds((4, total, d), BF16),
        sds((d, rows), BF16),
        sds((d, rows), BF16),
        sds((rows, d), BF16),
        sds((rows, d), F32),
        sds((rows, d), BF16),
        sds((8, d), F32),
        sds((leads, d), F32),
        sds((leads, d), F32),
        sds((leads, 1), F32),
        sds((leads, d), BF16),
    )
    return call(
        body,
        outs,
        (ANY, ANY, ANY) + (WHOLE,) * 10,
        [SMEM] + [WHOLE] * 4 + [ANY] * n_pieces,
        [
            VMEM((2, 4, d, d), BF16),
            VMEM((total, d), BF16),
            VMEM((total, d), F32),
            VMEM((2, total, d), BF16),
            VMEM((2, total, d), BF16),
            pltpu.SemaphoreType.DMA((n_copies(plan, 2),)),
            pltpu.SemaphoreType.DMA,
            pltpu.SemaphoreType.DMA((8,)),
        ],
        flops=2 * total * d * d * 8,
        nbytes=40e6,
    )(blk, y, lead_y, cot, nv, *pieces)


def put_blocks(blocked, blk_ref, src, out, lead, sems, base, slots):
    if not blocked:
        copies = [pltpu.make_async_copy(src, out.at[lead], sems.at[base])]
    else:
        rows = src.shape[0] // slots
        copies = [
            pltpu.make_async_copy(
                src.at[pl.ds(pl.multiple_of(blk_ref[s] * rows, 16), rows)],
                out.at[(lead[0], s, lead[1], pl.ds(0, rows))],
                sems.at[base + s],
            )
            for s in range(slots)
        ]
    for c in copies:
        c.start()
    return copies


def mlp_backward(core, slots, blocked, blk, dm, dmt, ybt, gb, gp, w, start):
    rows, d = dm.shape
    dblk = d // slots
    per = slots if blocked else 1

    def body(blk_ref, dm_ref, dmt_ref, ybt_ref, gb_hbm, gp_hbm, w_hbm, start_ref, g_out, dy_ref, *scr):
        gb_s, gp_s, w_s, du_s, gr, sin, sout = scr
        loads = []
        for y in range(2):
            j = 2 * core + y
            pair = [
                (gb_hbm.at[j, pl.ds(0, rows)], gb_s.at[y]),
                (gp_hbm.at[j, pl.ds(0, rows)], gp_s.at[y]),
                (w_hbm.at[1, j], w_s.at[y, 1]),
                (w_hbm.at[0, j], w_s.at[y, 0]),
            ]
            loads.append(
                [pltpu.make_async_copy(a, b, sin.at[4 * y + i]) for i, (a, b) in enumerate(pair)]
            )
            for c in loads[-1]:
                c.start()
        outs = []
        for y in range(2):
            for c in loads[y]:
                c.wait()
            dg = nn(dm_ref[...], w_s[y, 1])
            du_s[...] = (dg * gp_s[y].astype(F32)).astype(BF16)
            gr[y, 1] = nn(dmt_ref[...], gb_s[y]).astype(BF16)
            outs += put_blocks(
                blocked, blk_ref, gr.at[y, 1], g_out, (y, 1), sout, (2 * y) * per, slots
            )
            gr[y, 0] = nn(ybt_ref[...], du_s[...]).astype(BF16)
            outs += put_blocks(
                blocked, blk_ref, gr.at[y, 0], g_out, (y, 0), sout, (2 * y + 1) * per, slots
            )
            part = nt(du_s[...], w_s[y, 0])
            dy_ref[...] = (start_ref[...] if y == 0 else dy_ref[...]) + part
        for c in outs:
            c.wait()

    g_shape = (2, slots, 2, dblk, d) if blocked else (2, 2, d, d)
    return call(
        body,
        (sds(g_shape, BF16), sds((rows, d), F32)),
        (ANY, WHOLE),
        [SMEM, WHOLE, WHOLE, WHOLE, ANY, ANY, ANY, WHOLE],
        [
            VMEM((2, rows, d), BF16),
            VMEM((2, rows, d), BF16),
            VMEM((2, 2, d, d), BF16),
            VMEM((rows, d), BF16),
            VMEM((2, 2, d, d), BF16),
            pltpu.SemaphoreType.DMA((8,)),
            pltpu.SemaphoreType.DMA((4 * per,)),
        ],
        flops=2 * rows * d * d * 8,
        nbytes=20e6,
    )(blk, dm, dmt, ybt, gb, gp, w, start)


def attn_norm_back(dy, lead_dy, n1, r1, nv, sums2):
    rows, d = dy.shape

    def body(dy_ref, ld_ref, n_ref, r_ref, nv_ref, s2_ref, dh_ref, da_ref, dat_ref, sums_ref):
        sums_ref[0:2] = jnp.zeros((2, d), F32)
        sums_ref[2:4] = s2_ref[0:2]
        sums_ref[4:8] = jnp.zeros((4, d), F32)

        def one(t, _):
            at = pl.ds(pl.multiple_of(t * SEG, SEG), SEG)
            row = lax.broadcasted_iota(jnp.int32, (SEG, d), 0)
            grad = dy_ref[at] + jnp.where(row == 0, ld_ref[t][0:1], 0.0)
            n = n_ref[at].astype(F32)
            sums_ref[0:1] += jnp.sum(grad * n, axis=0, keepdims=True)
            sums_ref[1:2] += jnp.sum(grad, axis=0, keepdims=True)
            dh = norm_back(grad, n, r_ref[at], nv_ref[0:1])
            dh_ref[at] = dh
            da_ref[at] = dh.astype(BF16)
            return 0

        lax.fori_loop(0, rows // SEG, one, 0)
        dat_ref[...] = da_ref[...].T

    return call(
        body,
        (sds((rows, d), F32), sds((rows, d), BF16), sds((d, rows), BF16), sds((8, d), F32)),
        (WHOLE,) * 4,
        [WHOLE] * 6,
        flops=rows * d * 20,
        nbytes=8e6,
    )(dy, lead_dy, n1, r1, nv, sums2)


def attn_backward(core, slots, blocked, blk, da, dat, xt, q, k, v, o, p, w, start, sums):
    rows, d = da.shape
    segs, half, quarter = rows // SEG, d // 2, d // 4
    dblk = d // slots
    per = slots if blocked else 1
    pairs = half // SEG

    def body(blk_ref, da_ref, dat_ref, xt_ref, q_ref, k_ref, v_ref, o_ref, p_ref, w_hbm, start_ref,
             sums_ref, g_out, dx_ref, *scr):
        w_s, do_s, dq_s, dk_s, dv_s, gf, gr, ex, sin, sout = scr
        load = pltpu.make_async_copy(w_hbm, w_s, sin)
        load.start()
        if blocked:
            for b in range(slots):
                piece = sums_ref[:, b * dblk : (b + 1) * dblk]
                ex[b] = jnp.zeros((16, d), BF16)
                ex[b, 0:8, 0:dblk] = piece.astype(BF16)
        load.wait()
        cols = slice(core * half, (core + 1) * half)
        do_s[...] = nn(da_ref[...], w_s[3, :, cols]).astype(BF16)
        gf[3] = nn(dat_ref[...], o_ref[:, cols]).astype(BF16)

        def seg(t, _):
            at = pl.ds(pl.multiple_of(t * SEG, SEG), SEG)
            for pair in range(pairs):
                mine = slice(pair * SEG, (pair + 1) * SEG)
                wide = slice(core * half + pair * SEG, core * half + (pair + 1) * SEG)
                dout = do_s[at, mine]
                prob = p_ref[t, core * pairs + pair]
                pf = prob.astype(F32)
                dp = nt(dout, halves(v_ref[at, wide]))
                pd = pf * dp
                total = jnp.concatenate(
                    [
                        jnp.broadcast_to(jnp.sum(pd[:, :SEG], axis=-1, keepdims=True), (SEG, SEG)),
                        jnp.broadcast_to(jnp.sum(pd[:, SEG:], axis=-1, keepdims=True), (SEG, SEG)),
                    ],
                    axis=1,
                )
                ds = (pd - pf * total).astype(BF16)
                dv_s[at, mine] = unhalve(tn(prob, dout)).astype(BF16)
                dq_s[at, mine] = (nn(ds, halves(k_ref[at, wide])) * SCALE).astype(BF16)
                dk_s[at, mine] = (unhalve(tn(ds, q_ref[at, wide])) * SCALE).astype(BF16)
            return 0

        lax.fori_loop(0, segs, seg, 0)
        for t, s in enumerate((dq_s, dk_s, dv_s)):
            gf[t] = nn(xt_ref[...], s[...]).astype(BF16)
        outs = []
        for y in range(2):
            for t in range(4):
                gr[y, :, t * quarter : (t + 1) * quarter] = gf[t, :, y * quarter : (y + 1) * quarter]
            outs += put_blocks(blocked, blk_ref, gr.at[y], g_out, (y, 0), sout, y * per, slots)
            if blocked:
                for s in range(slots):
                    c = pltpu.make_async_copy(
                        ex.at[blk_ref[s]],
                        g_out.at[y, s, 0, pl.ds(dblk, 16)],
                        sout.at[2 * per + y * slots + s],
                    )
                    c.start()
                    outs.append(c)
        dx_ref[...] = (
            start_ref[...]
            + nt(dq_s[...], w_s[0, :, cols])
            + nt(dk_s[...], w_s[1, :, cols])
            + nt(dv_s[...], w_s[2, :, cols])
        )
        for c in outs:
            c.wait()

    g_shape = (2, slots, 1, dblk + 16, d) if blocked else (2, 1, d, d)
    return call(
        body,
        (sds(g_shape, BF16), sds((rows, d), F32)),
        (ANY, WHOLE),
        [SMEM] + [WHOLE] * 8 + [ANY, WHOLE, WHOLE],
        [
            VMEM((4, d, d), BF16),
            *(VMEM((rows, half), BF16) for _ in range(4)),
            VMEM((4, d, half), BF16),
            VMEM((2, d, d), BF16),
            VMEM((slots if blocked else 1, 16, d), BF16),
            pltpu.SemaphoreType.DMA,
            pltpu.SemaphoreType.DMA((4 * per,)),
        ],
        flops=2 * rows * d * half * 8,
        nbytes=20e6,
    )(blk, da, dat, xt, q, k, v, o, p, w, start, sums)


def group_mask():
    a = lax.broadcasted_iota(jnp.int32, (SEG, SEG), 0) // GROUP
    b = lax.broadcasted_iota(jnp.int32, (SEG, SEG), 1) // GROUP
    return a == b


def cross_attn(zl, onehot, nv, w):
    rows, d = zl.shape
    quarter = d // 4
    heads = quarter // HEAD
    tiles = rows // SEG

    def body(z_ref, oh_ref, nv_ref, w_ref, c_ref, qkv_ref, o_ref, p_ref, a_ref):
        def one(t, _):
            at = pl.ds(pl.multiple_of(t * SEG, SEG), SEG)
            c = z_ref[at]
            for i in range(8):
                c += oh_ref[at, i : i + 1].astype(F32) * nv_ref[8 + i : 9 + i]
            c_ref[at] = c
            qkv = nn(c.astype(BF16), w_ref[:, : 3 * quarter]).astype(BF16)
            qkv_ref[at] = qkv
            mask = group_mask()
            os = []
            for h in range(heads):
                q, k, v = (
                    qkv[:, i * quarter + h * HEAD : i * quarter + (h + 1) * HEAD] for i in range(3)
                )
                s = jnp.where(mask, nt(q, k) * SCALE, -1e30)
                ex = jnp.exp(s - jnp.max(s, axis=-1, keepdims=True))
                p = (ex / jnp.sum(ex, axis=-1, keepdims=True)).astype(BF16)
                p_ref[t, h] = p
                os.append(nn(p, v).astype(BF16))
            o = jnp.concatenate(os, axis=1)
            o_ref[at] = o
            a_ref[at] = nt(o, w_ref[:, 3 * quarter :]).astype(BF16)
            return 0

        lax.fori_loop(0, tiles, one, 0)

    return call(
        body,
        (
            sds((rows, d), F32),
            sds((rows, 3 * quarter), BF16),
            sds((rows, quarter), BF16),
            sds((tiles, heads, SEG, SEG), BF16),
            sds((rows, d), BF16),
        ),
        (WHOLE,) * 5,
        [WHOLE] * 4,
        flops=2 * rows * d * d,
        nbytes=3e6,
    )(zl, onehot, nv, w)


def cross_mlp(c, a0, a1, nv, w):
    rows, d = c.shape

    def body(c_ref, a0_ref, a1_ref, nv_ref, w_ref, y_ref, n_ref, r_ref, gb_ref, gp_ref, m_ref):
        n, r = norm_parts(c_ref[...] + (a0_ref[...].astype(F32) + a1_ref[...].astype(F32)))
        n_ref[...] = n
        r_ref[...] = r
        y = n * nv_ref[2:3] + nv_ref[6:7]
        y_ref[...] = y
        g, gd = gelu_both(nn(y.astype(BF16), w_ref[0]))
        gb_ref[...] = g.astype(BF16)
        gp_ref[...] = gd.astype(BF16)
        m_ref[...] = nt(gb_ref[...], w_ref[1]).astype(BF16)

    return call(
        body,
        (
            sds((rows, d), F32),
            sds((rows, d), F32),
            sds((rows, 1), F32),
            sds((rows, d), BF16),
            sds((rows, d), BF16),
            sds((rows, d), BF16),
        ),
        (WHOLE,) * 6,
        [WHOLE] * 5,
        flops=4 * rows * d * d,
        nbytes=5e6,
    )(c, a0, a1, nv, w)


def cross_mlp_back(y, m0, m1, cot, nv, w, gb, gp):
    rows, d = y.shape

    def body(y_ref, m0_ref, m1_ref, cot_ref, nv_ref, w_ref, gb_ref, gp_ref,
             e_ref, dh_ref, gd_ref, gu_ref, dy_ref, sums_ref):
        gain = nv_ref[3:4]
        n, r = norm_parts(y_ref[...] + (m0_ref[...].astype(F32) + m1_ref[...].astype(F32)))
        e_ref[...] = (n * gain + nv_ref[7:8]).astype(BF16)
        grad = cot_ref[...].astype(F32)
        sums_ref[...] = jnp.concatenate(
            [
                jnp.sum(grad * n, axis=0, keepdims=True),
                jnp.sum(grad, axis=0, keepdims=True),
                jnp.zeros((6, d), F32),
            ],
            axis=0,
        )
        dh = norm_back(grad, n, r, gain)
        dh_ref[...] = dh
        dm = dh.astype(BF16)
        du = (nn(dm, w_ref[1]) * gp_ref[...].astype(F32)).astype(BF16)
        dy_ref[...] = nt(du, w_ref[0]).astype(BF16)
        gd_ref[...] = tn(dm, gb_ref[...])
        gu_ref[...] = tn(y_ref[...].astype(BF16), du)

    return call(
        body,
        (
            sds((rows, d), BF16),
            sds((rows, d), F32),
            sds((d, d), F32),
            sds((d, d), F32),
            sds((rows, d), BF16),
            sds((8, d), F32),
        ),
        (WHOLE,) * 6,
        [WHOLE] * 8,
        flops=8 * rows * d * d,
        nbytes=9e6,
    )(y, m0, m1, cot, nv, w, gb, gp)


def cross_attn_back(dh2, d0, d1, n1, r1, c, qkv, o, p, nv, w):
    rows, d = dh2.shape
    quarter = d // 4
    heads = quarter // HEAD
    tiles = rows // SEG

    def body(dh2_ref, d0_ref, d1_ref, n_ref, r_ref, c_ref, qkv_ref, o_ref, p_ref, nv_ref, w_ref,
             dh_ref, dx_ref, g_ref, sums_ref, da_s, dqkv_s):
        grad = dh2_ref[...] + (d0_ref[...].astype(F32) + d1_ref[...].astype(F32))
        n = n_ref[...]
        sums_ref[...] = jnp.concatenate(
            [
                jnp.sum(grad * n, axis=0, keepdims=True),
                jnp.sum(grad, axis=0, keepdims=True),
                jnp.zeros((6, d), F32),
            ],
            axis=0,
        )
        dh = norm_back(grad, n, r_ref[...], nv_ref[2:3])
        dh_ref[...] = dh
        da_s[...] = dh.astype(BF16)
        g_ref[:, 3 * quarter :] = tn(da_s[...], o_ref[...])

        def one(t, _):
            at = pl.ds(pl.multiple_of(t * SEG, SEG), SEG)
            do = nn(da_s[at], w_ref[:, 3 * quarter :]).astype(BF16)
            qkv = qkv_ref[at]
            dq, dk, dv = [], [], []
            for h in range(heads):
                q, k, v = (
                    qkv[:, i * quarter + h * HEAD : i * quarter + (h + 1) * HEAD] for i in range(3)
                )
                doh = do[:, h * HEAD : (h + 1) * HEAD]
                prob = p_ref[t, h]
                pf = prob.astype(F32)
                pd = pf * nt(doh, v)
                ds = (pd - pf * jnp.sum(pd, axis=-1, keepdims=True)).astype(BF16)
                dv.append(tn(prob, doh).astype(BF16))
                dq.append((nn(ds, k) * SCALE).astype(BF16))
                dk.append((tn(ds, q) * SCALE).astype(BF16))
            dqkv_s[at] = jnp.concatenate(dq + dk + dv, axis=1)
            return 0

        lax.fori_loop(0, tiles, one, 0)
        dx_ref[...] = nt(dqkv_s[...], w_ref[:, : 3 * quarter]).astype(BF16)
        g_ref[:, : 3 * quarter] = tn(c_ref[...].astype(BF16), dqkv_s[...])

    return call(
        body,
        (sds((rows, d), F32), sds((rows, d), BF16), sds((d, d), F32), sds((8, d), F32)),
        (WHOLE,) * 4,
        [WHOLE] * 11,
        [VMEM((rows, d), BF16), VMEM((rows, 3 * quarter), BF16)],
        flops=4 * rows * d * d,
        nbytes=6e6,
    )(dh2, d0, d1, n1, r1, c, qkv, o, p, nv, w)


def lead_backward(dh, d0, d1, onehot, nl, rl, ybl, nv, gb, gp, w, main_rows):
    rows, d = dh.shape

    def body(dh_ref, d0_ref, d1_ref, oh_ref, n_ref, r_ref, yb_ref, nv_ref, gb_hbm, gp_hbm, w_hbm,
             dy_ref, gd_ref, gu_ref, sums_ref, gb_s, gp_s, w_s, dm_s, sin):
        loads = []
        for j in range(4):
            pair = [
                (gp_hbm.at[j, pl.ds(main_rows, rows)], gp_s.at[j]),
                (w_hbm.at[1, j], w_s.at[1, j]),
                (w_hbm.at[0, j], w_s.at[0, j]),
            ]
            loads.append(
                [pltpu.make_async_copy(a, b, sin.at[3 * j + i]) for i, (a, b) in enumerate(pair)]
            )
            for c in loads[-1]:
                c.start()
        load0 = pltpu.make_async_copy(gb_hbm.at[0, pl.ds(main_rows, rows)], gb_s, sin.at[12])
        load0.start()
        grad = dh_ref[...] + (d0_ref[...].astype(F32) + d1_ref[...].astype(F32))
        n = n_ref[...]
        tops = [jnp.sum(grad * n, axis=0, keepdims=True), jnp.sum(grad, axis=0, keepdims=True)]
        tops.append(jnp.zeros((6, d), F32))
        for i in range(8):
            tops.append(jnp.sum(oh_ref[:, i : i + 1].astype(F32) * grad, axis=0, keepdims=True))
        sums_ref[...] = jnp.concatenate(tops, axis=0)
        dy = norm_back(grad, n, r_ref[...], nv_ref[1:2])
        dy_ref[...] = dy
        dm_s[...] = dy.astype(BF16)
        load0.wait()
        gd_ref[...] = tn(dm_s[...], gb_s[...])
        for j in range(4):
            for c in loads[j]:
                c.wait()
            du = (nn(dm_s[...], w_s[1, j]) * gp_s[j].astype(F32)).astype(BF16)
            if j == 0:
                gu_ref[...] = tn(yb_ref[...], du)
            dy_ref[...] += nt(du, w_s[0, j])

    return call(
        body,
        (sds((rows, d), F32), sds((d, d), F32), sds((d, d), F32), sds((16, d), F32)),
        (WHOLE,) * 4,
        [WHOLE] * 8 + [ANY] * 3,
        [
            VMEM((rows, d), BF16),
            VMEM((4, rows, d), BF16),
            VMEM((2, 4, d, d), BF16),
            VMEM((rows, d), BF16),
            pltpu.SemaphoreType.DMA((13,)),
        ],
        flops=2 * rows * d * d * 10,
        nbytes=14e6,
    )(dh, d0, d1, onehot, nl, rl, ybl, nv, gb, gp, w)


def swap(axis, size, bit, value):
    return lax.ppermute(value, axis, [(i, i ^ bit) for i in range(size)])


core_swap = functools.partial(swap, "tensor", 4, 1)
y_swap = functools.partial(swap, "tensor", 4, 2)
x_swap = functools.partial(swap, "dp", 8, 1)


def z_swap(k, value):
    return swap("dp", 8, 2 * k, value)


def tied(*trees):
    return lax.optimization_barrier(trees)


PIECES = (
    [(0, (), 0, 0, 0)]
    + [(1, (k - 1,), 0, 0, k) for k in (1, 2, 3)]
    + [(2, (), 0, 1, 0), (3, (), 1, 0, 0)]
    + [(4, (k - 1,), 0, 1, k) for k in (1, 2, 3)]
    + [(5, (k - 1,), 1, 0, k) for k in (1, 2, 3)]
    + [(6, (k,), 1, 1, k) for k in (0, 1)]
    + [(7, (k - 2,), 1, 1, k) for k in (2, 3)]
)
FAST_PLAN = [
    (8 * c + which, lead, 2 * c + y, 4 * x + z)
    for c in range(2)
    for which, lead, y, x, z in PIECES
]
PLAIN_PLAN = [(0, (), j, None) for j in range(4)]


def xor_order(stacked, index, bits):
    shape = stacked.shape
    out = stacked.reshape((2,) * bits + shape[1:])
    for b in range(bits):
        out = jnp.where((index >> (bits - 1 - b)) & 1 == 1, jnp.flip(out, b), out)
    return out.reshape(shape)


def add(*parts):
    total = parts[0].astype(F32)
    for p in parts[1:]:
        total = total + p.astype(F32)
    return total


def low_add(*parts):
    return add(*parts).astype(BF16)


def scatter_sum(g0, g1):
    other = core_swap(g1)

    def own(y, x, zs):
        return (g0[y, x, zs], other[y, x, zs])

    lo, hi = slice(0, 2), slice(2, 4)
    from_x = x_swap(low_add(*own(1, 1, lo)))
    from_y = y_swap(low_add(*own(1, 1, hi)))
    to_x = jnp.concatenate([low_add(*own(0, 1, lo)), low_add(*own(0, 1, hi), from_y)])
    to_y = jnp.concatenate([low_add(*own(1, 0, lo), from_x), low_add(*own(1, 0, hi))])
    from_x, from_y = x_swap(to_x), y_swap(to_y)
    total = add(*own(0, 0, 0), from_x[0], from_y[0])
    back = [
        z_swap(k, low_add(*own(0, 0, k), from_x[k], from_y[k])) for k in (1, 2, 3)
    ]
    return add(total, *back)


def body(tokens, w_qkv, w_out, w_up, w_down, norm_gain, norm_bias, seg_table, seg_ids, cotangent):
    nd, ntens = lax.axis_size("dp"), lax.axis_size("tensor")
    fast = nd == 8
    di, ti = lax.axis_index("dp"), lax.axis_index("tensor")
    seqs, toks, d = tokens.shape
    rows, dblk = seqs * toks, tokens.shape[2] // nd
    per_dev = toks // SEG
    x = tokens.reshape(rows, d)
    cot = cotangent.reshape(rows, d)

    def pack(b):
        return (
            jnp.concatenate([w_qkv[b].reshape(dblk, -1), w_out[b].T], axis=1),
            jnp.stack([w_up[b], w_down[b].T]),
        )

    attn0, mlp0 = pack(0)
    attn1, mlp1 = pack(1)
    small = jnp.concatenate(
        [norm_gain.reshape(4, dblk), norm_bias.reshape(4, dblk), seg_table], axis=0
    )
    onehot = (seg_ids.reshape(-1, 1) == jnp.arange(128, dtype=jnp.int32)).astype(BF16)

    w1 = lax.all_gather(jnp.concatenate([attn1[None], mlp1]), "dp", axis=0)
    w1 = w1.transpose(1, 0, 2, 3).reshape(3, d, d)

    if fast:
        zi, xi = di // 2, di % 2
        blk = jnp.stack([(zi ^ k) * 2 + (xi ^ l) for l in range(2) for k in range(4)]).astype(jnp.int32)
        p1, p2 = attn0[None], mlp0
        sm = jnp.stack([small, x_swap(small)])
        z1 = [z_swap(k, p1) for k in (1, 2, 3)]
        x1, y1 = x_swap(p1), y_swap(p1)
        sz = [z_swap(k, sm) for k in (1, 2, 3)]
        z1, x1, y1, p2, sz = tied(z1, x1, y1, p2, sz)
        c1 = jnp.stack(z1)
        xc1, yc1 = x_swap(c1), y_swap(c1)
        z2 = [z_swap(k, p2) for k in (1, 2, 3)]
        x2, y2 = x_swap(p2), y_swap(p2)
        z2, xc1, yc1, x2, y2 = tied(z2, xc1, yc1, x2, y2)
        c2 = jnp.stack(z2)
        ex1, ey1 = x_swap(jnp.stack([y1, yc1[0]])), y_swap(xc1[1:])
        xc2, yc2 = x_swap(c2), y_swap(c2)
        ex1, ey1, xc2, yc2 = tied(ex1, ey1, xc2, yc2)
        mine1 = [p1, c1, x1, y1, xc1, yc1, ex1, ey1]
        attn_pieces = mine1 + [core_swap(v) for v in mine1]
        ex2, ey2 = x_swap(jnp.stack([y2, yc2[0]])), y_swap(xc2[1:])
        mine2 = [p2, c2, x2, y2, xc2, yc2, ex2, ey2]
        mlp_pieces = mine2 + [core_swap(v) for v in mine2]
        plan = FAST_PLAN
        slots = xor_order(jnp.stack([sm] + sz).reshape(nd, 16, dblk), di, 3)
        nv = slots.transpose(1, 0, 2).reshape(16, d).astype(F32)
    else:
        blk = jnp.zeros((8,), jnp.int32)

        def whole(p):
            g = lax.all_gather(p, ("tensor", "dp"), axis=0)
            g = g.reshape(ntens, nd, p.shape[0], dblk, d).transpose(0, 2, 1, 3, 4)
            g = g.reshape(ntens, p.shape[0], d, d)
            return xor_order(g, ti, 2)

        attn_pieces, mlp_pieces = [whole(attn0[None])], [whole(mlp0)]
        plan = PLAIN_PLAN
        nv = lax.all_gather(small, "dp", axis=1, tiled=True).astype(F32)
    npc = len(attn_pieces)

    w_a, q, k, v, o, p, xt, y, n1, r1, y_first = attn_forward(
        plan, npc, blk, x, nv, attn_pieces
    )

    leaders = jnp.concatenate(
        [
            y_first[:, 0].astype(BF16),
            cot.reshape(-1, SEG, d)[:, 0],
            onehot,
        ],
        axis=1,
    ).reshape(seqs, per_dev, -1)
    width = leaders.shape[-1]
    pay = lax.dynamic_update_slice(
        jnp.zeros((seqs, per_dev * ntens, width), BF16), leaders, (0, per_dev * ti, 0)
    )
    if fast:
        pay = pay + core_swap(pay)
        pay = pay + y_swap(pay)
        pay = jnp.stack([pay, x_swap(pay)])
        pay = jnp.stack([pay] + [z_swap(kk, pay) for kk in (1, 2, 3)])
        first = 0
    else:
        pay = lax.all_gather(lax.psum(pay, "tensor"), "dp", axis=0)
        first = di * seqs * per_dev * ntens
    pay = pay.reshape(-1, width)
    lead_y, lead_cot, lead_hot = pay[:, :d], pay[:, d : 2 * d], pay[:, 2 * d :]

    (w_m, gb, gp, ybt, dmt, dm, dh2, result, sums2, zl, nl, rl, ybl) = mlp_forward(
        plan, npc, blk, y, lead_y, cot, nv, mlp_pieces
    )

    g1, dy = mlp_backward(1, nd, fast, blk, dm, dmt, ybt, gb, gp, w_m, dh2)
    g0, dy = mlp_backward(0, nd, fast, blk, dm, dmt, ybt, gb, gp, w_m, dy)

    def partial_sum(part):
        if fast:
            half = low_add(part, core_swap(part))
            return half, y_swap(half)
        return lax.psum(part.astype(F32), "tensor"), jnp.zeros_like(part)

    c, cqkv, co, cp, ca = cross_attn(zl, lead_hot, nv, w1[0])
    cy, cn, cr, cgb, cgp, cm = cross_mlp(c, *partial_sum(ca), nv, w1[1:])
    e, cdh2, cgd, cgu, cdy, csum2 = cross_mlp_back(
        cy, *partial_sum(cm), lead_cot, nv, w1[1:], cgb, cgp
    )
    cdh, cdx, cga, csum1 = cross_attn_back(
        cdh2, *partial_sum(cdy), cn, cr, c, cqkv, co, cp, nv, w1[0]
    )
    dyl, lgd, lgu, lsum = lead_backward(
        cdh, *partial_sum(cdx), lead_hot, nl, rl, ybl, nv, gb, gp, w_m, rows
    )

    def own_leaders(full):
        part = lax.dynamic_slice_in_dim(full, first, seqs * per_dev * ntens, 0)
        part = part.reshape(seqs, per_dev * ntens, d)
        return lax.dynamic_slice_in_dim(part, per_dev * ti, per_dev, 1).reshape(-1, d)

    lead_dy = jnp.broadcast_to(own_leaders(dyl)[:, None], (rows // SEG, 8, d))
    dh, da, dat, sums = attn_norm_back(dy, lead_dy, n1, r1, nv, sums2)
    a1, dx = attn_backward(1, nd, fast, blk, da, dat, xt, q, k, v, o, p, w_a, dh, sums)
    a0, dx = attn_backward(0, nd, fast, blk, da, dat, xt, q, k, v, o, p, w_a, dx, sums)

    if fast:
        shape = (2, 2, 4)
        gm = scatter_sum(g0.reshape(*shape, *g0.shape[2:]), g1.reshape(*shape, *g1.shape[2:]))
        ga = scatter_sum(a0.reshape(*shape, *a0.shape[2:]), a1.reshape(*shape, *a1.shape[2:]))[0]
        norm_sums = ga[dblk : dblk + 8, :dblk]
        ga = ga[:dblk]
    else:

        def owned(lo, hi):
            g = jnp.concatenate([lo, hi])
            g = xor_order(g, ti, 2).astype(F32)
            g = lax.psum_scatter(g, "tensor", scatter_dimension=0)
            return lax.psum_scatter(g, "dp", scatter_dimension=1, tiled=True)

        gm, ga = owned(g0, g1), owned(a0, a1)[0]
        norm_sums = lax.psum_scatter(
            lax.psum(sums, "tensor"), "dp", scatter_dimension=1, tiled=True
        )

    def rows_of(full):
        return lax.dynamic_slice_in_dim(full, di * dblk, dblk, 0)

    def cols_of(full):
        return lax.dynamic_slice_in_dim(full, di * dblk, dblk, 1)

    gu0, gd0 = gm[0] + rows_of(lgu), gm[1] + rows_of(lgd)
    ga1, gu1, gd1 = rows_of(cga), rows_of(cgu), rows_of(cgd)
    wide = w_qkv.shape[3] * 3
    grad_qkv = jnp.stack([ga[:, :wide], ga1[:, :wide]]).reshape(w_qkv.shape)
    grad_out = jnp.stack([ga[:, wide:].T, ga1[:, wide:].T])
    grad_up = jnp.stack([gu0, gu1])
    grad_down = jnp.stack([gd0.T, gd1.T])
    lsum, csum1, csum2 = cols_of(lsum), cols_of(csum1), cols_of(csum2)
    grad_gain = jnp.stack(
        [
            jnp.stack([norm_sums[0], norm_sums[2] + lsum[0]]),
            jnp.stack([csum1[0], csum2[0]]),
        ]
    )
    grad_bias = jnp.stack(
        [
            jnp.stack([norm_sums[1], norm_sums[3] + lsum[1]]),
            jnp.stack([csum1[1], csum2[1]]),
        ]
    )
    result = result.reshape(-1, SEG, d).at[:, 0].set(own_leaders(e)).reshape(tokens.shape)
    return (
        result,
        dx.reshape(tokens.shape),
        grad_qkv,
        grad_out,
        grad_up,
        grad_down,
        grad_gain,
        grad_bias,
        lsum[8:16],
    )


def solution(mesh):
    return jax.shard_map(
        body,
        mesh=mesh,
        in_specs=(
            P("dp", "tensor", None),
            P(None, "dp", None, "tensor"),
            P(None, "tensor", "dp"),
            P(None, "dp", "tensor"),
            P(None, "tensor", "dp"),
            P(None, None, "dp"),
            P(None, None, "dp"),
            P(None, "dp"),
            P("dp", "tensor"),
            P("dp", "tensor", None),
        ),
        out_specs=(
            P("dp", "tensor", None),
            P("dp", "tensor", None),
            P(None, "dp", None, "tensor"),
            P(None, "tensor", "dp"),
            P(None, "dp", "tensor"),
            P(None, "tensor", "dp"),
            P(None, None, "dp"),
            P(None, None, "dp"),
            P(None, "dp"),
        ),
        check_vma=False,
    )
```

```python
import functools
import math

import jax
import jax.numpy as jnp
from jax import lax
from jax.experimental import pallas as pl
from jax.experimental.pallas import tpu as pltpu
from jax.sharding import PartitionSpec as P

HEAD = 64
SEG = 128
GROUP = 8
F32, BF16 = jnp.float32, jnp.bfloat16
VMEM = pltpu.VMEM
ANY = pl.BlockSpec(memory_space=pl.ANY)
WHOLE = pl.BlockSpec(memory_space=pltpu.VMEM)
SMEM = pl.BlockSpec(memory_space=pltpu.SMEM)
PARAMS = pltpu.CompilerParams(vmem_limit_bytes=60 << 20)
EPS = 1e-05
SCALE = HEAD ** (-0.5)
RSQRT2 = 1.0 / math.sqrt(2.0)
RSQRT2PI = 1.0 / math.sqrt(2.0 * math.pi)


def nn(a, b):
    return lax.dot_general(a, b, (((1,), (0,)), ((), ())), preferred_element_type=F32)


def nt(a, b):
    return lax.dot_general(a, b, (((1,), (1,)), ((), ())), preferred_element_type=F32)


def tn(a, b):
    return lax.dot_general(a, b, (((0,), (0,)), ((), ())), preferred_element_type=F32)


def norm_parts(h):
    center = h - jnp.mean(h, axis=-1, keepdims=True)
    rstd = lax.rsqrt(jnp.mean(center * center, axis=-1, keepdims=True) + EPS)
    return center * rstd, rstd


def norm_back(grad, normed, rstd, gain):
    dn = grad * gain
    return rstd * (
        dn
        - jnp.mean(dn, axis=-1, keepdims=True)
        - normed * jnp.mean(dn * normed, axis=-1, keepdims=True)
    )


def gelu_both(u):
    cdf = 0.5 + 0.5 * lax.erf(u * RSQRT2)
    return u * cdf, cdf + u * (jnp.exp(-0.5 * u * u) * RSQRT2PI)


def halves(pair):
    lane = lax.broadcasted_iota(jnp.int32, pair.shape, 1)
    zero = jnp.zeros_like(pair)
    return jnp.concatenate(
        [jnp.where(lane < HEAD, pair, zero), jnp.where(lane < HEAD, zero, pair)], axis=0
    )


def unhalve(stacked):
    lane = lax.broadcasted_iota(jnp.int32, (SEG, 2 * HEAD), 1)
    return jnp.where(lane < HEAD, stacked[:SEG], stacked[SEG:])


def half_softmax(s):
    top = jnp.concatenate(
        [
            jnp.broadcast_to(jnp.max(s[:, :SEG], axis=-1, keepdims=True), (SEG, SEG)),
            jnp.broadcast_to(jnp.max(s[:, SEG:], axis=-1, keepdims=True), (SEG, SEG)),
        ],
        axis=1,
    )
    ex = jnp.exp(s - top)
    inv = jnp.concatenate(
        [
            jnp.broadcast_to(1.0 / jnp.sum(ex[:, :SEG], axis=-1, keepdims=True), (SEG, SEG)),
            jnp.broadcast_to(1.0 / jnp.sum(ex[:, SEG:], axis=-1, keepdims=True), (SEG, SEG)),
        ],
        axis=1,
    )
    return ex * inv


def call(body, outs, out_specs, in_specs, scratch=(), us=10):
    return pl.pallas_call(
        body,
        out_shape=outs,
        in_specs=in_specs,
        out_specs=out_specs,
        scratch_shapes=list(scratch),
        compiler_params=PARAMS,
        cost_estimate=pl.CostEstimate(flops=int(us * 2e9), bytes_accessed=1, transcendentals=0),
    )


def sds(shape, dtype):
    return jax.ShapeDtypeStruct(shape, dtype)


DMA = pltpu.SemaphoreType.DMA


class Copies:
    def __init__(self, sems):
        self.sems, self.used, self.open = sems, 0, []

    def start(self, src, dst):
        copy = pltpu.make_async_copy(src, dst, self.sems.at[self.used])
        self.used += 1
        copy.start()
        self.open.append(copy)
        return copy

    def wait(self, *copies):
        for c in copies:
            if any(c is other for other in self.open):
                self.open = [other for other in self.open if other is not c]
                c.wait()

    def wait_all(self):
        for c in self.open:
            c.wait()
        self.open = []


def fetch(cp, plan, pieces, pack, blk_ref, dst, d):
    out = []
    for which, lead, j, slot in plan:
        cols = pl.ds(j * d, d)
        if slot is None:
            out.append(cp.start(pieces[which].at[j, pack], dst.at[:, cols]))
        else:
            src = pieces[which].at[(*lead, pack)]
            rows = src.shape[0]
            at = pl.ds(pl.multiple_of(blk_ref[slot] * rows, 16), rows)
            out.append(cp.start(src, dst.at[at, cols]))
    return out


def row_tiles(rows, tile):
    return [slice(i, min(i + tile, rows)) for i in range(0, rows, tile)]


def attn_forward(plan, blk, x, nv, pieces):
    rows, d = x.shape
    segs, quarter = rows // SEG, d // 4
    pairs = d // SEG
    np_ = len(pieces)

    def body(blk_ref, x_hbm, nv_ref, *refs):
        ins, refs = refs[:np_], refs[np_:]
        w_out, qkv_out, o_out, p_out, y_out, n_out, r_ref, yl_ref = refs[:8]
        raw, w, x_s, qkv, o_s, p_s, y_s, n_s, sems = refs[8:]
        cp = Copies(sems)
        got = fetch(cp, plan, ins, 0, blk_ref, raw, d)
        got_x = cp.start(x_hbm, x_s)
        cp.wait(*got)
        for t in range(4):
            for half in range(2):
                j = 2 * half
                at = slice(t * d + j * quarter, t * d + (j + 2) * quarter)
                w[:, at] = jnp.concatenate(
                    [
                        raw[:, j * d + t * quarter : j * d + (t + 1) * quarter],
                        raw[:, (j + 1) * d + t * quarter : (j + 1) * d + (t + 1) * quarter],
                    ],
                    axis=1,
                )
        cp.start(w, w_out)
        cp.wait(got_x)
        qkv[...] = nn(x_s[...], w[:, : 3 * d]).astype(BF16)
        cp.start(qkv, qkv_out)
        for t in range(segs):
            at = slice(t * SEG, (t + 1) * SEG)
            probs = []
            for pair in range(pairs):
                lo = pair * SEG
                s = nt(qkv[at, lo : lo + SEG], halves(qkv[at, d + lo : d + lo + SEG])) * SCALE
                probs.append(half_softmax(s).astype(BF16))
            for pair in range(pairs):
                lo = pair * SEG
                p_s[t, pair] = probs[pair]
                o_s[at, lo : lo + SEG] = nn(
                    probs[pair], halves(qkv[at, 2 * d + lo : 2 * d + lo + SEG])
                ).astype(BF16)
            cp.start(p_s.at[t], p_out.at[t])
        cp.start(o_s, o_out)
        y_s[...] = nt(o_s[...], w[:, 3 * d :])
        for t in range(segs):
            at = slice(t * SEG, (t + 1) * SEG)
            n, r = norm_parts(x_s[at].astype(F32) + y_s[at])
            y = n * nv_ref[0:1] + nv_ref[4:5]
            y_s[at] = y
            n_s[at] = n.astype(BF16)
            r_ref[at] = r
            yl_ref[t] = y[0:8].astype(BF16)
            cp.start(y_s.at[at], y_out.at[at])
            cp.start(n_s.at[at], n_out.at[at])
        cp.wait_all()

    return call(
        body,
        (
            sds((d, 4 * d), BF16),
            sds((rows, 3 * d), BF16),
            sds((rows, d), BF16),
            sds((segs, pairs, SEG, 2 * SEG), BF16),
            sds((rows, d), F32),
            sds((rows, d), BF16),
            sds((rows, 1), F32),
            sds((segs, 8, d), BF16),
        ),
        (ANY,) * 6 + (WHOLE,) * 2,
        [SMEM, ANY, WHOLE] + [ANY] * np_,
        [
            VMEM((d, 4 * d), BF16),
            VMEM((d, 4 * d), BF16),
            VMEM((rows, d), BF16),
            VMEM((rows, 3 * d), BF16),
            VMEM((rows, d), BF16),
            VMEM((segs, pairs, SEG, 2 * SEG), BF16),
            VMEM((rows, d), F32),
            VMEM((rows, d), BF16),
            DMA((len(plan) + 4 + 3 * segs,)),
        ],
        us=30,
    )(blk, x, nv, *pieces)


def lead_forward(plan, blk, lead_y, nv, pieces):
    leads, d = lead_y.shape
    np_ = len(pieces)

    def body(blk_ref, yl_ref, nv_ref, *refs):
        ins, refs = refs[:np_], refs[np_:]
        wu_out, wd_out, gb_ref, gp_ref, zl_ref, nl_ref, rl_ref, wu, wd, sems = refs
        cp = Copies(sems)
        got_u = fetch(cp, plan, ins, 0, blk_ref, wu, d)
        got_d = fetch(cp, plan, ins, 1, blk_ref, wd, d)
        cp.wait(*got_u)
        cp.start(wu, wu_out)
        for at in row_tiles(leads, SEG):
            g, gd = gelu_both(nn(yl_ref[at], wu[...]))
            gb_ref[at] = g.astype(BF16)
            gp_ref[at] = gd.astype(BF16)
        cp.wait(*got_d)
        cp.start(wd, wd_out)
        for at in row_tiles(leads, SEG):
            n, r = norm_parts(yl_ref[at].astype(F32) + nt(gb_ref[at], wd[...]))
            zl_ref[at] = n * nv_ref[1:2] + nv_ref[5:6]
            nl_ref[at] = n
            rl_ref[at] = r
        cp.wait_all()

    return call(
        body,
        (
            sds((d, 4 * d), BF16),
            sds((d, 4 * d), BF16),
            sds((leads, 4 * d), BF16),
            sds((leads, 4 * d), BF16),
            sds((leads, d), F32),
            sds((leads, d), F32),
            sds((leads, 1), F32),
        ),
        (ANY, ANY) + (WHOLE,) * 5,
        [SMEM, WHOLE, WHOLE] + [ANY] * np_,
        [VMEM((d, 4 * d), BF16), VMEM((d, 4 * d), BF16), DMA((2 * len(plan) + 2,))],
        us=20,
    )(blk, lead_y, nv, *pieces)


def mlp_forward(y, cot, nv, wu_, wd_):
    rows, d = y.shape

    def body(y_hbm, cot_hbm, nv_ref, wu_hbm, wd_hbm, *refs):
        gb_out, gp_out, yb_out, dm_out, dh_out, res_out, sums_ref = refs[:7]
        y_s, cot_s, wu, wd, yb, gb, gp, dm, dh_s, res, sems = refs[7:]
        cp = Copies(sems)
        got_y = cp.start(y_hbm, y_s)
        up, down = [], []
        for j in range(4):
            cols = pl.ds(j * d, d)
            up.append(cp.start(wu_hbm.at[:, cols], wu.at[:, cols]))
        down.append(cp.start(wd_hbm, wd))
        got_cot = cp.start(cot_hbm, cot_s)
        cp.wait(got_y)
        yb[...] = y_s[...].astype(BF16)
        cp.start(yb, yb_out)
        for j in range(4):
            cols = slice(j * d, (j + 1) * d)
            cp.wait(up[j])
            g, gd = gelu_both(nn(yb[...], wu[:, cols]))
            gb[:, cols] = g.astype(BF16)
            gp[:, cols] = gd.astype(BF16)
            cp.start(gb.at[:, pl.ds(j * d, d)], gb_out.at[:, pl.ds(j * d, d)])
            cp.start(gp.at[:, pl.ds(j * d, d)], gp_out.at[:, pl.ds(j * d, d)])
        cp.wait(*down)
        cp.wait(got_cot)
        gain, bias = nv_ref[1:2], nv_ref[5:6]
        top, bottom = jnp.zeros((1, d), F32), jnp.zeros((1, d), F32)
        dh_s[...] = nt(gb[...], wd[...])
        for at in row_tiles(rows, SEG):
            n, r = norm_parts(y_s[at] + dh_s[at])
            res[at] = (n * gain + bias).astype(BF16)
            row = lax.broadcasted_iota(jnp.int32, (SEG, d), 0)
            grad = jnp.where(row == 0, 0.0, cot_s[at].astype(F32))
            top += jnp.sum(grad * n, axis=0, keepdims=True)
            bottom += jnp.sum(grad, axis=0, keepdims=True)
            dh = norm_back(grad, n, r, gain)
            dh_s[at] = dh
            dm[at] = dh.astype(BF16)
            for s, out in ((res, res_out), (dh_s, dh_out), (dm, dm_out)):
                cp.start(s.at[at], out.at[at])
        sums_ref[...] = jnp.concatenate([top, bottom, jnp.zeros((6, d), F32)], axis=0)
        cp.wait_all()

    return call(
        body,
        (
            sds((rows, 4 * d), BF16),
            sds((rows, 4 * d), BF16),
            sds((rows, d), BF16),
            sds((rows, d), BF16),
            sds((rows, d), F32),
            sds((rows, d), BF16),
            sds((8, d), F32),
        ),
        (ANY,) * 6 + (WHOLE,),
        [ANY, ANY, WHOLE, ANY, ANY],
        [
            VMEM((rows, d), F32),
            VMEM((rows, d), BF16),
            VMEM((d, 4 * d), BF16),
            VMEM((d, 4 * d), BF16),
            VMEM((rows, d), BF16),
            VMEM((rows, 4 * d), BF16),
            VMEM((rows, 4 * d), BF16),
            VMEM((rows, d), BF16),
            VMEM((rows, d), F32),
            VMEM((rows, d), BF16),
            DMA((16 + 3 * (rows // SEG),)),
        ],
        us=0.01,
    )(y, cot, nv, wu_, wd_)


def put_blocks(cp, blocked, blk_ref, src, out, y, pack, slots):
    if not blocked:
        cp.start(src, out.at[y, pack])
        return
    rows = src.shape[0] // slots
    for s in range(slots):
        at = pl.ds(pl.multiple_of(blk_ref[s] * rows, 16), rows)
        cp.start(src.at[at], out.at[y, s, pack, pl.ds(0, rows)])


def mlp_backward(core, slots, blocked, blk, dm_, yb_, gb_, gp_, wu_, wd_, start_):
    rows, d = dm_.shape
    dblk = d // slots
    per = slots if blocked else 1
    half = 2 * d

    def body(blk_ref, dm_hbm, yb_hbm, gb_hbm, gp_hbm, wu_hbm, wd_hbm, st_hbm, g_out, dy_out, *scr):
        dm, yb, gb, gp, wu, wd, st, du, gd, gu, dy, sems = scr
        cp = Copies(sems)
        cols = pl.ds(core * half, half)
        got_dm = cp.start(dm_hbm, dm)
        got_gb = cp.start(gb_hbm.at[:, cols], gb)
        got_wd = cp.start(wd_hbm.at[:, cols], wd)
        got_gp = cp.start(gp_hbm.at[:, cols], gp)
        got_yb = cp.start(yb_hbm, yb)
        got_wu = cp.start(wu_hbm.at[:, cols], wu)
        got_st = cp.start(st_hbm, st)
        cp.wait(got_dm, got_gb)
        for y in range(2):
            mine = slice(y * d, (y + 1) * d)
            gd[:, mine] = tn(dm[...], gb[:, mine]).astype(BF16)
            put_blocks(cp, blocked, blk_ref, gd.at[:, pl.ds(y * d, d)], g_out, y, 1, slots)
        cp.wait(got_wd, got_gp)
        for y in range(2):
            mine = slice(y * d, (y + 1) * d)
            du[:, mine] = (nn(dm[...], wd[:, mine]) * gp[:, mine].astype(F32)).astype(BF16)
        cp.wait(got_yb)
        for y in range(2):
            mine = slice(y * d, (y + 1) * d)
            gu[:, mine] = tn(yb[...], du[:, mine]).astype(BF16)
            put_blocks(cp, blocked, blk_ref, gu.at[:, pl.ds(y * d, d)], g_out, y, 0, slots)
        cp.wait(got_wu, got_st)
        dy[...] = st[...] + nt(du[...], wu[...])
        cp.start(dy, dy_out)
        cp.wait_all()

    g_shape = (2, slots, 2, dblk, d) if blocked else (2, 2, d, d)
    return call(
        body,
        (sds(g_shape, BF16), sds((rows, d), F32)),
        (ANY, ANY),
        [SMEM] + [ANY] * 7,
        [
            VMEM((rows, d), BF16),
            VMEM((rows, d), BF16),
            VMEM((rows, half), BF16),
            VMEM((rows, half), BF16),
            VMEM((d, half), BF16),
            VMEM((d, half), BF16),
            VMEM((rows, d), F32),
            VMEM((rows, half), BF16),
            VMEM((d, half), BF16),
            VMEM((d, half), BF16),
            VMEM((rows, d), F32),
            DMA((7 + 4 * per + rows // (2 * SEG),)),
        ],
        us=8,
    )(blk, dm_, yb_, gb_, gp_, wu_, wd_, start_)


def attn_backward(core, slots, blocked, blk, x_, qkv_, o_, p_, w_, first, rest):
    rows, d = x_.shape
    segs, half, quarter = rows // SEG, d // 2, d // 4
    dblk = d // slots
    per = slots if blocked else 1
    pairs = half // SEG
    opening = first is not None
    extra = first if opening else rest

    def body(blk_ref, x_hbm, qkv_hbm, o_hbm, p_hbm, w_hbm, *refs):
        more, refs = refs[: len(extra)], refs[len(extra) :]
        n_out = 4 if opening else 2
        outs, scr = refs[:n_out], refs[n_out:]
        g_out, dx_out = outs[:2]
        x, qkv, o, p, w, st, da, do, dqkv, gr, ex, dx, sems = scr[:13]
        cp = Copies(sems)
        if opening:
            dy_hbm, ld_ref, n_hbm, r_ref, nv_ref, s2_ref = more
            da_out, sums_ref = outs[2:]
            nb = scr[13]
            got_dy = cp.start(dy_hbm, st)
            got_n = cp.start(n_hbm, nb)
        else:
            da_hbm, st_hbm, sums_ref = more
            got_da = cp.start(da_hbm, da)
        got_w = [
            cp.start(w_hbm.at[:, pl.ds(t * d + core * half, half)], w.at[:, pl.ds(t * half, half)])
            for t in (3, 0, 1, 2)
        ]
        got_qkv = [
            cp.start(
                qkv_hbm.at[:, pl.ds(t * d + core * half, half)], qkv.at[:, pl.ds(t * half, half)]
            )
            for t in (2, 0, 1)
        ]
        got_p = cp.start(p_hbm.at[:, pl.ds(core * pairs, pairs)], p)
        got_o = cp.start(o_hbm.at[:, pl.ds(core * half, half)], o)
        got_x = cp.start(x_hbm, x)
        if opening:
            cp.wait(got_dy, got_n)
            top, bottom = jnp.zeros((1, d), F32), jnp.zeros((1, d), F32)
            for t in range(segs):
                at = slice(t * SEG, (t + 1) * SEG)
                row = lax.broadcasted_iota(jnp.int32, (SEG, d), 0)
                grad = st[at] + jnp.where(row == 0, ld_ref[t : t + 1], 0.0)
                n = nb[at].astype(F32)
                top += jnp.sum(grad * n, axis=0, keepdims=True)
                bottom += jnp.sum(grad, axis=0, keepdims=True)
                dh = norm_back(grad, n, r_ref[at], nv_ref[0:1])
                st[at] = dh
                da[at] = dh.astype(BF16)
            cp.start(da, da_out)
            sums_ref[...] = jnp.concatenate(
                [top, bottom, s2_ref[0:2], jnp.zeros((4, d), F32)], axis=0
            )
        else:
            got_st = cp.start(st_hbm, st)
            cp.wait(got_da)
        if blocked:
            for b in range(slots):
                ex[b] = jnp.zeros((16, d), BF16)
                ex[b, 0:8, 0:dblk] = sums_ref[:, b * dblk : (b + 1) * dblk].astype(BF16)
            for y in range(2):
                for s in range(slots):
                    cp.start(ex.at[blk_ref[s]], g_out.at[y, s, 0, pl.ds(dblk, 16)])
        cp.wait(got_w[0])
        do[...] = nn(da[...], w[:, 3 * half :]).astype(BF16)
        cp.wait(got_p, *got_qkv)
        for t in range(segs):
            at = slice(t * SEG, (t + 1) * SEG)
            dss = []
            for pair in range(pairs):
                mine = slice(pair * SEG, (pair + 1) * SEG)
                pf = p[t, pair].astype(F32)
                v = qkv[at, 2 * half + pair * SEG : 2 * half + (pair + 1) * SEG]
                pd = pf * nt(do[at, mine], halves(v))
                parts = [
                    pd[:, c] - pf[:, c] * jnp.sum(pd[:, c], axis=-1, keepdims=True)
                    for c in (slice(0, SEG), slice(SEG, 2 * SEG))
                ]
                dss.append(jnp.concatenate(parts, axis=1).astype(BF16))
            for pair in range(pairs):
                mine = slice(pair * SEG, (pair + 1) * SEG)
                q, k = (qkv[at, i * half + pair * SEG : i * half + (pair + 1) * SEG] for i in (0, 1))
                ds = dss[pair]
                dv = unhalve(tn(p[t, pair], do[at, mine]))
                dk = unhalve(tn(ds, q)) * SCALE
                dq = nn(ds, halves(k)) * SCALE
                for i, g in enumerate((dq, dk, dv)):
                    dqkv[at, i * half + pair * SEG : i * half + (pair + 1) * SEG] = g.astype(BF16)
        cp.wait(got_x, got_o)
        gf = tn(x[...], dqkv[...]).astype(BF16)
        go = tn(da[...], o[...]).astype(BF16)
        for y in range(2):
            at = slice(y * quarter, (y + 1) * quarter)
            cut = [gf[:, i * half + y * quarter : i * half + (y + 1) * quarter] for i in range(3)]
            cut.append(go[:, at])
            gr[y, :, :half] = jnp.concatenate(cut[:2], axis=1)
            gr[y, :, half:] = jnp.concatenate(cut[2:], axis=1)
            put_blocks(cp, blocked, blk_ref, gr.at[y], g_out, y, 0, slots)
        if not opening:
            cp.wait(got_st)
        cp.wait(*got_w)
        dx[...] = st[...] + nt(dqkv[...], w[:, : 3 * half])
        cp.start(dx, dx_out)
        cp.wait_all()

    g_shape = (2, slots, 1, dblk + 16, d) if blocked else (2, 1, d, d)
    outs = [sds(g_shape, BF16), sds((rows, d), F32)]
    specs = [ANY, ANY]
    in_more = [ANY, ANY, WHOLE]
    if opening:
        outs += [sds((rows, d), BF16), sds((8, d), F32)]
        specs += [ANY, WHOLE]
        in_more = [ANY, WHOLE, ANY, WHOLE, WHOLE, WHOLE]
    scratch = [
        VMEM((rows, d), BF16),
        VMEM((rows, 3 * half), BF16),
        VMEM((rows, half), BF16),
        VMEM((segs, pairs, SEG, 2 * SEG), BF16),
        VMEM((d, 4 * half), BF16),
        VMEM((rows, d), F32),
        VMEM((rows, d), BF16),
        VMEM((rows, half), BF16),
        VMEM((rows, 3 * half), BF16),
        VMEM((2, d, d), BF16),
        VMEM((slots if blocked else 1, 16, d), BF16),
        VMEM((rows, d), F32),
        DMA((16 + 4 * per + rows // (2 * SEG),)),
    ]
    if opening:
        scratch.append(VMEM((rows, d), BF16))
    return call(
        body,
        tuple(outs),
        tuple(specs),
        [SMEM] + [ANY] * 5 + in_more,
        scratch,
        us=9,
    )(blk, x_, qkv_, o_, p_, w_, *extra)


def fetch_cross(cp, pieces, blk_ref, dst):
    if len(pieces) == 1:
        return [cp.start(pieces[0], dst)]
    packs, d, _ = dst.shape
    rows = d // 8
    out = []
    for slot in range(8):
        at = pl.ds(pl.multiple_of(blk_ref[slot] * rows, 16), rows)
        for p in range(packs):
            src = pieces[slot // 4].at[slot % 4, pl.ds(p * rows, rows)]
            out.append(cp.start(src, dst.at[p, at]))
    return out


def own_rows(cp, blocked, blk_ref, src, out):
    if blocked:
        rows = out.shape[0]
        src = src.at[pl.ds(pl.multiple_of(blk_ref[0] * rows, 8), rows)]
    cp.start(src, out)


def group_mask():
    a = lax.broadcasted_iota(jnp.int32, (SEG, SEG), 0) // GROUP
    b = lax.broadcasted_iota(jnp.int32, (SEG, SEG), 1) // GROUP
    return a == b


def sums_of(grad, n):
    d = grad.shape[1]
    return jnp.concatenate(
        [
            jnp.sum(grad * n, axis=0, keepdims=True),
            jnp.sum(grad, axis=0, keepdims=True),
            jnp.zeros((6, d), F32),
        ],
        axis=0,
    )


def cross_attn(blk, zl, onehot, nv, w):
    rows, d = zl.shape
    quarter = d // 4
    heads = quarter // HEAD
    tiles = rows // SEG

    def body(blk_ref, z_ref, oh_ref, nv_ref, *refs):
        c_ref, qkv_ref, o_ref, p_ref, a_ref, w_s, sems = refs[len(w) :]
        cp = Copies(sems)
        fetch_cross(cp, refs[: len(w)], blk_ref, w_s)
        cs = []
        for at in row_tiles(rows, SEG):
            c = z_ref[at]
            for i in range(8):
                c += oh_ref[at, i : i + 1].astype(F32) * nv_ref[8 + i : 9 + i]
            c_ref[at] = c
            cs.append(c.astype(BF16))
        cp.wait_all()
        mask = group_mask()
        for t, at in enumerate(row_tiles(rows, SEG)):
            qkv = nn(cs[t], w_s[0, :, : 3 * quarter]).astype(BF16)
            qkv_ref[at] = qkv
            cut = [
                [qkv[:, i * quarter + h * HEAD : i * quarter + (h + 1) * HEAD] for i in range(3)]
                for h in range(heads)
            ]
            probs = []
            for q, k, v in cut:
                s = jnp.where(mask, nt(q, k) * SCALE, -1e30)
                ex = jnp.exp(s - jnp.max(s, axis=-1, keepdims=True))
                probs.append((ex * (1.0 / jnp.sum(ex, axis=-1, keepdims=True))).astype(BF16))
            os = []
            for h in range(heads):
                p_ref[t, h] = probs[h]
                os.append(nn(probs[h], cut[h][2]).astype(BF16))
            o = jnp.concatenate(os, axis=1)
            o_ref[at] = o
            a_ref[at] = nt(o, w_s[0, :, 3 * quarter :]).astype(BF16)

    return call(
        body,
        (
            sds((rows, d), F32),
            sds((rows, 3 * quarter), BF16),
            sds((rows, quarter), BF16),
            sds((tiles, heads, SEG, SEG), BF16),
            sds((rows, d), BF16),
        ),
        (WHOLE,) * 5,
        [SMEM] + [WHOLE] * 3 + [ANY] * len(w),
        [VMEM((1, d, d), BF16), DMA((8,))],
        us=0.01,
    )(blk, zl, onehot, nv, *w)


def cross_mlp(blk, c, a0, a1, nv, w):
    rows, d = c.shape

    def body(blk_ref, c_ref, a0_ref, a1_ref, nv_ref, *refs):
        y_ref, n_ref, r_ref, gb_ref, gp_ref, m_ref, w_s, sems = refs[len(w) :]
        cp = Copies(sems)
        fetch_cross(cp, refs[: len(w)], blk_ref, w_s)
        n, r = norm_parts(c_ref[...] + (a0_ref[...].astype(F32) + a1_ref[...].astype(F32)))
        n_ref[...] = n
        r_ref[...] = r
        y = n * nv_ref[2:3] + nv_ref[6:7]
        y_ref[...] = y
        cp.wait_all()
        g, gd = gelu_both(nn(y.astype(BF16), w_s[0]))
        gb_ref[...] = g.astype(BF16)
        gp_ref[...] = gd.astype(BF16)
        m_ref[...] = nt(gb_ref[...], w_s[1]).astype(BF16)

    return call(
        body,
        (
            sds((rows, d), F32),
            sds((rows, d), F32),
            sds((rows, 1), F32),
            sds((rows, d), BF16),
            sds((rows, d), BF16),
            sds((rows, d), BF16),
        ),
        (WHOLE,) * 6,
        [SMEM] + [WHOLE] * 4 + [ANY] * len(w),
        [VMEM((2, d, d), BF16), DMA((16,))],
        us=4,
    )(blk, c, a0, a1, nv, *w)


def cross_mlp_back(slots, blocked, blk, y, m0, m1, cot, nv, gb, gp, w):
    rows, d = y.shape
    own = d // slots if blocked else d

    def body(blk_ref, y_ref, m0_ref, m1_ref, cot_ref, nv_ref, gb_ref, gp_ref, *refs):
        (e_ref, dh_ref, gd_out, gu_out, dy_ref, sums_ref, w_s, gd, gu, sems) = refs[len(w) :]
        cp = Copies(sems)
        got = fetch_cross(cp, refs[: len(w)], blk_ref, w_s)
        gain = nv_ref[3:4]
        n, r = norm_parts(y_ref[...] + (m0_ref[...].astype(F32) + m1_ref[...].astype(F32)))
        e_ref[...] = (n * gain + nv_ref[7:8]).astype(BF16)
        grad = cot_ref[...].astype(F32)
        sums_ref[...] = sums_of(grad, n)
        dh = norm_back(grad, n, r, gain)
        dh_ref[...] = dh
        dm = dh.astype(BF16)
        cp.wait(*got)
        du = (nn(dm, w_s[1]) * gp_ref[...].astype(F32)).astype(BF16)
        dy_ref[...] = nt(du, w_s[0]).astype(BF16)
        gd[...] = tn(dm, gb_ref[...])
        own_rows(cp, blocked, blk_ref, gd, gd_out)
        gu[...] = tn(y_ref[...].astype(BF16), du)
        own_rows(cp, blocked, blk_ref, gu, gu_out)
        cp.wait_all()

    return call(
        body,
        (
            sds((rows, d), BF16),
            sds((rows, d), F32),
            sds((own, d), F32),
            sds((own, d), F32),
            sds((rows, d), BF16),
            sds((8, d), F32),
        ),
        (WHOLE, WHOLE, ANY, ANY, WHOLE, WHOLE),
        [SMEM] + [WHOLE] * 7 + [ANY] * len(w),
        [VMEM((2, d, d), BF16), VMEM((d, d), F32), VMEM((d, d), F32), DMA((18,))],
        us=30,
    )(blk, y, m0, m1, cot, nv, gb, gp, *w)


def cross_attn_back(slots, blocked, blk, dh2, d0, d1, n1, r1, c, qkv, o, p, nv, w):
    rows, d = dh2.shape
    quarter = d // 4
    heads = quarter // HEAD
    own = d // slots if blocked else d

    def body(blk_ref, dh2_ref, d0_ref, d1_ref, n_ref, r_ref, c_ref, qkv_ref, o_ref, p_ref, nv_ref,
             *refs):
        dh_ref, dx_ref, g_out, sums_ref, da_s, dqkv_s, w_s, g, sems = refs[len(w) :]
        cp = Copies(sems)
        got = fetch_cross(cp, refs[: len(w)], blk_ref, w_s)
        grad = dh2_ref[...] + (d0_ref[...].astype(F32) + d1_ref[...].astype(F32))
        n = n_ref[...]
        sums_ref[...] = sums_of(grad, n)
        dh = norm_back(grad, n, r_ref[...], nv_ref[2:3])
        dh_ref[...] = dh
        da_s[...] = dh.astype(BF16)
        cp.wait(*got)
        for t, at in enumerate(row_tiles(rows, SEG)):
            do = nn(da_s[at], w_s[0, :, 3 * quarter :]).astype(BF16)
            qkv_t = qkv_ref[at]
            cut = [
                [qkv_t[:, i * quarter + h * HEAD : i * quarter + (h + 1) * HEAD] for i in range(3)]
                for h in range(heads)
            ]
            dos = [do[:, h * HEAD : (h + 1) * HEAD] for h in range(heads)]
            dss = []
            for h in range(heads):
                pf = p_ref[t, h].astype(F32)
                pd = pf * nt(dos[h], cut[h][2])
                dss.append((pd - pf * jnp.sum(pd, axis=-1, keepdims=True)).astype(BF16))
            dq, dk, dv = [], [], []
            for h in range(heads):
                dv.append(tn(p_ref[t, h], dos[h]).astype(BF16))
                dq.append((nn(dss[h], cut[h][1]) * SCALE).astype(BF16))
                dk.append((tn(dss[h], cut[h][0]) * SCALE).astype(BF16))
            dqkv_s[at] = jnp.concatenate(dq + dk + dv, axis=1)
        dx_ref[...] = nt(dqkv_s[...], w_s[0, :, : 3 * quarter]).astype(BF16)
        g[:, : 3 * quarter] = tn(c_ref[...].astype(BF16), dqkv_s[...])
        g[:, 3 * quarter :] = tn(da_s[...], o_ref[...])
        own_rows(cp, blocked, blk_ref, g, g_out)
        cp.wait_all()

    return call(
        body,
        (sds((rows, d), F32), sds((rows, d), BF16), sds((own, d), F32), sds((8, d), F32)),
        (WHOLE, WHOLE, ANY, WHOLE),
        [SMEM] + [WHOLE] * 10 + [ANY] * len(w),
        [
            VMEM((rows, d), BF16),
            VMEM((rows, 3 * quarter), BF16),
            VMEM((1, d, d), BF16),
            VMEM((d, d), F32),
            DMA((9,)),
        ],
        us=5,
    )(blk, dh2, d0, d1, n1, r1, c, qkv, o, p, nv, *w)


def lead_backward(slots, blocked, blk, dh, d0, d1, onehot, nl, rl, ybl, nv, gb_, gp_, wu_, wd_):
    rows, d = dh.shape
    own = d // slots if blocked else d

    def body(blk_ref, dh_ref, d0_ref, d1_ref, oh_ref, n_ref, r_ref, yb_ref, nv_ref, gb_hbm, gp_hbm,
             wu_hbm, wd_hbm, dy_ref, gd_out, gu_out, sums_ref, gb, gp, wu, wd, gd, gu, sems):
        cp = Copies(sems)
        got_wd = cp.start(wd_hbm, wd)
        got_gp = cp.start(gp_hbm, gp)
        got_wu = cp.start(wu_hbm, wu)
        got_gb = cp.start(gb_hbm.at[:, pl.ds(0, d)], gb)
        grad = dh_ref[...] + (d0_ref[...].astype(F32) + d1_ref[...].astype(F32))
        n = n_ref[...]
        tops = [sums_of(grad, n)]
        for i in range(8):
            tops.append(jnp.sum(oh_ref[:, i : i + 1].astype(F32) * grad, axis=0, keepdims=True))
        sums_ref[...] = jnp.concatenate(tops, axis=0)
        dh2 = norm_back(grad, n, r_ref[...], nv_ref[1:2])
        dm = dh2.astype(BF16)
        cp.wait(got_wd, got_gp)
        du = (nn(dm, wd[...]) * gp[...].astype(F32)).astype(BF16)
        cp.wait(got_wu)
        dy_ref[...] = dh2 + nt(du, wu[...])
        cp.wait(got_gb)
        gd[...] = tn(dm, gb[...])
        own_rows(cp, blocked, blk_ref, gd, gd_out)
        gu[...] = tn(yb_ref[...], du[:, :d])
        own_rows(cp, blocked, blk_ref, gu, gu_out)
        cp.wait_all()

    return call(
        body,
        (sds((rows, d), F32), sds((own, d), F32), sds((own, d), F32), sds((16, d), F32)),
        (WHOLE, ANY, ANY, WHOLE),
        [SMEM] + [WHOLE] * 8 + [ANY] * 4,
        [
            VMEM((rows, d), BF16),
            VMEM((rows, 4 * d), BF16),
            VMEM((d, 4 * d), BF16),
            VMEM((d, 4 * d), BF16),
            VMEM((d, d), F32),
            VMEM((d, d), F32),
            DMA((6,)),
        ],
        us=7,
    )(blk, dh, d0, d1, onehot, nl, rl, ybl, nv, gb_, gp_, wu_, wd_)


def swap(axis, size, bit, value):
    return lax.ppermute(value, axis, [(i, i ^ bit) for i in range(size)])


core_swap = functools.partial(swap, "tensor", 4, 1)
y_swap = functools.partial(swap, "tensor", 4, 2)
x_swap = functools.partial(swap, "dp", 8, 1)


def z_swap(k, value):
    return swap("dp", 8, 2 * k, value)


def tied(*trees):
    return lax.optimization_barrier(trees)


ATTN_PIECES = (
    [(0, (), 0, 0, 0)]
    + [(1, (k - 1,), 0, 0, k) for k in (1, 2, 3)]
    + [(2, (), 0, 1, 0), (3, (), 1, 0, 0)]
    + [(4, (k - 1,), 0, 1, k) for k in (1, 2, 3)]
    + [(5, (k - 1,), 1, 0, k) for k in (1, 2, 3)]
    + [(6, (k,), 1, 1, k) for k in (0, 1)]
    + [(7, (k - 2,), 1, 1, k) for k in (2, 3)]
)
MLP_PIECES = (
    [(0, (k,), 0, 0, k) for k in range(4)]
    + [(1, (k,), 0, 1, k) for k in range(4)]
    + [(2, (k,), 1, 0, k) for k in range(4)]
    + [(3, (k,), 1, 1, k) for k in (0, 1)]
    + [(4, (k - 2,), 1, 1, k) for k in (2, 3)]
)


def both_cores(pieces, count):
    return [
        (count * c + which, lead, 2 * c + y, 4 * x + z)
        for c in range(2)
        for which, lead, y, x, z in pieces
    ]


PLAIN_PLAN = [(0, (), j, None) for j in range(4)]


def xor_order(stacked, index, bits):
    shape = stacked.shape
    out = stacked.reshape((2,) * bits + shape[1:])
    for b in range(bits):
        out = jnp.where((index >> (bits - 1 - b)) & 1 == 1, jnp.flip(out, b), out)
    return out.reshape(shape)


def add(*parts):
    total = parts[0].astype(F32)
    for p in parts[1:]:
        total = total + p.astype(F32)
    return total


def low_add(*parts):
    return add(*parts).astype(BF16)


class Scatter:
    def __init__(self, g0, g1_swapped):
        self.g = (g0, g1_swapped)

    def own(self, y, x, zs):
        return tuple(g[y, x, zs] for g in self.g)

    def diagonal(self):
        return low_add(*self.own(1, 1, slice(0, 2))), low_add(*self.own(1, 1, slice(2, 4)))

    def columns(self, from_x, from_y):
        lo, hi = slice(0, 2), slice(2, 4)
        to_x = jnp.concatenate([low_add(*self.own(0, 1, lo)), low_add(*self.own(0, 1, hi), from_y)])
        to_y = jnp.concatenate([low_add(*self.own(1, 0, lo), from_x), low_add(*self.own(1, 0, hi))])
        return to_x, to_y

    def planes(self, from_x, from_y):
        self.mine = (*self.own(0, 0, 0), from_x[0], from_y[0])
        return [low_add(*self.own(0, 0, k), from_x[k], from_y[k]) for k in (1, 2, 3)]

    def last(self, back):
        return add(*self.mine, *back)


def body(tokens, w_qkv, w_out, w_up, w_down, norm_gain, norm_bias, seg_table, seg_ids, cotangent):
    nd, ntens = lax.axis_size("dp"), lax.axis_size("tensor")
    fast = nd == 8
    di, ti = lax.axis_index("dp"), lax.axis_index("tensor")
    seqs, toks, d = tokens.shape
    rows, dblk = seqs * toks, tokens.shape[2] // nd
    per_dev = toks // SEG
    x = tokens.reshape(rows, d)
    cot = cotangent.reshape(rows, d)

    def pack(b):
        return (
            jnp.concatenate([w_qkv[b].reshape(dblk, -1), w_out[b].T], axis=1),
            jnp.stack([w_up[b], w_down[b].T]),
        )

    attn0, mlp0 = pack(0)
    attn1, mlp1 = pack(1)
    small = jnp.concatenate(
        [norm_gain.reshape(4, dblk), norm_bias.reshape(4, dblk), seg_table], axis=0
    )
    onehot = (seg_ids.reshape(-1, 1) == jnp.arange(128, dtype=jnp.int32)).astype(BF16)

    p3 = jnp.concatenate([attn1[None], mlp1])

    def place(leaders):
        leaders = leaders.reshape(seqs, per_dev, -1)
        space = jnp.zeros((seqs, per_dev * ntens, leaders.shape[-1]), BF16)
        return lax.dynamic_update_slice(space, leaders, (0, per_dev * ti, 0)).reshape(
            -1, leaders.shape[-1]
        )

    early = jnp.pad(onehot, ((0, 0), (0, d - onehot.shape[1])))
    early = jnp.stack([place(early), place(cot.reshape(-1, SEG, d)[:, 0])])
    if fast:
        zi, xi = di // 2, di % 2
        blk = jnp.stack([(zi ^ k) * 2 + (xi ^ l) for l in range(2) for k in range(4)]).astype(jnp.int32)
        p1, pu, pd = attn0[None], mlp0[:1], mlp0[1:]

        def z_all(p):
            return [z_swap(k, p) for k in (1, 2, 3)]

        z1, x1, y1 = z_all(p1), x_swap(p1), y_swap(p1)
        x1, small = tied(x1, small)
        sm = jnp.stack([small, x_swap(small)])
        early = early + core_swap(early)
        early = early + y_swap(early)
        z1, x1, y1, pu, early = tied(z1, x1, y1, pu, early)
        p3a = jnp.concatenate([p3[0], early[0]])
        p3u, p3d = p3[1], jnp.concatenate([p3[2], early[1]])
        c1 = jnp.stack(z1)
        xc1, yc1 = x_swap(c1), y_swap(c1)
        zu = z_all(pu)
        xc1, sm = tied(xc1, sm)
        sz = z_all(sm)
        zu, xc1, yc1, pd = tied(zu, xc1, yc1, pd)
        ex1, ey1 = x_swap(jnp.stack([y1, yc1[0]])), y_swap(xc1[1:])
        zd = z_all(pd)
        zd, ex1, ey1 = tied(zd, ex1, ey1)
        mine1 = [p1, c1, x1, y1, xc1, yc1, ex1, ey1]
        attn_pieces = mine1 + [core_swap(v) for v in mine1]
        attn_plan = both_cores(ATTN_PIECES, 8)
        c2 = jnp.stack([jnp.concatenate(v) for v in zip([pu] + zu, [pd] + zd)])
        xc2, yc2 = x_swap(c2), y_swap(c2)
        p3a = tied(p3a, zd)[0]
        z3a = z_all(p3a)
        slots = xor_order(jnp.stack([sm] + sz).reshape(nd, 16, dblk), di, 3)
        nv = slots.transpose(1, 0, 2).reshape(16, d).astype(F32)
    else:
        blk = jnp.zeros((8,), jnp.int32)

        def whole(p):
            g = lax.all_gather(p, ("tensor", "dp"), axis=0)
            g = g.reshape(ntens, nd, p.shape[0], dblk, d).transpose(0, 2, 1, 3, 4)
            g = g.reshape(ntens, p.shape[0], d, d)
            return xor_order(g, ti, 2)

        attn_pieces, mlp_pieces = [whole(attn0[None])], [whole(mlp0)]
        attn_plan = mlp_plan = PLAIN_PLAN
        w1 = lax.all_gather(p3, "dp", axis=1, tiled=True)
        w1a, w1m = [w1[:1]], [w1[1:]]
        nv = lax.all_gather(small, "dp", axis=1, tiled=True).astype(F32)
    w_a, qkv, o, p, y, n1, r1, y_first = attn_forward(attn_plan, blk, x, nv, attn_pieces)
    if fast:
        y_first, z3a = tied(y_first, z3a)

    pay = place(y_first[:, 0])
    if fast:
        pay = pay + core_swap(pay)
        pay = pay + y_swap(pay)
        xc2, yc2, p3u, pay = tied(xc2, yc2, p3u, pay)
        ex2, ey2 = x_swap(yc2[:2]), y_swap(xc2[2:])
        z3u = z_all(p3u)
        pay = jnp.stack([pay, x_swap(pay)])
        ex2, ey2, pay, z3u, p3d = tied(ex2, ey2, pay, z3u, p3d)
        mine2 = [c2, xc2, yc2, ex2, ey2]
        mlp_pieces = mine2 + [core_swap(v) for v in mine2]
        mlp_plan = both_cores(MLP_PIECES, 5)
        pay = jnp.stack([pay] + z_all(pay))
        first = 0
        z3d = z_all(p3d)
        w1a = jnp.stack([p3a] + z3a)
        w1a = [w1a, x_swap(w1a)]
        lead_hot = jnp.stack(w1a, axis=1)[:, :, dblk:, :128].reshape(-1, 128)
    else:
        pay = lax.all_gather(lax.psum(pay, "tensor"), "dp", axis=0)
        early = lax.all_gather(lax.psum(early, "tensor"), "dp", axis=1)
        lead_hot, lead_cot = early[0, ..., :128].reshape(-1, 128), early[1].reshape(-1, d)
        first = di * seqs * per_dev * ntens
    lead_y = pay.reshape(-1, d)

    wu, wd, gbl, gpl, zl, nl, rl = lead_forward(mlp_plan, blk, lead_y, nv, mlp_pieces)
    if fast:
        z3d, zl = tied(z3d, zl)
        w1m = jnp.stack([jnp.concatenate(v) for v in zip([p3u] + z3u, [p3d] + z3d)])
        w1m = [w1m, x_swap(w1m)]
        lead_cot = jnp.stack(w1m, axis=1)[:, :, 2 * dblk :].reshape(-1, d)

    def near_sum(part):
        if fast:
            return low_add(part, core_swap(part))
        return lax.psum(part.astype(F32), "tensor")

    def far_sum(half):
        return y_swap(half) if fast else jnp.zeros_like(half)

    c, cqkv, co, cp, ca = cross_attn(blk, zl, lead_hot, nv, w1a)
    s1 = near_sum(ca)
    t1 = far_sum(s1)
    y, s1 = tied(y, s1)
    gb, gp, yb, dm, dh2, result, sums2 = mlp_forward(y, cot, nv, wu, wd)
    t1, sums2, w1m = tied(t1, sums2, w1m)
    cy, cn, cr, cgb, cgp, cm = cross_mlp(blk, c, s1, t1, nv, w1m)
    s2 = near_sum(cm)
    t2 = far_sum(s2)
    dm, s2 = tied(dm, s2)
    g1, dy = mlp_backward(1, nd, fast, blk, dm, yb, gb, gp, wu, wd, dh2)
    t2, dy = tied(t2, dy)
    e, cdh2, cgd, cgu, cdy, csum2 = cross_mlp_back(
        nd, fast, blk, cy, s2, t2, lead_cot, nv, cgb, cgp, w1m
    )
    if fast:

        def shards(g):
            return g.reshape(2, 2, 4, *g.shape[2:])

        other_m, cdy = tied(core_swap(shards(g1)), cdy)
    s3 = near_sum(cdy)
    t3 = far_sum(s3)
    dy, s3 = tied(dy, s3)
    g0, dy = mlp_backward(0, nd, fast, blk, dm, yb, gb, gp, wu, wd, dy)
    if fast:
        sm_ = Scatter(shards(g0), other_m)
        ops = sm_.diagonal()
        t3, ops = tied(t3, ops)
        diag = x_swap(ops[0]), y_swap(ops[1])
    t3, dy = tied(t3, dy)
    cdh, cdx, cga, csum1 = cross_attn_back(
        nd, fast, blk, cdh2, s3, t3, cn, cr, c, cqkv, co, cp, nv, w1a
    )
    s4 = near_sum(cdx)
    t4 = far_sum(s4)
    if fast:
        diag, s4 = tied(diag, s4)
        ops = sm_.columns(*diag)
        t4, ops = tied(t4, ops)
        cols = x_swap(ops[0]), y_swap(ops[1])
    dyl, lgd, lgu, lsum = lead_backward(
        nd, fast, blk, cdh, s4, t4, lead_hot, nl, rl, lead_y, nv, gbl, gpl, wu, wd
    )

    def own_leaders(full):
        part = lax.dynamic_slice_in_dim(full, first, seqs * per_dev * ntens, 0)
        part = part.reshape(seqs, per_dev * ntens, d)
        return lax.dynamic_slice_in_dim(part, per_dev * ti, per_dev, 1).reshape(-1, d)

    first_in = (dy, own_leaders(dyl), n1, r1, nv, sums2)
    a1, dx, da, sums = attn_backward(1, nd, fast, blk, x, qkv, o, p, w_a, first_in, None)
    if fast:
        cols, dx = tied(cols, dx)
        ops = sm_.planes(*cols)
        dx, ops = tied(dx, ops)
        planes = [z_swap(kk, op) for kk, op in zip((1, 2, 3), ops)]
        other = core_swap(shards(a1))
    a0, dx = attn_backward(0, nd, fast, blk, x, qkv, o, p, w_a, None, (da, dx, sums))

    if fast:
        sa = Scatter(shards(a0), other)
        ops = sa.diagonal()
        diag = x_swap(ops[0]), y_swap(ops[1])
        planes, diag = tied(planes, diag)
        ops = sa.columns(*diag)
        cols = x_swap(ops[0]), y_swap(ops[1])
        ops = sa.planes(*cols)
        gm = sm_.last(planes)
        ga = sa.last([z_swap(kk, op) for kk, op in zip((1, 2, 3), ops)])[0]
        norm_sums = ga[dblk : dblk + 8, :dblk]
        ga = ga[:dblk]
    else:

        def owned(lo, hi):
            g = jnp.concatenate([lo, hi])
            g = xor_order(g, ti, 2).astype(F32)
            g = lax.psum_scatter(g, "tensor", scatter_dimension=0)
            return lax.psum_scatter(g, "dp", scatter_dimension=1, tiled=True)

        gm, ga = owned(g0, g1), owned(a0, a1)[0]
        norm_sums = lax.psum_scatter(
            lax.psum(sums, "tensor"), "dp", scatter_dimension=1, tiled=True
        )

    def rows_of(full):
        if fast:
            return full
        return lax.dynamic_slice_in_dim(full, di * dblk, dblk, 0)

    def cols_of(full):
        return lax.dynamic_slice_in_dim(full, di * dblk, dblk, 1)

    gu0, gd0 = gm[0] + rows_of(lgu), gm[1] + rows_of(lgd)
    ga1, gu1, gd1 = rows_of(cga), rows_of(cgu), rows_of(cgd)
    wide = w_qkv.shape[3] * 3
    grad_qkv = jnp.stack([ga[:, :wide], ga1[:, :wide]]).reshape(w_qkv.shape)
    grad_out = jnp.stack([ga[:, wide:].T, ga1[:, wide:].T])
    grad_up = jnp.stack([gu0, gu1])
    grad_down = jnp.stack([gd0.T, gd1.T])
    lsum, csum1, csum2 = cols_of(lsum), cols_of(csum1), cols_of(csum2)
    grad_gain = jnp.stack(
        [
            jnp.stack([norm_sums[0], norm_sums[2] + lsum[0]]),
            jnp.stack([csum1[0], csum2[0]]),
        ]
    )
    grad_bias = jnp.stack(
        [
            jnp.stack([norm_sums[1], norm_sums[3] + lsum[1]]),
            jnp.stack([csum1[1], csum2[1]]),
        ]
    )
    result = result.reshape(-1, SEG, d).at[:, 0].set(own_leaders(e)).reshape(tokens.shape)
    return (
        result,
        dx.reshape(tokens.shape),
        grad_qkv,
        grad_out,
        grad_up,
        grad_down,
        grad_gain,
        grad_bias,
        lsum[8:16],
    )


def solution(mesh):
    return jax.shard_map(
        body,
        mesh=mesh,
        in_specs=(
            P("dp", "tensor", None),
            P(None, "dp", None, "tensor"),
            P(None, "tensor", "dp"),
            P(None, "dp", "tensor"),
            P(None, "tensor", "dp"),
            P(None, None, "dp"),
            P(None, None, "dp"),
            P(None, "dp"),
            P("dp", "tensor"),
            P("dp", "tensor", None),
        ),
        out_specs=(
            P("dp", "tensor", None),
            P("dp", "tensor", None),
            P(None, "dp", None, "tensor"),
            P(None, "tensor", "dp"),
            P(None, "dp", "tensor"),
            P(None, "tensor", "dp"),
            P(None, None, "dp"),
            P(None, None, "dp"),
            P(None, "dp"),
        ),
        check_vma=False,
    )
```

```python
import functools
import math

import jax
import jax.numpy as jnp
from jax import lax
from jax.experimental import pallas as pl
from jax.experimental.pallas import tpu as pltpu
from jax.sharding import PartitionSpec as P

HEAD = 64
SEG = 128
GROUP = 8
F32, BF16 = jnp.float32, jnp.bfloat16
VMEM = pltpu.VMEM
ANY = pl.BlockSpec(memory_space=pl.ANY)
WHOLE = pl.BlockSpec(memory_space=pltpu.VMEM)
SMEM = pl.BlockSpec(memory_space=pltpu.SMEM)
PARAMS = pltpu.CompilerParams(vmem_limit_bytes=60 << 20)
EPS = 1e-05
SCALE = HEAD ** (-0.5)
RSQRT2 = 1.0 / math.sqrt(2.0)
RSQRT2PI = 1.0 / math.sqrt(2.0 * math.pi)


def nn(a, b):
    return lax.dot_general(a, b, (((1,), (0,)), ((), ())), preferred_element_type=F32)


def nt(a, b):
    return lax.dot_general(a, b, (((1,), (1,)), ((), ())), preferred_element_type=F32)


def tn(a, b):
    return lax.dot_general(a, b, (((0,), (0,)), ((), ())), preferred_element_type=F32)


def norm_parts(h):
    center = h - jnp.mean(h, axis=-1, keepdims=True)
    rstd = lax.rsqrt(jnp.mean(center * center, axis=-1, keepdims=True) + EPS)
    return center * rstd, rstd


def norm_back(grad, normed, rstd, gain):
    dn = grad * gain
    return rstd * (
        dn
        - jnp.mean(dn, axis=-1, keepdims=True)
        - normed * jnp.mean(dn * normed, axis=-1, keepdims=True)
    )


def gelu_both(u):
    cdf = 0.5 + 0.5 * lax.erf(u * RSQRT2)
    return u * cdf, cdf + u * (jnp.exp(-0.5 * u * u) * RSQRT2PI)


def halves(pair):
    lane = lax.broadcasted_iota(jnp.int32, pair.shape, 1)
    zero = jnp.zeros_like(pair)
    return jnp.concatenate(
        [jnp.where(lane < HEAD, pair, zero), jnp.where(lane < HEAD, zero, pair)], axis=0
    )


def unhalve(stacked):
    lane = lax.broadcasted_iota(jnp.int32, (SEG, 2 * HEAD), 1)
    return jnp.where(lane < HEAD, stacked[:SEG], stacked[SEG:])


def half_softmax(s):
    top = jnp.concatenate(
        [
            jnp.broadcast_to(jnp.max(s[:, :SEG], axis=-1, keepdims=True), (SEG, SEG)),
            jnp.broadcast_to(jnp.max(s[:, SEG:], axis=-1, keepdims=True), (SEG, SEG)),
        ],
        axis=1,
    )
    ex = jnp.exp(s - top)
    inv = jnp.concatenate(
        [
            jnp.broadcast_to(1.0 / jnp.sum(ex[:, :SEG], axis=-1, keepdims=True), (SEG, SEG)),
            jnp.broadcast_to(1.0 / jnp.sum(ex[:, SEG:], axis=-1, keepdims=True), (SEG, SEG)),
        ],
        axis=1,
    )
    return ex * inv


def call(body, outs, out_specs, in_specs, scratch=(), us=10):
    return pl.pallas_call(
        body,
        out_shape=outs,
        in_specs=in_specs,
        out_specs=out_specs,
        scratch_shapes=list(scratch),
        compiler_params=PARAMS,
        cost_estimate=pl.CostEstimate(flops=int(us * 2e9), bytes_accessed=1, transcendentals=0),
    )


def sds(shape, dtype):
    return jax.ShapeDtypeStruct(shape, dtype)


DMA = pltpu.SemaphoreType.DMA


class Copies:
    def __init__(self, sems):
        self.sems, self.used, self.open = sems, 0, []

    def start(self, src, dst):
        copy = pltpu.make_async_copy(src, dst, self.sems.at[self.used])
        self.used += 1
        copy.start()
        self.open.append(copy)
        return copy

    def wait(self, *copies):
        for c in copies:
            if any(c is other for other in self.open):
                self.open = [other for other in self.open if other is not c]
                c.wait()

    def wait_all(self):
        for c in self.open:
            c.wait()
        self.open = []


def fetch(cp, plan, pieces, pack, blk_ref, dst, d):
    out = []
    for which, lead, start, j, slot in plan:
        rows = d if slot is None else d // 8
        src = pieces[which].at[(*lead, pl.ds((start + pack) * rows, rows))]
        at = pl.ds(0 if slot is None else pl.multiple_of(blk_ref[slot] * rows, 16), rows)
        out.append(cp.start(src, dst.at[at, pl.ds(j * d, d)]))
    return out


def row_tiles(rows, tile):
    return [slice(i, min(i + tile, rows)) for i in range(0, rows, tile)]


def attn_forward(plan, blk, x, pieces):
    rows, d = x.shape
    segs, quarter = rows // SEG, d // 4
    pairs = d // SEG
    np_ = len(pieces)

    def body(blk_ref, x_hbm, *refs):
        ins, refs = refs[:np_], refs[np_:]
        w_out, qkv_out, o_out, p_out, n_out, r_ref, nl_ref = refs[:7]
        raw, w, x_s, qkv, o_s, p_s, n_s, sems = refs[7:]
        cp = Copies(sems)
        got = fetch(cp, plan, ins, 0, blk_ref, raw, d)
        got_x = cp.start(x_hbm, x_s)
        cp.wait(*got)
        for t in range(4):
            for half in range(2):
                j = 2 * half
                at = slice(t * d + j * quarter, t * d + (j + 2) * quarter)
                w[:, at] = jnp.concatenate(
                    [
                        raw[:, j * d + t * quarter : j * d + (t + 1) * quarter],
                        raw[:, (j + 1) * d + t * quarter : (j + 1) * d + (t + 1) * quarter],
                    ],
                    axis=1,
                )
        cp.start(w, w_out)
        cp.wait(got_x)
        qkv[...] = nn(x_s[...], w[:, : 3 * d]).astype(BF16)
        cp.start(qkv, qkv_out)
        for t in range(segs):
            at = slice(t * SEG, (t + 1) * SEG)
            probs = []
            for pair in range(pairs):
                lo = pair * SEG
                s = nt(qkv[at, lo : lo + SEG], halves(qkv[at, d + lo : d + lo + SEG])) * SCALE
                probs.append(half_softmax(s).astype(BF16))
            for pair in range(pairs):
                lo = pair * SEG
                p_s[t, pair] = probs[pair]
                o_s[at, lo : lo + SEG] = nn(
                    probs[pair], halves(qkv[at, 2 * d + lo : 2 * d + lo + SEG])
                ).astype(BF16)
            cp.start(p_s.at[t], p_out.at[t])
        cp.start(o_s, o_out)
        n_s[...] = nt(o_s[...], w[:, 3 * d :])
        for t in range(segs):
            at = slice(t * SEG, (t + 1) * SEG)
            n, r = norm_parts(x_s[at].astype(F32) + n_s[at])
            n_s[at] = n
            r_ref[at] = r
            nl_ref[t] = n[0:8].astype(BF16)
            cp.start(n_s.at[at], n_out.at[at])
        cp.wait_all()

    return call(
        body,
        (
            sds((d, 4 * d), BF16),
            sds((rows, 3 * d), BF16),
            sds((rows, d), BF16),
            sds((segs, pairs, SEG, 2 * SEG), BF16),
            sds((rows, d), F32),
            sds((rows, 1), F32),
            sds((segs, 8, d), BF16),
        ),
        (ANY,) * 5 + (WHOLE,) * 2,
        [SMEM, ANY] + [ANY] * np_,
        [
            VMEM((d, 4 * d), BF16),
            VMEM((d, 4 * d), BF16),
            VMEM((rows, d), BF16),
            VMEM((rows, 3 * d), BF16),
            VMEM((rows, d), BF16),
            VMEM((segs, pairs, SEG, 2 * SEG), BF16),
            VMEM((rows, d), F32),
            DMA((len(plan) + 4 + 2 * segs,)),
        ],
        us=30,
    )(blk, x, *pieces)


def lead_forward(plan, blk, lead_n, nv, pieces):
    leads, d = lead_n.shape
    np_ = len(pieces)

    def body(blk_ref, ln_ref, nv_ref, *refs):
        ins, refs = refs[:np_], refs[np_:]
        wu_out, wd_out, yb_ref, gb_ref, gp_ref, zl_ref, nl_ref, rl_ref, wu, wd, sems = refs

        def lead_y(at):
            return ln_ref[at].astype(F32) * nv_ref[0:1] + nv_ref[4:5]

        cp = Copies(sems)
        got_u = fetch(cp, plan, ins, 0, blk_ref, wu, d)
        got_d = fetch(cp, plan, ins, 1, blk_ref, wd, d)
        cp.wait(*got_u)
        cp.start(wu, wu_out)
        for at in row_tiles(leads, SEG):
            yb_ref[at] = lead_y(at).astype(BF16)
            g, gd = gelu_both(nn(yb_ref[at], wu[...]))
            gb_ref[at] = g.astype(BF16)
            gp_ref[at] = gd.astype(BF16)
        cp.wait(*got_d)
        cp.start(wd, wd_out)
        for at in row_tiles(leads, SEG):
            n, r = norm_parts(lead_y(at) + nt(gb_ref[at], wd[...]))
            zl_ref[at] = n * nv_ref[1:2] + nv_ref[5:6]
            nl_ref[at] = n
            rl_ref[at] = r
        cp.wait_all()

    return call(
        body,
        (
            sds((d, 4 * d), BF16),
            sds((d, 4 * d), BF16),
            sds((leads, d), BF16),
            sds((leads, 4 * d), BF16),
            sds((leads, 4 * d), BF16),
            sds((leads, d), F32),
            sds((leads, d), F32),
            sds((leads, 1), F32),
        ),
        (ANY, ANY) + (WHOLE,) * 6,
        [SMEM, WHOLE, WHOLE] + [ANY] * np_,
        [VMEM((d, 4 * d), BF16), VMEM((d, 4 * d), BF16), DMA((2 * len(plan) + 2,))],
        us=20,
    )(blk, lead_n, nv, *pieces)


def put_blocks(cp, blocked, blk_ref, src, out, y, pack, slots):
    if not blocked:
        cp.start(src, out.at[y, pack])
        return
    rows = src.shape[0] // slots
    for s in range(slots):
        at = pl.ds(pl.multiple_of(blk_ref[s] * rows, 16), rows)
        cp.start(src.at[at], out.at[y, s, pack, pl.ds(0, rows)])


def mlp_forward(slots, blocked, blk, n1, cot, nv, wu_, wd_):
    rows, d = n1.shape
    half, dblk = 2 * d, d // slots
    per = slots if blocked else 1

    def body(blk_ref, y_hbm, cot_hbm, nv_ref, wu_hbm, wd_hbm, *refs):
        gb_out, gp_out, yb_out, dm_out, g_out, dy_out, res_out, sums_ref = refs[:8]
        y_s, cot_s, wu, wd, yb, gb, gp, dm, dh_s, res, du, gd, gu, sems = refs[8:]
        cp = Copies(sems)
        got_y = cp.start(y_hbm, y_s)
        up, down = [], []
        for j in range(4):
            cols = pl.ds(j * d, d)
            up.append(cp.start(wu_hbm.at[:, cols], wu.at[:, cols]))
        down.append(cp.start(wd_hbm, wd))
        got_cot = cp.start(cot_hbm, cot_s)
        cp.wait(got_y)
        y_s[...] = y_s[...] * nv_ref[0:1] + nv_ref[4:5]
        yb[...] = y_s[...].astype(BF16)
        cp.start(yb, yb_out)
        for j in range(4):
            cols = slice(j * d, (j + 1) * d)
            cp.wait(up[j])
            act, slope = gelu_both(nn(yb[...], wu[:, cols]))
            gb[:, cols] = act.astype(BF16)
            gp[:, cols] = slope.astype(BF16)
            if j < 2:
                cp.start(gb.at[:, pl.ds(j * d, d)], gb_out.at[:, pl.ds(j * d, d)])
                cp.start(gp.at[:, pl.ds(j * d, d)], gp_out.at[:, pl.ds(j * d, d)])
        cp.wait(*down)
        cp.wait(got_cot)
        gain, bias = nv_ref[1:2], nv_ref[5:6]
        top, bottom = jnp.zeros((1, d), F32), jnp.zeros((1, d), F32)
        dh_s[...] = nt(gb[...], wd[...])
        for at in row_tiles(rows, SEG):
            n, r = norm_parts(y_s[at] + dh_s[at])
            res[at] = (n * gain + bias).astype(BF16)
            row = lax.broadcasted_iota(jnp.int32, (SEG, d), 0)
            grad = jnp.where(row == 0, 0.0, cot_s[at].astype(F32))
            top += jnp.sum(grad * n, axis=0, keepdims=True)
            bottom += jnp.sum(grad, axis=0, keepdims=True)
            dh = norm_back(grad, n, r, gain)
            dh_s[at] = dh
            dm[at] = dh.astype(BF16)
            for s, out in ((res, res_out), (dm, dm_out)):
                cp.start(s.at[at], out.at[at])
        sums_ref[...] = jnp.concatenate([top, bottom, jnp.zeros((6, d), F32)], axis=0)
        for y in range(2):
            mine = slice(y * d, (y + 1) * d)
            wide = slice(half + y * d, half + (y + 1) * d)
            gd[:, mine] = tn(dm[...], gb[:, wide]).astype(BF16)
            put_blocks(cp, blocked, blk_ref, gd.at[:, pl.ds(y * d, d)], g_out, y, 1, slots)
            du[:, mine] = (nn(dm[...], wd[:, wide]) * gp[:, wide].astype(F32)).astype(BF16)
        for y in range(2):
            mine = slice(y * d, (y + 1) * d)
            gu[:, mine] = tn(yb[...], du[:, mine]).astype(BF16)
            put_blocks(cp, blocked, blk_ref, gu.at[:, pl.ds(y * d, d)], g_out, y, 0, slots)
        y_s[...] = dh_s[...] + nt(du[...], wu[:, half:])
        cp.start(y_s, dy_out)
        cp.wait_all()

    g_shape = (2, slots, 2, dblk, d) if blocked else (2, 2, d, d)

    return call(
        body,
        (
            sds((rows, half), BF16),
            sds((rows, half), BF16),
            sds((rows, d), BF16),
            sds((rows, d), BF16),
            sds(g_shape, BF16),
            sds((rows, d), F32),
            sds((rows, d), BF16),
            sds((8, d), F32),
        ),
        (ANY,) * 7 + (WHOLE,),
        [SMEM, ANY, ANY, WHOLE, ANY, ANY],
        [
            VMEM((rows, d), F32),
            VMEM((rows, d), BF16),
            VMEM((d, 4 * d), BF16),
            VMEM((d, 4 * d), BF16),
            VMEM((rows, d), BF16),
            VMEM((rows, 4 * d), BF16),
            VMEM((rows, 4 * d), BF16),
            VMEM((rows, d), BF16),
            VMEM((rows, d), F32),
            VMEM((rows, d), BF16),
            VMEM((rows, half), BF16),
            VMEM((d, half), BF16),
            VMEM((d, half), BF16),
            DMA((14 + 2 * (rows // SEG) + 4 * per,)),
        ],
        us=0.01,
    )(blk, n1, cot, nv, wu_, wd_)


def mlp_backward(slots, blocked, blk, dm_, yb_, gb_, gp_, wu_, wd_, start_):
    rows, d = dm_.shape
    dblk = d // slots
    per = slots if blocked else 1
    half = 2 * d

    def body(blk_ref, dm_hbm, yb_hbm, gb_hbm, gp_hbm, wu_hbm, wd_hbm, st_hbm, g_out, dy_out, *scr):
        dm, yb, gb, gp, wu, wd, st, du, gd, gu, dy, sems = scr
        cp = Copies(sems)
        cols = pl.ds(0, half)
        got_dm = cp.start(dm_hbm, dm)
        got_gb = cp.start(gb_hbm, gb)
        got_wd = cp.start(wd_hbm.at[:, cols], wd)
        got_gp = cp.start(gp_hbm, gp)
        got_yb = cp.start(yb_hbm, yb)
        got_wu = cp.start(wu_hbm.at[:, cols], wu)
        got_st = cp.start(st_hbm, st)
        cp.wait(got_dm, got_gb)
        for y in range(2):
            mine = slice(y * d, (y + 1) * d)
            gd[:, mine] = tn(dm[...], gb[:, mine]).astype(BF16)
            put_blocks(cp, blocked, blk_ref, gd.at[:, pl.ds(y * d, d)], g_out, y, 1, slots)
        cp.wait(got_wd, got_gp)
        for y in range(2):
            mine = slice(y * d, (y + 1) * d)
            du[:, mine] = (nn(dm[...], wd[:, mine]) * gp[:, mine].astype(F32)).astype(BF16)
        cp.wait(got_yb)
        for y in range(2):
            mine = slice(y * d, (y + 1) * d)
            gu[:, mine] = tn(yb[...], du[:, mine]).astype(BF16)
            put_blocks(cp, blocked, blk_ref, gu.at[:, pl.ds(y * d, d)], g_out, y, 0, slots)
        cp.wait(got_wu, got_st)
        dy[...] = st[...] + nt(du[...], wu[...])
        cp.start(dy, dy_out)
        cp.wait_all()

    g_shape = (2, slots, 2, dblk, d) if blocked else (2, 2, d, d)
    return call(
        body,
        (sds(g_shape, BF16), sds((rows, d), F32)),
        (ANY, ANY),
        [SMEM] + [ANY] * 7,
        [
            VMEM((rows, d), BF16),
            VMEM((rows, d), BF16),
            VMEM((rows, half), BF16),
            VMEM((rows, half), BF16),
            VMEM((d, half), BF16),
            VMEM((d, half), BF16),
            VMEM((rows, d), F32),
            VMEM((rows, half), BF16),
            VMEM((d, half), BF16),
            VMEM((d, half), BF16),
            VMEM((rows, d), F32),
            DMA((7 + 4 * per + rows // (2 * SEG),)),
        ],
        us=8,
    )(blk, dm_, yb_, gb_, gp_, wu_, wd_, start_)


def own_rows(cp, blocked, blk_ref, src, out):
    if blocked:
        rows = out.shape[0]
        src = src.at[pl.ds(pl.multiple_of(blk_ref[0] * rows, 8), rows)]
    cp.start(src, out)


def sums_of(grad, n):
    d = grad.shape[1]
    return jnp.concatenate(
        [
            jnp.sum(grad * n, axis=0, keepdims=True),
            jnp.sum(grad, axis=0, keepdims=True),
            jnp.zeros((6, d), F32),
        ],
        axis=0,
    )


LEAD_INS = [WHOLE] * 7 + [ANY] * 4


def lead_scratch(rows, d):
    return [
        VMEM((rows, d), BF16),
        VMEM((rows, 4 * d), BF16),
        VMEM((d, 4 * d), BF16),
        VMEM((d, 4 * d), BF16),
        VMEM((d, d), F32),
        VMEM((d, d), F32),
    ]


def lead_fetch(cp, ins, scr):
    gb_hbm, gp_hbm, wu_hbm, wd_hbm = ins[7:]
    gb, gp, wu, wd, _, _ = scr
    d = gb.shape[1]
    got = [cp.start(wd_hbm, wd), cp.start(gp_hbm, gp), cp.start(wu_hbm, wu)]
    return got + [cp.start(gb_hbm.at[:, pl.ds(0, d)], gb)]


def lead_grads(cp, blocked, blk_ref, nv_ref, ins, scr, got, dy_ref, gd_out, gu_out, sums_ref):
    dh_ref, d0_ref, d1_ref, oh_ref, n_ref, r_ref, yb_ref = ins[:7]
    gb, gp, wu, wd, gd, gu = scr
    d = gb.shape[1]
    grad = dh_ref[...] + (d0_ref[...].astype(F32) + d1_ref[...].astype(F32))
    n = n_ref[...]
    tops = [sums_of(grad, n)]
    for i in range(8):
        tops.append(jnp.sum(oh_ref[:, i : i + 1].astype(F32) * grad, axis=0, keepdims=True))
    sums_ref[...] = jnp.concatenate(tops, axis=0)
    dh2 = norm_back(grad, n, r_ref[...], nv_ref[1:2])
    dm = dh2.astype(BF16)
    cp.wait(*got[:2])
    du = (nn(dm, wd[...]) * gp[...].astype(F32)).astype(BF16)
    cp.wait(got[2])
    dy_ref[...] = dh2 + nt(du, wu[...])
    cp.wait(got[3])
    gd[...] = tn(dm, gb[...])
    own_rows(cp, blocked, blk_ref, gd, gd_out)
    gu[...] = tn(yb_ref[...], du[:, :d])
    own_rows(cp, blocked, blk_ref, gu, gu_out)


def lead_backward(slots, blocked, blk, nv, lead):
    rows, d = lead[0].shape
    own = d // slots if blocked else d
    n_in = len(lead)

    def body(blk_ref, nv_ref, *refs):
        ins, refs = refs[:n_in], refs[n_in:]
        dy_ref, gd_out, gu_out, sums_ref, *scr, sems = refs
        cp = Copies(sems)
        got = lead_fetch(cp, ins, scr)
        lead_grads(cp, blocked, blk_ref, nv_ref, ins, scr, got, dy_ref, gd_out, gu_out, sums_ref)
        cp.wait_all()

    return call(
        body,
        (sds((rows, d), F32), sds((own, d), F32), sds((own, d), F32), sds((16, d), F32)),
        (WHOLE, ANY, ANY, WHOLE),
        [SMEM, WHOLE] + LEAD_INS,
        lead_scratch(rows, d) + [DMA((6,))],
        us=7,
    )(blk, nv, *lead)


def attn_backward(core, slots, blocked, blk, x_, qkv_, o_, p_, w_, first, rest, lead=None):
    rows, d = x_.shape
    segs, half, quarter = rows // SEG, d // 2, d // 4
    dblk = d // slots
    per = slots if blocked else 1
    pairs = half // SEG
    opening = first is not None
    extra = first if opening else rest
    inside = lead is not None
    leads = lead[0].shape[0] if inside else 0
    lead = tuple(lead) if inside else ()

    def body(blk_ref, x_hbm, qkv_hbm, o_hbm, p_hbm, w_hbm, *refs):
        more, refs = refs[: len(extra)], refs[len(extra) :]
        lead_ins, refs = refs[: len(lead)], refs[len(lead) :]
        n_out = (4 if opening else 2) + (3 if inside else 0)
        outs, scr = refs[:n_out], refs[n_out:]
        g_out, dx_out = outs[:2]
        x, qkv, o, p, w, st, da, do, dqkv, gr, ex, dx, sems = scr[:13]
        cp = Copies(sems)
        if opening:
            dy_hbm, ld_ref, n_hbm, r_ref, nv_ref, s2_ref = more
            da_out, sums_ref = outs[2:4]
            nb = scr[13]
            if inside:
                got_lead = lead_fetch(cp, lead_ins, scr[15:])
            got_dy = cp.start(dy_hbm, st)
            got_n = cp.start(n_hbm, nb)
        else:
            da_hbm, st_hbm, sums_ref = more
            got_da = cp.start(da_hbm, da)
        got_w = [
            cp.start(w_hbm.at[:, pl.ds(t * d + core * half, half)], w.at[:, pl.ds(t * half, half)])
            for t in (3, 0, 1, 2)
        ]
        got_qkv = [
            cp.start(
                qkv_hbm.at[:, pl.ds(t * d + core * half, half)], qkv.at[:, pl.ds(t * half, half)]
            )
            for t in (2, 0, 1)
        ]
        got_p = cp.start(p_hbm.at[:, pl.ds(core * pairs, pairs)], p)
        got_o = cp.start(o_hbm.at[:, pl.ds(core * half, half)], o)
        got_x = cp.start(x_hbm, x)
        if inside:
            lead_grads(
                cp, blocked, blk_ref, nv_ref, lead_ins, scr[15:], got_lead, scr[14], *outs[4:]
            )
        if opening:
            cp.wait(got_dy, got_n)
            top, bottom = jnp.zeros((1, d), F32), jnp.zeros((1, d), F32)
            for t in range(segs):
                at = slice(t * SEG, (t + 1) * SEG)
                row = lax.broadcasted_iota(jnp.int32, (SEG, d), 0)
                mine = scr[14][pl.ds(ld_ref[t], 1)] if inside else ld_ref[t : t + 1]
                grad = st[at] + jnp.where(row == 0, mine, 0.0)
                n = nb[at]
                top += jnp.sum(grad * n, axis=0, keepdims=True)
                bottom += jnp.sum(grad, axis=0, keepdims=True)
                dh = norm_back(grad, n, r_ref[at], nv_ref[0:1])
                st[at] = dh
                da[at] = dh.astype(BF16)
            cp.start(da, da_out)
            sums_ref[...] = jnp.concatenate(
                [top, bottom, s2_ref[0:2], jnp.zeros((4, d), F32)], axis=0
            )
        else:
            got_st = cp.start(st_hbm, st)
            cp.wait(got_da)
        if blocked:
            for b in range(slots):
                ex[b] = jnp.zeros((16, d), BF16)
                ex[b, 0:8, 0:dblk] = sums_ref[:, b * dblk : (b + 1) * dblk].astype(BF16)
            for y in range(2):
                for s in range(slots):
                    cp.start(ex.at[blk_ref[s]], g_out.at[y, s, 0, pl.ds(dblk, 16)])
        cp.wait(got_w[0])
        do[...] = nn(da[...], w[:, 3 * half :]).astype(BF16)
        cp.wait(got_p, *got_qkv)
        for t in range(segs):
            at = slice(t * SEG, (t + 1) * SEG)
            dss = []
            for pair in range(pairs):
                mine = slice(pair * SEG, (pair + 1) * SEG)
                pf = p[t, pair].astype(F32)
                v = qkv[at, 2 * half + pair * SEG : 2 * half + (pair + 1) * SEG]
                pd = pf * nt(do[at, mine], halves(v))
                parts = [
                    pd[:, c] - pf[:, c] * jnp.sum(pd[:, c], axis=-1, keepdims=True)
                    for c in (slice(0, SEG), slice(SEG, 2 * SEG))
                ]
                dss.append(jnp.concatenate(parts, axis=1).astype(BF16))
            for pair in range(pairs):
                mine = slice(pair * SEG, (pair + 1) * SEG)
                q, k = (qkv[at, i * half + pair * SEG : i * half + (pair + 1) * SEG] for i in (0, 1))
                ds = dss[pair]
                dv = unhalve(tn(p[t, pair], do[at, mine]))
                dk = unhalve(tn(ds, q)) * SCALE
                dq = nn(ds, halves(k)) * SCALE
                for i, g in enumerate((dq, dk, dv)):
                    dqkv[at, i * half + pair * SEG : i * half + (pair + 1) * SEG] = g.astype(BF16)
        cp.wait(got_x, got_o)
        gf = tn(x[...], dqkv[...]).astype(BF16)
        go = tn(da[...], o[...]).astype(BF16)
        for y in range(2):
            at = slice(y * quarter, (y + 1) * quarter)
            cut = [gf[:, i * half + y * quarter : i * half + (y + 1) * quarter] for i in range(3)]
            cut.append(go[:, at])
            gr[y, :, :half] = jnp.concatenate(cut[:2], axis=1)
            gr[y, :, half:] = jnp.concatenate(cut[2:], axis=1)
            put_blocks(cp, blocked, blk_ref, gr.at[y], g_out, y, 0, slots)
        if not opening:
            cp.wait(got_st)
        cp.wait(*got_w)
        dx[...] = st[...] + nt(dqkv[...], w[:, : 3 * half])
        cp.start(dx, dx_out)
        cp.wait_all()

    g_shape = (2, slots, 1, dblk + 16, d) if blocked else (2, 1, d, d)
    outs = [sds(g_shape, BF16), sds((rows, d), F32)]
    specs = [ANY, ANY]
    in_more = [ANY, ANY, WHOLE]
    if opening:
        outs += [sds((rows, d), BF16), sds((8, d), F32)]
        specs += [ANY, WHOLE]
        in_more = [ANY, SMEM if inside else WHOLE, ANY, WHOLE, WHOLE, WHOLE]
    if inside:
        own = d // slots if blocked else d
        outs += [sds((own, d), F32), sds((own, d), F32), sds((16, d), F32)]
        specs += [ANY, ANY, WHOLE]
        in_more += LEAD_INS
    scratch = [
        VMEM((rows, d), BF16),
        VMEM((rows, 3 * half), BF16),
        VMEM((rows, half), BF16),
        VMEM((segs, pairs, SEG, 2 * SEG), BF16),
        VMEM((d, 4 * half), BF16),
        VMEM((rows, d), F32),
        VMEM((rows, d), BF16),
        VMEM((rows, half), BF16),
        VMEM((rows, 3 * half), BF16),
        VMEM((2, d, d), BF16),
        VMEM((slots if blocked else 1, 16, d), BF16),
        VMEM((rows, d), F32),
        DMA((24 + 4 * per,)),
    ]
    if opening:
        scratch.append(VMEM((rows, d), F32))
    if inside:
        scratch += [VMEM((leads, d), F32)] + lead_scratch(leads, d)
    return call(
        body,
        tuple(outs),
        tuple(specs),
        [SMEM] + [ANY] * 5 + in_more,
        scratch,
        us=30,
    )(blk, x_, qkv_, o_, p_, w_, *extra, *lead)


def fetch_cross(cp, pieces, blk_ref, dst):
    if len(pieces) == 1:
        return [cp.start(pieces[0], dst)]
    packs, d, _ = dst.shape
    rows = d // 8
    out = []
    for slot in range(8):
        at = pl.ds(pl.multiple_of(blk_ref[slot] * rows, 16), rows)
        for p in range(packs):
            src = pieces[slot // 4].at[slot % 4, pl.ds(p * rows, rows)]
            out.append(cp.start(src, dst.at[p, at]))
    return out


def group_mask():
    a = lax.broadcasted_iota(jnp.int32, (SEG, SEG), 0) // GROUP
    b = lax.broadcasted_iota(jnp.int32, (SEG, SEG), 1) // GROUP
    return a == b


def cross_attn(blk, zl, onehot, nv, w):
    rows, d = zl.shape
    quarter = d // 4
    heads = quarter // HEAD
    tiles = rows // SEG

    def body(blk_ref, z_ref, oh_ref, nv_ref, *refs):
        c_ref, qkv_ref, o_ref, p_ref, a_ref, w_s, sems = refs[len(w) :]
        cp = Copies(sems)
        fetch_cross(cp, refs[: len(w)], blk_ref, w_s)
        cs = []
        for at in row_tiles(rows, SEG):
            c = z_ref[at]
            for i in range(8):
                c += oh_ref[at, i : i + 1].astype(F32) * nv_ref[8 + i : 9 + i]
            c_ref[at] = c
            cs.append(c.astype(BF16))
        cp.wait_all()
        mask = group_mask()
        for t, at in enumerate(row_tiles(rows, SEG)):
            qkv = nn(cs[t], w_s[0, :, : 3 * quarter]).astype(BF16)
            qkv_ref[at] = qkv
            cut = [
                [qkv[:, i * quarter + h * HEAD : i * quarter + (h + 1) * HEAD] for i in range(3)]
                for h in range(heads)
            ]
            probs = []
            for q, k, v in cut:
                s = jnp.where(mask, nt(q, k) * SCALE, -1e30)
                ex = jnp.exp(s - jnp.max(s, axis=-1, keepdims=True))
                probs.append((ex * (1.0 / jnp.sum(ex, axis=-1, keepdims=True))).astype(BF16))
            os = []
            for h in range(heads):
                p_ref[t, h] = probs[h]
                os.append(nn(probs[h], cut[h][2]).astype(BF16))
            o = jnp.concatenate(os, axis=1)
            o_ref[at] = o
            a_ref[at] = nt(o, w_s[0, :, 3 * quarter :]).astype(BF16)

    return call(
        body,
        (
            sds((rows, d), F32),
            sds((rows, 3 * quarter), BF16),
            sds((rows, quarter), BF16),
            sds((tiles, heads, SEG, SEG), BF16),
            sds((rows, d), BF16),
        ),
        (WHOLE,) * 5,
        [SMEM] + [WHOLE] * 3 + [ANY] * len(w),
        [VMEM((1, d, d), BF16), DMA((8,))],
        us=0.01,
    )(blk, zl, onehot, nv, *w)


def cross_mlp(blk, c, a0, a1, nv, w):
    rows, d = c.shape

    def body(blk_ref, c_ref, a0_ref, a1_ref, nv_ref, *refs):
        y_ref, n_ref, r_ref, gb_ref, gp_ref, m_ref, w_s, sems = refs[len(w) :]
        cp = Copies(sems)
        fetch_cross(cp, refs[: len(w)], blk_ref, w_s)
        n, r = norm_parts(c_ref[...] + (a0_ref[...].astype(F32) + a1_ref[...].astype(F32)))
        n_ref[...] = n
        r_ref[...] = r
        y = n * nv_ref[2:3] + nv_ref[6:7]
        y_ref[...] = y
        cp.wait_all()
        g, gd = gelu_both(nn(y.astype(BF16), w_s[0]))
        gb_ref[...] = g.astype(BF16)
        gp_ref[...] = gd.astype(BF16)
        m_ref[...] = nt(gb_ref[...], w_s[1]).astype(BF16)

    return call(
        body,
        (
            sds((rows, d), F32),
            sds((rows, d), F32),
            sds((rows, 1), F32),
            sds((rows, d), BF16),
            sds((rows, d), BF16),
            sds((rows, d), BF16),
        ),
        (WHOLE,) * 6,
        [SMEM] + [WHOLE] * 4 + [ANY] * len(w),
        [VMEM((2, d, d), BF16), DMA((16,))],
        us=4,
    )(blk, c, a0, a1, nv, *w)


def cross_mlp_back(slots, blocked, blk, y, m0, m1, cot, nv, gb, gp, w):
    rows, d = y.shape
    own = d // slots if blocked else d

    def body(blk_ref, y_ref, m0_ref, m1_ref, cot_ref, nv_ref, gb_ref, gp_ref, *refs):
        (e_ref, dh_ref, gd_out, gu_out, dy_ref, sums_ref, w_s, gd, gu, sems) = refs[len(w) :]
        cp = Copies(sems)
        got = fetch_cross(cp, refs[: len(w)], blk_ref, w_s)
        gain = nv_ref[3:4]
        n, r = norm_parts(y_ref[...] + (m0_ref[...].astype(F32) + m1_ref[...].astype(F32)))
        e_ref[...] = (n * gain + nv_ref[7:8]).astype(BF16)
        grad = cot_ref[...].astype(F32)
        sums_ref[...] = sums_of(grad, n)
        dh = norm_back(grad, n, r, gain)
        dh_ref[...] = dh
        dm = dh.astype(BF16)
        cp.wait(*got)
        du = (nn(dm, w_s[1]) * gp_ref[...].astype(F32)).astype(BF16)
        dy_ref[...] = nt(du, w_s[0]).astype(BF16)
        gd[...] = tn(dm, gb_ref[...])
        own_rows(cp, blocked, blk_ref, gd, gd_out)
        gu[...] = tn(y_ref[...].astype(BF16), du)
        own_rows(cp, blocked, blk_ref, gu, gu_out)
        cp.wait_all()

    return call(
        body,
        (
            sds((rows, d), BF16),
            sds((rows, d), F32),
            sds((own, d), F32),
            sds((own, d), F32),
            sds((rows, d), BF16),
            sds((8, d), F32),
        ),
        (WHOLE, WHOLE, ANY, ANY, WHOLE, WHOLE),
        [SMEM] + [WHOLE] * 7 + [ANY] * len(w),
        [VMEM((2, d, d), BF16), VMEM((d, d), F32), VMEM((d, d), F32), DMA((18,))],
        us=30,
    )(blk, y, m0, m1, cot, nv, gb, gp, *w)


def cross_attn_back(slots, blocked, blk, dh2, d0, d1, n1, r1, c, qkv, o, p, nv, w):
    rows, d = dh2.shape
    quarter = d // 4
    heads = quarter // HEAD
    own = d // slots if blocked else d

    def body(blk_ref, dh2_ref, d0_ref, d1_ref, n_ref, r_ref, c_ref, qkv_ref, o_ref, p_ref, nv_ref,
             *refs):
        dh_ref, dx_ref, g_out, sums_ref, da_s, dqkv_s, w_s, g, sems = refs[len(w) :]
        cp = Copies(sems)
        got = fetch_cross(cp, refs[: len(w)], blk_ref, w_s)
        grad = dh2_ref[...] + (d0_ref[...].astype(F32) + d1_ref[...].astype(F32))
        n = n_ref[...]
        sums_ref[...] = sums_of(grad, n)
        dh = norm_back(grad, n, r_ref[...], nv_ref[2:3])
        dh_ref[...] = dh
        da_s[...] = dh.astype(BF16)
        cp.wait(*got)
        for t, at in enumerate(row_tiles(rows, SEG)):
            do = nn(da_s[at], w_s[0, :, 3 * quarter :]).astype(BF16)
            qkv_t = qkv_ref[at]
            cut = [
                [qkv_t[:, i * quarter + h * HEAD : i * quarter + (h + 1) * HEAD] for i in range(3)]
                for h in range(heads)
            ]
            dos = [do[:, h * HEAD : (h + 1) * HEAD] for h in range(heads)]
            dss = []
            for h in range(heads):
                pf = p_ref[t, h].astype(F32)
                pd = pf * nt(dos[h], cut[h][2])
                dss.append((pd - pf * jnp.sum(pd, axis=-1, keepdims=True)).astype(BF16))
            dq, dk, dv = [], [], []
            for h in range(heads):
                dv.append(tn(p_ref[t, h], dos[h]).astype(BF16))
                dq.append((nn(dss[h], cut[h][1]) * SCALE).astype(BF16))
                dk.append((tn(dss[h], cut[h][0]) * SCALE).astype(BF16))
            dqkv_s[at] = jnp.concatenate(dq + dk + dv, axis=1)
        dx_ref[...] = nt(dqkv_s[...], w_s[0, :, : 3 * quarter]).astype(BF16)
        g[:, : 3 * quarter] = tn(c_ref[...].astype(BF16), dqkv_s[...])
        g[:, 3 * quarter :] = tn(da_s[...], o_ref[...])
        own_rows(cp, blocked, blk_ref, g, g_out)
        cp.wait_all()

    return call(
        body,
        (sds((rows, d), F32), sds((rows, d), BF16), sds((own, d), F32), sds((8, d), F32)),
        (WHOLE, WHOLE, ANY, WHOLE),
        [SMEM] + [WHOLE] * 10 + [ANY] * len(w),
        [
            VMEM((rows, d), BF16),
            VMEM((rows, 3 * quarter), BF16),
            VMEM((1, d, d), BF16),
            VMEM((d, d), F32),
            DMA((9,)),
        ],
        us=5,
    )(blk, dh2, d0, d1, n1, r1, c, qkv, o, p, nv, *w)


def swap(axis, size, bit, value):
    return lax.ppermute(value, axis, [(i, i ^ bit) for i in range(size)])


core_swap = functools.partial(swap, "tensor", 4, 1)
y_swap = functools.partial(swap, "tensor", 4, 2)
x_swap = functools.partial(swap, "dp", 8, 1)


def z_swap(k, value):
    return swap("dp", 8, 2 * k, value)


def tied(*trees):
    return lax.optimization_barrier(trees)


PLANES = ((0, 0), (0, 1), (1, 0))
ATTN_PIECES = (
    [(n, (), 0, y, x, 0) for n, (y, x) in enumerate(PLANES)]
    + [(3 + n, (k - 1,), 0, y, x, k) for n, (y, x) in enumerate(PLANES) for k in (1, 2, 3)]
    + [(6, (k,), 0, 1, 1, k) for k in (0, 1)]
    + [(7, (k - 2,), 0, 1, 1, k) for k in (2, 3)]
)
MLP_PIECES = (
    [(n, (), 1, y, x, 0) for n, (y, x) in enumerate(PLANES)]
    + [(3 + n, (k - 1,), 0, y, x, k) for n, (y, x) in enumerate(PLANES) for k in (1, 2, 3)]
    + [(6, (k,), 0, 1, 1, k) for k in (0, 1)]
    + [(7, (k - 2,), 0, 1, 1, k) for k in (2, 3)]
)


def both_cores(pieces, count):
    return [
        (count * c + which, lead, pack, 2 * c + y, 4 * x + z)
        for c in range(2)
        for which, lead, pack, y, x, z in pieces
    ]


PLAIN_PLAN = [(0, (j,), 0, j, None) for j in range(4)]


def xor_order(stacked, index, bits):
    shape = stacked.shape
    out = stacked.reshape((2,) * bits + shape[1:])
    for b in range(bits):
        out = jnp.where((index >> (bits - 1 - b)) & 1 == 1, jnp.flip(out, b), out)
    return out.reshape(shape)


def add(*parts):
    total = parts[0].astype(F32)
    for p in parts[1:]:
        total = total + p.astype(F32)
    return total


def low_add(*parts):
    return add(*parts).astype(BF16)


class Scatter:
    def __init__(self, g0, g1_swapped):
        self.g = (g0, g1_swapped)

    def own(self, y, x, zs):
        return tuple(g[y, x, zs] for g in self.g)

    def diagonal(self):
        return low_add(*self.own(1, 1, slice(0, 2))), low_add(*self.own(1, 1, slice(2, 4)))

    def columns(self, from_x, from_y):
        lo, hi = slice(0, 2), slice(2, 4)
        to_x = jnp.concatenate([low_add(*self.own(0, 1, lo)), low_add(*self.own(0, 1, hi), from_y)])
        to_y = jnp.concatenate([low_add(*self.own(1, 0, lo), from_x), low_add(*self.own(1, 0, hi))])
        return to_x, to_y

    def planes(self, from_x, from_y):
        self.mine = (*self.own(0, 0, 0), from_x[0], from_y[0])
        return [low_add(*self.own(0, 0, k), from_x[k], from_y[k]) for k in (1, 2, 3)]

    def last(self, back):
        return add(*self.mine, *back)


def body(tokens, w_qkv, w_out, w_up, w_down, norm_gain, norm_bias, seg_table, seg_ids, cotangent):
    nd, ntens = lax.axis_size("dp"), lax.axis_size("tensor")
    fast = nd == 8
    di, ti = lax.axis_index("dp"), lax.axis_index("tensor")
    seqs, toks, d = tokens.shape
    rows, dblk = seqs * toks, tokens.shape[2] // nd
    per_dev = toks // SEG
    x = tokens.reshape(rows, d)
    cot = cotangent.reshape(rows, d)

    def pack(b):
        return (
            jnp.concatenate([w_qkv[b].reshape(dblk, -1), w_out[b].T], axis=1),
            jnp.stack([w_up[b], w_down[b].T]),
        )

    attn0, mlp0 = pack(0)
    attn1, mlp1 = pack(1)
    small = jnp.concatenate(
        [norm_gain.reshape(4, dblk), norm_bias.reshape(4, dblk), seg_table], axis=0
    )
    onehot = (seg_ids.reshape(-1, 1) == jnp.arange(128, dtype=jnp.int32)).astype(BF16)

    p3 = jnp.concatenate([attn1[None], mlp1])

    def place(leaders):
        leaders = leaders.reshape(seqs, per_dev, -1)
        space = jnp.zeros((seqs, per_dev * ntens, leaders.shape[-1]), BF16)
        return lax.dynamic_update_slice(space, leaders, (0, per_dev * ti, 0)).reshape(
            -1, leaders.shape[-1]
        )

    early = jnp.pad(onehot, ((0, 0), (0, d - onehot.shape[1])))
    early = jnp.stack([place(early), place(cot.reshape(-1, SEG, d)[:, 0])])
    if fast:
        zi, xi = di // 2, di % 2
        blk = jnp.stack([(zi ^ k) * 2 + (xi ^ l) for l in range(2) for k in range(4)]).astype(jnp.int32)

        def z_all(p):
            return [z_swap(k, p) for k in (1, 2, 3)]

        tiny = jnp.pad(small, ((0, 0), (0, d - dblk)))
        p_all = jnp.concatenate([attn0, mlp0.reshape(-1, d), tiny])
        z1, x0, y0 = z_all(p_all[:dblk]), x_swap(p_all), y_swap(p_all)
        early = early + core_swap(early)
        z1, x0, y0, pm, early = tied(z1, x0, y0, p_all[dblk:], early)
        c1 = jnp.stack(z1)
        xc1, yc1 = x_swap(c1), y_swap(c1)
        zm = z_all(pm)
        xc1, yc1, early = tied(xc1, yc1, early)
        ex1, ey1 = x_swap(jnp.stack([y0[:dblk], yc1[0]])), y_swap(xc1[1:])
        early = early + y_swap(early)
        ex1, ey1, early = tied(ex1, ey1, early)
        p3a = jnp.concatenate([p3[0], early[0]])
        p3u, p3d = p3[1], jnp.concatenate([p3[2], early[1]])
        base = [p_all, x0, y0]
        base_core = [core_swap(v) for v in base]
        mine1 = [c1, xc1, yc1, ex1, ey1]
        attn_pieces = base + mine1 + base_core + [core_swap(v) for v in mine1]
        attn_plan = both_cores(ATTN_PIECES, 8)
        cm = jnp.stack(zm)
        xcm, ycm = x_swap(cm), y_swap(cm)
    else:
        blk = jnp.zeros((8,), jnp.int32)

        def whole(p):
            g = lax.all_gather(p, ("tensor", "dp"), axis=0)
            g = g.reshape(ntens, nd, p.shape[0], dblk, d).transpose(0, 2, 1, 3, 4)
            g = g.reshape(ntens, p.shape[0] * d, d)
            return xor_order(g, ti, 2)

        attn_pieces, mlp_pieces = [whole(attn0[None])], [whole(mlp0)]
        attn_plan = mlp_plan = PLAIN_PLAN
        w1 = lax.all_gather(p3, "dp", axis=1, tiled=True)
        w1a, w1m = [w1[:1]], [w1[1:]]
        nv = lax.all_gather(small, "dp", axis=1, tiled=True).astype(F32)
    w_a, qkv, o, p, n1, r1, n_first = attn_forward(attn_plan, blk, x, attn_pieces)

    pay = place(n_first[:, 0])
    if fast:
        p3a = tied(p3a, n_first)[0]
        z3a = z_all(p3a)
        pay = pay + core_swap(pay)
        pay = pay + y_swap(pay)
        xcm, ycm, z3a, pay = tied(xcm, ycm, z3a, pay)
        to_x, to_y, p3u = tied(jnp.stack([y0[dblk:], ycm[0]]), xcm[1:], p3u)
        ex2, ey2 = x_swap(to_x), y_swap(to_y)
        z3u = z_all(p3u)
        pay = jnp.stack([pay, x_swap(pay)])
        at = 3 * dblk
        tiny = jnp.stack(
            [jnp.stack([p_all[at:], x0[at:]])]
            + [jnp.stack([a[2 * dblk :], b[2 * dblk :]]) for a, b in zip(zm, xcm)]
        )[..., :dblk]
        nv = xor_order(tiny.reshape(nd, 16, dblk), di, 3)
        nv = nv.transpose(1, 0, 2).reshape(16, d).astype(F32)
        ex2, ey2, pay, z3u, p3d = tied(ex2, ey2, pay, z3u, p3d)
        mine2 = [cm, xcm, ycm, ex2, ey2]
        mlp_pieces = base + mine2 + base_core + [core_swap(v) for v in mine2]
        mlp_plan = both_cores(MLP_PIECES, 8)
        pay = jnp.stack([pay] + z_all(pay))
        first = 0
        z3d = z_all(p3d)
        w1a = jnp.stack([p3a] + z3a)
        w1a = [w1a, x_swap(w1a)]
        lead_hot = jnp.stack(w1a, axis=1)[:, :, dblk:, :128].reshape(-1, 128)
    else:
        pay = lax.all_gather(lax.psum(pay, "tensor"), "dp", axis=0)
        early = lax.all_gather(lax.psum(early, "tensor"), "dp", axis=1)
        lead_hot, lead_cot = early[0, ..., :128].reshape(-1, 128), early[1].reshape(-1, d)
        first = di * seqs * per_dev * ntens
    lead_n = pay.reshape(-1, d)

    wu, wd, ybl, gbl, gpl, zl, nl, rl = lead_forward(mlp_plan, blk, lead_n, nv, mlp_pieces)
    if fast:
        z3d, zl = tied(z3d, zl)
        w1m = jnp.stack([jnp.concatenate(v) for v in zip([p3u] + z3u, [p3d] + z3d)])
        w1m = [w1m, x_swap(w1m)]
        lead_cot = jnp.stack(w1m, axis=1)[:, :, 2 * dblk :].reshape(-1, d)

    def near_sum(part):
        if fast:
            return low_add(part, core_swap(part))
        return lax.psum(part.astype(F32), "tensor")

    def far_sum(half):
        return y_swap(half) if fast else jnp.zeros_like(half)

    c, cqkv, co, cp, ca = cross_attn(blk, zl, lead_hot, nv, w1a)
    s1 = near_sum(ca)
    t1 = far_sum(s1)
    n2, s1 = tied(n1, s1)
    gb, gp, yb, dm, g1, dy, result, sums2 = mlp_forward(nd, fast, blk, n2, cot, nv, wu, wd)
    t1, sums2, w1m = tied(t1, sums2, w1m)
    cy, cn, cr, cgb, cgp, cm = cross_mlp(blk, c, s1, t1, nv, w1m)
    s2 = near_sum(cm)
    t2 = far_sum(s2)
    dm, s2 = tied(dm, s2)
    g0, dy = mlp_backward(nd, fast, blk, dm, yb, gb, gp, wu, wd, dy)
    t2, dy = tied(t2, dy)
    e, cdh2, cgd, cgu, cdy, csum2 = cross_mlp_back(
        nd, fast, blk, cy, s2, t2, lead_cot, nv, cgb, cgp, w1m
    )
    if fast:

        def shards(g):
            return g.reshape(2, 2, 4, *g.shape[2:])

        other_m, cdy = tied(core_swap(shards(g1)), cdy)
    s3 = near_sum(cdy)
    t3 = far_sum(s3)
    if fast:
        sm_ = Scatter(shards(g0), other_m)
        ops = sm_.diagonal()
        t3, ops = tied(t3, ops)
        diag = x_swap(ops[0]), y_swap(ops[1])
    t3, dy = tied(t3, dy)
    cdh, cdx, cga, csum1 = cross_attn_back(
        nd, fast, blk, cdh2, s3, t3, cn, cr, c, cqkv, co, cp, nv, w1a
    )
    s4 = near_sum(cdx)
    t4 = far_sum(s4)
    if fast:
        diag, s4 = tied(diag, s4)
        ops = sm_.columns(*diag)
        t4, ops = tied(t4, ops)
        cols = x_swap(ops[0]), y_swap(ops[1])
    def own_leaders(full):
        part = lax.dynamic_slice_in_dim(full, first, seqs * per_dev * ntens, 0)
        part = part.reshape(seqs, per_dev * ntens, d)
        return lax.dynamic_slice_in_dim(part, per_dev * ti, per_dev, 1).reshape(-1, d)

    lead = (cdh, s4, t4, lead_hot, nl, rl, ybl, gbl, gpl, wu, wd)
    if fast:
        spot = jnp.stack([s * per_dev * ntens + per_dev * ti + i for s in range(seqs) for i in range(per_dev)])
        first_in = (dy, spot.astype(jnp.int32), n1, r1, nv, sums2)
        a1, dx, da, sums, lgd, lgu, lsum = attn_backward(
            1, nd, fast, blk, x, qkv, o, p, w_a, first_in, None, lead
        )
    else:
        dyl, lgd, lgu, lsum = lead_backward(nd, fast, blk, nv, lead)
        first_in = (dy, own_leaders(dyl), n1, r1, nv, sums2)
        a1, dx, da, sums = attn_backward(1, nd, fast, blk, x, qkv, o, p, w_a, first_in, None)
    if fast:
        cols, dx = tied(cols, dx)
        ops = sm_.planes(*cols)
        dx, ops = tied(dx, ops)
        planes = [z_swap(kk, op) for kk, op in zip((1, 2, 3), ops)]
        other = core_swap(shards(a1))
    a0, dx = attn_backward(0, nd, fast, blk, x, qkv, o, p, w_a, None, (da, dx, sums))
    dx, e, csum1, csum2, cga, cgu, cgd, lsum, lgd, lgu = tied(
        dx, e, csum1, csum2, cga, cgu, cgd, lsum, lgd, lgu
    )

    if fast:
        sa = Scatter(shards(a0), other)
        ops = sa.diagonal()
        diag = x_swap(ops[0]), y_swap(ops[1])
        planes, diag = tied(planes, diag)
        ops = sa.columns(*diag)
        cols = x_swap(ops[0]), y_swap(ops[1])
        ops = sa.planes(*cols)
        gm = sm_.last(planes)
        ga = sa.last([z_swap(kk, op) for kk, op in zip((1, 2, 3), ops)])[0]
        norm_sums = ga[dblk : dblk + 8, :dblk]
        ga = ga[:dblk]
    else:

        def owned(lo, hi):
            g = jnp.concatenate([lo, hi])
            g = xor_order(g, ti, 2).astype(F32)
            g = lax.psum_scatter(g, "tensor", scatter_dimension=0)
            return lax.psum_scatter(g, "dp", scatter_dimension=1, tiled=True)

        gm, ga = owned(g0, g1), owned(a0, a1)[0]
        norm_sums = lax.psum_scatter(
            lax.psum(sums, "tensor"), "dp", scatter_dimension=1, tiled=True
        )

    def rows_of(full):
        if fast:
            return full
        return lax.dynamic_slice_in_dim(full, di * dblk, dblk, 0)

    def cols_of(full):
        return lax.dynamic_slice_in_dim(full, di * dblk, dblk, 1)

    gu0, gd0 = gm[0] + rows_of(lgu), gm[1] + rows_of(lgd)
    ga1, gu1, gd1 = rows_of(cga), rows_of(cgu), rows_of(cgd)
    wide = w_qkv.shape[3] * 3
    grad_qkv = jnp.stack([ga[:, :wide], ga1[:, :wide]]).reshape(w_qkv.shape)
    grad_out = jnp.stack([ga[:, wide:].T, ga1[:, wide:].T])
    grad_up = jnp.stack([gu0, gu1])
    grad_down = jnp.stack([gd0.T, gd1.T])
    lsum, csum1, csum2 = cols_of(lsum), cols_of(csum1), cols_of(csum2)
    grad_gain = jnp.stack(
        [
            jnp.stack([norm_sums[0], norm_sums[2] + lsum[0]]),
            jnp.stack([csum1[0], csum2[0]]),
        ]
    )
    grad_bias = jnp.stack(
        [
            jnp.stack([norm_sums[1], norm_sums[3] + lsum[1]]),
            jnp.stack([csum1[1], csum2[1]]),
        ]
    )
    result = result.reshape(-1, SEG, d).at[:, 0].set(own_leaders(e)).reshape(tokens.shape)
    return (
        result,
        dx.reshape(tokens.shape),
        grad_qkv,
        grad_out,
        grad_up,
        grad_down,
        grad_gain,
        grad_bias,
        lsum[8:16],
    )


def solution(mesh):
    return jax.shard_map(
        body,
        mesh=mesh,
        in_specs=(
            P("dp", "tensor", None),
            P(None, "dp", None, "tensor"),
            P(None, "tensor", "dp"),
            P(None, "dp", "tensor"),
            P(None, "tensor", "dp"),
            P(None, None, "dp"),
            P(None, None, "dp"),
            P(None, "dp"),
            P("dp", "tensor"),
            P("dp", "tensor", None),
        ),
        out_specs=(
            P("dp", "tensor", None),
            P("dp", "tensor", None),
            P(None, "dp", None, "tensor"),
            P(None, "tensor", "dp"),
            P(None, "dp", "tensor"),
            P(None, "tensor", "dp"),
            P(None, None, "dp"),
            P(None, None, "dp"),
            P(None, "dp"),
        ),
        check_vma=False,
    )
```

```python
import functools
import math

import jax
import jax.numpy as jnp
from jax import lax
from jax.experimental import pallas as pl
from jax.experimental.pallas import tpu as pltpu
from jax.sharding import PartitionSpec as P

HEAD = 64
SEG = 128
GROUP = 8
F32, BF16 = jnp.float32, jnp.bfloat16
VMEM = pltpu.VMEM
ANY = pl.BlockSpec(memory_space=pl.ANY)
WHOLE = pl.BlockSpec(memory_space=pltpu.VMEM)
SMEM = pl.BlockSpec(memory_space=pltpu.SMEM)
PARAMS = pltpu.CompilerParams(vmem_limit_bytes=60 << 20)
EPS = 1e-05
SCALE = HEAD ** (-0.5)
RSQRT2 = 1.0 / math.sqrt(2.0)
RSQRT2PI = 1.0 / math.sqrt(2.0 * math.pi)


def nn(a, b):
    return lax.dot_general(a, b, (((1,), (0,)), ((), ())), preferred_element_type=F32)


def nt(a, b):
    return lax.dot_general(a, b, (((1,), (1,)), ((), ())), preferred_element_type=F32)


def tn(a, b):
    return lax.dot_general(a, b, (((0,), (0,)), ((), ())), preferred_element_type=F32)


def norm_parts(h):
    center = h - jnp.mean(h, axis=-1, keepdims=True)
    rstd = lax.rsqrt(jnp.mean(center * center, axis=-1, keepdims=True) + EPS)
    return center * rstd, rstd


def norm_back(grad, normed, rstd, gain):
    dn = grad * gain
    return rstd * (
        dn
        - jnp.mean(dn, axis=-1, keepdims=True)
        - normed * jnp.mean(dn * normed, axis=-1, keepdims=True)
    )


def gelu_both(u):
    cdf = 0.5 + 0.5 * lax.erf(u * RSQRT2)
    return u * cdf, cdf + u * (jnp.exp(-0.5 * u * u) * RSQRT2PI)


def halves(pair):
    lane = lax.broadcasted_iota(jnp.int32, pair.shape, 1)
    zero = jnp.zeros_like(pair)
    return jnp.concatenate(
        [jnp.where(lane < HEAD, pair, zero), jnp.where(lane < HEAD, zero, pair)], axis=0
    )


def unhalve(stacked):
    lane = lax.broadcasted_iota(jnp.int32, (SEG, 2 * HEAD), 1)
    return jnp.where(lane < HEAD, stacked[:SEG], stacked[SEG:])


def half_softmax(s):
    top = jnp.concatenate(
        [
            jnp.broadcast_to(jnp.max(s[:, :SEG], axis=-1, keepdims=True), (SEG, SEG)),
            jnp.broadcast_to(jnp.max(s[:, SEG:], axis=-1, keepdims=True), (SEG, SEG)),
        ],
        axis=1,
    )
    ex = jnp.exp(s - top)
    inv = jnp.concatenate(
        [
            jnp.broadcast_to(1.0 / jnp.sum(ex[:, :SEG], axis=-1, keepdims=True), (SEG, SEG)),
            jnp.broadcast_to(1.0 / jnp.sum(ex[:, SEG:], axis=-1, keepdims=True), (SEG, SEG)),
        ],
        axis=1,
    )
    return ex * inv


def call(body, outs, out_specs, in_specs, scratch=(), us=10):
    return pl.pallas_call(
        body,
        out_shape=outs,
        in_specs=in_specs,
        out_specs=out_specs,
        scratch_shapes=list(scratch),
        compiler_params=PARAMS,
        cost_estimate=pl.CostEstimate(flops=int(us * 2e9), bytes_accessed=1, transcendentals=0),
    )


def sds(shape, dtype):
    return jax.ShapeDtypeStruct(shape, dtype)


DMA = pltpu.SemaphoreType.DMA


class Copies:
    def __init__(self, sems):
        self.sems, self.used, self.open = sems, 0, []

    def start(self, src, dst):
        copy = pltpu.make_async_copy(src, dst, self.sems.at[self.used])
        self.used += 1
        copy.start()
        self.open.append(copy)
        return copy

    def wait(self, *copies):
        for c in copies:
            if any(c is other for other in self.open):
                self.open = [other for other in self.open if other is not c]
                c.wait()

    def wait_all(self):
        for c in self.open:
            c.wait()
        self.open = []


def fetch(cp, plan, pieces, pack, blk_ref, dst, d):
    out = []
    for which, lead, start, j, slot in plan:
        rows = d if slot is None else d // 8
        src = pieces[which].at[(*lead, pl.ds((start + pack) * rows, rows))]
        at = pl.ds(0 if slot is None else pl.multiple_of(blk_ref[slot] * rows, 16), rows)
        out.append(cp.start(src, dst.at[at, pl.ds(j * d, d)]))
    return out


def row_tiles(rows, tile):
    return [slice(i, min(i + tile, rows)) for i in range(0, rows, tile)]


def attn_forward(plan, blk, x, pieces):
    rows, d = x.shape
    segs, quarter = rows // SEG, d // 4
    pairs = d // SEG
    np_ = len(pieces)

    def body(blk_ref, x_hbm, *refs):
        ins, refs = refs[:np_], refs[np_:]
        w_out, qkv_out, o_out, p_out, n_out, r_ref, nl_ref = refs[:7]
        raw, w, x_s, qkv, o_s, p_s, n_s, sems = refs[7:]
        cp = Copies(sems)
        got = fetch(cp, plan, ins, 0, blk_ref, raw, d)
        got_x = cp.start(x_hbm, x_s)
        cp.wait(*got)
        for t in range(4):
            for half in range(2):
                j = 2 * half
                at = slice(t * d + j * quarter, t * d + (j + 2) * quarter)
                w[:, at] = jnp.concatenate(
                    [
                        raw[:, j * d + t * quarter : j * d + (t + 1) * quarter],
                        raw[:, (j + 1) * d + t * quarter : (j + 1) * d + (t + 1) * quarter],
                    ],
                    axis=1,
                )
        cp.start(w, w_out)
        cp.wait(got_x)
        qkv[...] = nn(x_s[...], w[:, : 3 * d]).astype(BF16)
        cp.start(qkv, qkv_out)
        for t in range(segs):
            at = slice(t * SEG, (t + 1) * SEG)
            probs = []
            for pair in range(pairs):
                lo = pair * SEG
                s = nt(qkv[at, lo : lo + SEG], halves(qkv[at, d + lo : d + lo + SEG])) * SCALE
                probs.append(half_softmax(s).astype(BF16))
            for pair in range(pairs):
                lo = pair * SEG
                p_s[t, pair] = probs[pair]
                o_s[at, lo : lo + SEG] = nn(
                    probs[pair], halves(qkv[at, 2 * d + lo : 2 * d + lo + SEG])
                ).astype(BF16)
            cp.start(p_s.at[t], p_out.at[t])
        cp.start(o_s, o_out)
        n_s[...] = nt(o_s[...], w[:, 3 * d :])
        for t in range(segs):
            at = slice(t * SEG, (t + 1) * SEG)
            n, r = norm_parts(x_s[at].astype(F32) + n_s[at])
            n_s[at] = n
            r_ref[at] = r
            nl_ref[t] = n[0:8].astype(BF16)
            cp.start(n_s.at[at], n_out.at[at])
        cp.wait_all()

    return call(
        body,
        (
            sds((d, 4 * d), BF16),
            sds((rows, 3 * d), BF16),
            sds((rows, d), BF16),
            sds((segs, pairs, SEG, 2 * SEG), BF16),
            sds((rows, d), F32),
            sds((rows, 1), F32),
            sds((segs, 8, d), BF16),
        ),
        (ANY,) * 5 + (WHOLE,) * 2,
        [SMEM, ANY] + [ANY] * np_,
        [
            VMEM((d, 4 * d), BF16),
            VMEM((d, 4 * d), BF16),
            VMEM((rows, d), BF16),
            VMEM((rows, 3 * d), BF16),
            VMEM((rows, d), BF16),
            VMEM((segs, pairs, SEG, 2 * SEG), BF16),
            VMEM((rows, d), F32),
            DMA((len(plan) + 4 + 2 * segs,)),
        ],
        us=30,
    )(blk, x, *pieces)


def lead_forward(plan, blk, lead_n, nv, pieces):
    leads, d = lead_n.shape
    np_ = len(pieces)

    def body(blk_ref, ln_ref, nv_ref, *refs):
        ins, refs = refs[:np_], refs[np_:]
        wu_out, wd_out, yb_ref, gb_ref, gp_ref, zl_ref, nl_ref, rl_ref, wu, wd, sems = refs

        def lead_y(at):
            return ln_ref[at].astype(F32) * nv_ref[0:1] + nv_ref[4:5]

        cp = Copies(sems)
        got_u = fetch(cp, plan, ins, 0, blk_ref, wu, d)
        got_d = fetch(cp, plan, ins, 1, blk_ref, wd, d)
        cp.wait(*got_u)
        cp.start(wu, wu_out)
        for at in row_tiles(leads, SEG):
            yb_ref[at] = lead_y(at).astype(BF16)
            g, gd = gelu_both(nn(yb_ref[at], wu[...]))
            gb_ref[at] = g.astype(BF16)
            gp_ref[at] = gd.astype(BF16)
        cp.wait(*got_d)
        cp.start(wd, wd_out)
        for at in row_tiles(leads, SEG):
            n, r = norm_parts(lead_y(at) + nt(gb_ref[at], wd[...]))
            zl_ref[at] = n * nv_ref[1:2] + nv_ref[5:6]
            nl_ref[at] = n
            rl_ref[at] = r
        cp.wait_all()

    return call(
        body,
        (
            sds((d, 4 * d), BF16),
            sds((d, 4 * d), BF16),
            sds((leads, d), BF16),
            sds((leads, 4 * d), BF16),
            sds((leads, 4 * d), BF16),
            sds((leads, d), F32),
            sds((leads, d), F32),
            sds((leads, 1), F32),
        ),
        (ANY, ANY) + (WHOLE,) * 6,
        [SMEM, WHOLE, WHOLE] + [ANY] * np_,
        [VMEM((d, 4 * d), BF16), VMEM((d, 4 * d), BF16), DMA((2 * len(plan) + 2,))],
        us=20,
    )(blk, lead_n, nv, *pieces)


def put_blocks(cp, blocked, blk_ref, src, out, y, pack, slots):
    if not blocked:
        cp.start(src, out.at[y, pack])
        return
    rows = src.shape[0] // slots
    for s in range(slots):
        at = pl.ds(pl.multiple_of(blk_ref[s] * rows, 16), rows)
        cp.start(src.at[at], out.at[y, s, pack, pl.ds(0, rows)])


def mlp_forward(slots, blocked, blk, n1, cot, nv, wu_, wd_):
    rows, d = n1.shape
    half, dblk = 2 * d, d // slots
    per = slots if blocked else 1

    def body(blk_ref, y_hbm, cot_hbm, nv_ref, wu_hbm, wd_hbm, *refs):
        gb_out, gp_out, yb_out, dm_out, g_out, dy_out, res_out, sums_ref = refs[:8]
        y_s, cot_s, wu, wd, yb, gb, gp, dm, dh_s, res, du, gd, gu, sems = refs[8:]
        cp = Copies(sems)
        got_y = cp.start(y_hbm, y_s)
        up, down = [], []
        for j in range(4):
            cols = pl.ds(j * d, d)
            up.append(cp.start(wu_hbm.at[:, cols], wu.at[:, cols]))
        down.append(cp.start(wd_hbm, wd))
        got_cot = cp.start(cot_hbm, cot_s)
        cp.wait(got_y)
        y_s[...] = y_s[...] * nv_ref[0:1] + nv_ref[4:5]
        yb[...] = y_s[...].astype(BF16)
        cp.start(yb, yb_out)
        for j in range(4):
            cols = slice(j * d, (j + 1) * d)
            cp.wait(up[j])
            act, slope = gelu_both(nn(yb[...], wu[:, cols]))
            gb[:, cols] = act.astype(BF16)
            gp[:, cols] = slope.astype(BF16)
            if j < 2:
                cp.start(gb.at[:, pl.ds(j * d, d)], gb_out.at[:, pl.ds(j * d, d)])
                cp.start(gp.at[:, pl.ds(j * d, d)], gp_out.at[:, pl.ds(j * d, d)])
        cp.wait(*down)
        cp.wait(got_cot)
        gain, bias = nv_ref[1:2], nv_ref[5:6]
        top, bottom = jnp.zeros((1, d), F32), jnp.zeros((1, d), F32)
        dh_s[...] = nt(gb[...], wd[...])
        for at in row_tiles(rows, SEG):
            n, r = norm_parts(y_s[at] + dh_s[at])
            res[at] = (n * gain + bias).astype(BF16)
            row = lax.broadcasted_iota(jnp.int32, (SEG, d), 0)
            grad = jnp.where(row == 0, 0.0, cot_s[at].astype(F32))
            top += jnp.sum(grad * n, axis=0, keepdims=True)
            bottom += jnp.sum(grad, axis=0, keepdims=True)
            dh = norm_back(grad, n, r, gain)
            dh_s[at] = dh
            dm[at] = dh.astype(BF16)
            for s, out in ((res, res_out), (dm, dm_out)):
                cp.start(s.at[at], out.at[at])
        sums_ref[...] = jnp.concatenate([top, bottom, jnp.zeros((6, d), F32)], axis=0)
        for y in range(2):
            mine = slice(y * d, (y + 1) * d)
            wide = slice(half + y * d, half + (y + 1) * d)
            gd[:, mine] = tn(dm[...], gb[:, wide]).astype(BF16)
            put_blocks(cp, blocked, blk_ref, gd.at[:, pl.ds(y * d, d)], g_out, y, 1, slots)
            du[:, mine] = (nn(dm[...], wd[:, wide]) * gp[:, wide].astype(F32)).astype(BF16)
        for y in range(2):
            mine = slice(y * d, (y + 1) * d)
            gu[:, mine] = tn(yb[...], du[:, mine]).astype(BF16)
            put_blocks(cp, blocked, blk_ref, gu.at[:, pl.ds(y * d, d)], g_out, y, 0, slots)
        y_s[...] = dh_s[...] + nt(du[...], wu[:, half:])
        cp.start(y_s, dy_out)
        cp.wait_all()

    g_shape = (2, slots, 2, dblk, d) if blocked else (2, 2, d, d)

    return call(
        body,
        (
            sds((rows, half), BF16),
            sds((rows, half), BF16),
            sds((rows, d), BF16),
            sds((rows, d), BF16),
            sds(g_shape, BF16),
            sds((rows, d), F32),
            sds((rows, d), BF16),
            sds((8, d), F32),
        ),
        (ANY,) * 7 + (WHOLE,),
        [SMEM, ANY, ANY, WHOLE, ANY, ANY],
        [
            VMEM((rows, d), F32),
            VMEM((rows, d), BF16),
            VMEM((d, 4 * d), BF16),
            VMEM((d, 4 * d), BF16),
            VMEM((rows, d), BF16),
            VMEM((rows, 4 * d), BF16),
            VMEM((rows, 4 * d), BF16),
            VMEM((rows, d), BF16),
            VMEM((rows, d), F32),
            VMEM((rows, d), BF16),
            VMEM((rows, half), BF16),
            VMEM((d, half), BF16),
            VMEM((d, half), BF16),
            DMA((14 + 2 * (rows // SEG) + 4 * per,)),
        ],
        us=0.01,
    )(blk, n1, cot, nv, wu_, wd_)


def mlp_backward(slots, blocked, blk, dm_, yb_, gb_, gp_, wu_, wd_, start_):
    rows, d = dm_.shape
    dblk = d // slots
    per = slots if blocked else 1
    half = 2 * d

    def body(blk_ref, dm_hbm, yb_hbm, gb_hbm, gp_hbm, wu_hbm, wd_hbm, st_hbm, g_out, dy_out, *scr):
        dm, yb, gb, gp, wu, wd, st, du, gd, gu, dy, sems = scr
        cp = Copies(sems)
        cols = pl.ds(0, half)
        got_dm = cp.start(dm_hbm, dm)
        got_gb = cp.start(gb_hbm, gb)
        got_wd = cp.start(wd_hbm.at[:, cols], wd)
        got_gp = cp.start(gp_hbm, gp)
        got_yb = cp.start(yb_hbm, yb)
        got_wu = cp.start(wu_hbm.at[:, cols], wu)
        got_st = cp.start(st_hbm, st)
        cp.wait(got_dm, got_gb)
        for y in range(2):
            mine = slice(y * d, (y + 1) * d)
            gd[:, mine] = tn(dm[...], gb[:, mine]).astype(BF16)
            put_blocks(cp, blocked, blk_ref, gd.at[:, pl.ds(y * d, d)], g_out, y, 1, slots)
        cp.wait(got_wd, got_gp)
        for y in range(2):
            mine = slice(y * d, (y + 1) * d)
            du[:, mine] = (nn(dm[...], wd[:, mine]) * gp[:, mine].astype(F32)).astype(BF16)
        cp.wait(got_yb)
        for y in range(2):
            mine = slice(y * d, (y + 1) * d)
            gu[:, mine] = tn(yb[...], du[:, mine]).astype(BF16)
            put_blocks(cp, blocked, blk_ref, gu.at[:, pl.ds(y * d, d)], g_out, y, 0, slots)
        cp.wait(got_wu, got_st)
        dy[...] = st[...] + nt(du[...], wu[...])
        cp.start(dy, dy_out)
        cp.wait_all()

    g_shape = (2, slots, 2, dblk, d) if blocked else (2, 2, d, d)
    return call(
        body,
        (sds(g_shape, BF16), sds((rows, d), F32)),
        (ANY, ANY),
        [SMEM] + [ANY] * 7,
        [
            VMEM((rows, d), BF16),
            VMEM((rows, d), BF16),
            VMEM((rows, half), BF16),
            VMEM((rows, half), BF16),
            VMEM((d, half), BF16),
            VMEM((d, half), BF16),
            VMEM((rows, d), F32),
            VMEM((rows, half), BF16),
            VMEM((d, half), BF16),
            VMEM((d, half), BF16),
            VMEM((rows, d), F32),
            DMA((7 + 4 * per + rows // (2 * SEG),)),
        ],
        us=8,
    )(blk, dm_, yb_, gb_, gp_, wu_, wd_, start_)


def own_rows(cp, blocked, blk_ref, src, out):
    if blocked:
        rows = out.shape[0]
        src = src.at[pl.ds(pl.multiple_of(blk_ref[0] * rows, 8), rows)]
    cp.start(src, out)


def sums_of(grad, n):
    d = grad.shape[1]
    return jnp.concatenate(
        [
            jnp.sum(grad * n, axis=0, keepdims=True),
            jnp.sum(grad, axis=0, keepdims=True),
            jnp.zeros((6, d), F32),
        ],
        axis=0,
    )


LEAD_INS = [WHOLE] * 7 + [ANY] * 4


def lead_scratch(rows, d):
    return [
        VMEM((rows, d), BF16),
        VMEM((rows, 4 * d), BF16),
        VMEM((d, 4 * d), BF16),
        VMEM((d, 4 * d), BF16),
        VMEM((d, d), F32),
        VMEM((d, d), F32),
    ]


def lead_fetch(cp, ins, scr):
    gb_hbm, gp_hbm, wu_hbm, wd_hbm = ins[7:]
    gb, gp, wu, wd, _, _ = scr
    d = gb.shape[1]
    got = [cp.start(wd_hbm, wd), cp.start(gp_hbm, gp), cp.start(wu_hbm, wu)]
    return got + [cp.start(gb_hbm.at[:, pl.ds(0, d)], gb)]


def lead_grads(cp, blocked, blk_ref, nv_ref, ins, scr, got, dy_ref, gd_out, gu_out, sums_ref):
    dh_ref, d0_ref, d1_ref, oh_ref, n_ref, r_ref, yb_ref = ins[:7]
    gb, gp, wu, wd, gd, gu = scr
    d = gb.shape[1]
    grad = dh_ref[...] + (d0_ref[...].astype(F32) + d1_ref[...].astype(F32))
    n = n_ref[...]
    tops = [sums_of(grad, n)]
    for i in range(8):
        tops.append(jnp.sum(oh_ref[:, i : i + 1].astype(F32) * grad, axis=0, keepdims=True))
    sums_ref[...] = jnp.concatenate(tops, axis=0)
    dh2 = norm_back(grad, n, r_ref[...], nv_ref[1:2])
    dm = dh2.astype(BF16)
    cp.wait(*got[:2])
    du = (nn(dm, wd[...]) * gp[...].astype(F32)).astype(BF16)
    cp.wait(got[2])
    dy_ref[...] = dh2 + nt(du, wu[...])
    cp.wait(got[3])
    gd[...] = tn(dm, gb[...])
    own_rows(cp, blocked, blk_ref, gd, gd_out)
    gu[...] = tn(yb_ref[...], du[:, :d])
    own_rows(cp, blocked, blk_ref, gu, gu_out)


def lead_backward(slots, blocked, blk, nv, lead):
    rows, d = lead[0].shape
    own = d // slots if blocked else d
    n_in = len(lead)

    def body(blk_ref, nv_ref, *refs):
        ins, refs = refs[:n_in], refs[n_in:]
        dy_ref, gd_out, gu_out, sums_ref, *scr, sems = refs
        cp = Copies(sems)
        got = lead_fetch(cp, ins, scr)
        lead_grads(cp, blocked, blk_ref, nv_ref, ins, scr, got, dy_ref, gd_out, gu_out, sums_ref)
        cp.wait_all()

    return call(
        body,
        (sds((rows, d), F32), sds((own, d), F32), sds((own, d), F32), sds((16, d), F32)),
        (WHOLE, ANY, ANY, WHOLE),
        [SMEM, WHOLE] + LEAD_INS,
        lead_scratch(rows, d) + [DMA((6,))],
        us=7,
    )(blk, nv, *lead)


def attn_backward(core, slots, blocked, blk, x_, qkv_, o_, p_, w_, first, rest, lead=None):
    rows, d = x_.shape
    segs, half, quarter = rows // SEG, d // 2, d // 4
    dblk = d // slots
    per = slots if blocked else 1
    pairs = half // SEG
    opening = first is not None
    extra = first if opening else rest
    inside = lead is not None
    leads = lead[0].shape[0] if inside else 0
    lead = tuple(lead) if inside else ()

    def body(blk_ref, x_hbm, qkv_hbm, o_hbm, p_hbm, w_hbm, *refs):
        more, refs = refs[: len(extra)], refs[len(extra) :]
        lead_ins, refs = refs[: len(lead)], refs[len(lead) :]
        n_out = (4 if opening else 2) + (3 if inside else 0)
        outs, scr = refs[:n_out], refs[n_out:]
        g_out, dx_out = outs[:2]
        x, qkv, o, p, w, st, da, do, dqkv, gr, ex, dx, sems = scr[:13]
        cp = Copies(sems)
        if opening:
            dy_hbm, ld_ref, n_hbm, r_ref, nv_ref, s2_ref = more
            da_out, sums_ref = outs[2:4]
            nb = scr[13]
            if inside:
                got_lead = lead_fetch(cp, lead_ins, scr[15:])
            got_dy = cp.start(dy_hbm, st)
            got_n = cp.start(n_hbm, nb)
        else:
            da_hbm, st_hbm, sums_ref = more
            got_da = cp.start(da_hbm, da)
        got_w = [
            cp.start(w_hbm.at[:, pl.ds(t * d + core * half, half)], w.at[:, pl.ds(t * half, half)])
            for t in (3, 0, 1, 2)
        ]
        got_qkv = [
            cp.start(
                qkv_hbm.at[:, pl.ds(t * d + core * half, half)], qkv.at[:, pl.ds(t * half, half)]
            )
            for t in (2, 0, 1)
        ]
        got_p = cp.start(p_hbm.at[:, pl.ds(core * pairs, pairs)], p)
        got_o = cp.start(o_hbm.at[:, pl.ds(core * half, half)], o)
        got_x = cp.start(x_hbm, x)
        if inside:
            lead_grads(
                cp, blocked, blk_ref, nv_ref, lead_ins, scr[15:], got_lead, scr[14], *outs[4:]
            )
        if opening:
            cp.wait(got_dy, got_n)
            top, bottom = jnp.zeros((1, d), F32), jnp.zeros((1, d), F32)
            for t in range(segs):
                at = slice(t * SEG, (t + 1) * SEG)
                row = lax.broadcasted_iota(jnp.int32, (SEG, d), 0)
                mine = scr[14][pl.ds(ld_ref[t], 1)] if inside else ld_ref[t : t + 1]
                grad = st[at] + jnp.where(row == 0, mine, 0.0)
                n = nb[at]
                top += jnp.sum(grad * n, axis=0, keepdims=True)
                bottom += jnp.sum(grad, axis=0, keepdims=True)
                dh = norm_back(grad, n, r_ref[at], nv_ref[0:1])
                st[at] = dh
                da[at] = dh.astype(BF16)
            cp.start(da, da_out)
            sums_ref[...] = jnp.concatenate(
                [top, bottom, s2_ref[0:2], jnp.zeros((4, d), F32)], axis=0
            )
        else:
            got_st = cp.start(st_hbm, st)
            cp.wait(got_da)
        if blocked:
            for b in range(slots):
                ex[b] = jnp.zeros((16, d), BF16)
                ex[b, 0:8, 0:dblk] = sums_ref[:, b * dblk : (b + 1) * dblk].astype(BF16)
            for y in range(2):
                for s in range(slots):
                    cp.start(ex.at[blk_ref[s]], g_out.at[y, s, 0, pl.ds(dblk, 16)])
        cp.wait(got_w[0])
        do[...] = nn(da[...], w[:, 3 * half :]).astype(BF16)
        cp.wait(got_p, *got_qkv)
        for t in range(segs):
            at = slice(t * SEG, (t + 1) * SEG)
            dss = []
            for pair in range(pairs):
                mine = slice(pair * SEG, (pair + 1) * SEG)
                pf = p[t, pair].astype(F32)
                v = qkv[at, 2 * half + pair * SEG : 2 * half + (pair + 1) * SEG]
                pd = pf * nt(do[at, mine], halves(v))
                parts = [
                    pd[:, c] - pf[:, c] * jnp.sum(pd[:, c], axis=-1, keepdims=True)
                    for c in (slice(0, SEG), slice(SEG, 2 * SEG))
                ]
                dss.append(jnp.concatenate(parts, axis=1).astype(BF16))
            for pair in range(pairs):
                mine = slice(pair * SEG, (pair + 1) * SEG)
                q, k = (qkv[at, i * half + pair * SEG : i * half + (pair + 1) * SEG] for i in (0, 1))
                ds = dss[pair]
                dv = unhalve(tn(p[t, pair], do[at, mine]))
                dk = unhalve(tn(ds, q)) * SCALE
                dq = nn(ds, halves(k)) * SCALE
                for i, g in enumerate((dq, dk, dv)):
                    dqkv[at, i * half + pair * SEG : i * half + (pair + 1) * SEG] = g.astype(BF16)
        cp.wait(got_x, got_o)
        gf = tn(x[...], dqkv[...]).astype(BF16)
        go = tn(da[...], o[...]).astype(BF16)
        for y in range(2):
            at = slice(y * quarter, (y + 1) * quarter)
            cut = [gf[:, i * half + y * quarter : i * half + (y + 1) * quarter] for i in range(3)]
            cut.append(go[:, at])
            gr[y, :, :half] = jnp.concatenate(cut[:2], axis=1)
            gr[y, :, half:] = jnp.concatenate(cut[2:], axis=1)
            put_blocks(cp, blocked, blk_ref, gr.at[y], g_out, y, 0, slots)
        if not opening:
            cp.wait(got_st)
        cp.wait(*got_w)
        dx[...] = st[...] + nt(dqkv[...], w[:, : 3 * half])
        cp.start(dx, dx_out)
        cp.wait_all()

    g_shape = (2, slots, 1, dblk + 16, d) if blocked else (2, 1, d, d)
    outs = [sds(g_shape, BF16), sds((rows, d), F32)]
    specs = [ANY, ANY]
    in_more = [ANY, ANY, WHOLE]
    if opening:
        outs += [sds((rows, d), BF16), sds((8, d), F32)]
        specs += [ANY, WHOLE]
        in_more = [ANY, SMEM if inside else WHOLE, ANY, WHOLE, WHOLE, WHOLE]
    if inside:
        own = d // slots if blocked else d
        outs += [sds((own, d), F32), sds((own, d), F32), sds((16, d), F32)]
        specs += [ANY, ANY, WHOLE]
        in_more += LEAD_INS
    scratch = [
        VMEM((rows, d), BF16),
        VMEM((rows, 3 * half), BF16),
        VMEM((rows, half), BF16),
        VMEM((segs, pairs, SEG, 2 * SEG), BF16),
        VMEM((d, 4 * half), BF16),
        VMEM((rows, d), F32),
        VMEM((rows, d), BF16),
        VMEM((rows, half), BF16),
        VMEM((rows, 3 * half), BF16),
        VMEM((2, d, d), BF16),
        VMEM((slots if blocked else 1, 16, d), BF16),
        VMEM((rows, d), F32),
        DMA((24 + 4 * per,)),
    ]
    if opening:
        scratch.append(VMEM((rows, d), F32))
    if inside:
        scratch += [VMEM((leads, d), F32)] + lead_scratch(leads, d)
    return call(
        body,
        tuple(outs),
        tuple(specs),
        [SMEM] + [ANY] * 5 + in_more,
        scratch,
        us=30,
    )(blk, x_, qkv_, o_, p_, w_, *extra, *lead)


def fetch_cross(cp, pieces, blk_ref, dst):
    if len(pieces) == 1:
        return [cp.start(pieces[0], dst)]
    packs, d, _ = dst.shape
    rows = d // 8
    out = []
    for slot in range(8):
        at = pl.ds(pl.multiple_of(blk_ref[slot] * rows, 16), rows)
        for p in range(packs):
            src = pieces[slot // 4].at[slot % 4, pl.ds(p * rows, rows)]
            out.append(cp.start(src, dst.at[p, at]))
    return out


def group_mask():
    a = lax.broadcasted_iota(jnp.int32, (SEG, SEG), 0) // GROUP
    b = lax.broadcasted_iota(jnp.int32, (SEG, SEG), 1) // GROUP
    return a == b


def cross_attn(blk, zl, onehot, nv, w):
    rows, d = zl.shape
    quarter = d // 4
    heads = quarter // HEAD
    tiles = rows // SEG

    def body(blk_ref, z_ref, oh_ref, nv_ref, *refs):
        c_ref, qkv_ref, o_ref, p_ref, a_ref, w_s, sems = refs[len(w) :]
        cp = Copies(sems)
        fetch_cross(cp, refs[: len(w)], blk_ref, w_s)
        cs = []
        for at in row_tiles(rows, SEG):
            c = z_ref[at]
            for i in range(8):
                c += oh_ref[at, i : i + 1].astype(F32) * nv_ref[8 + i : 9 + i]
            c_ref[at] = c
            cs.append(c.astype(BF16))
        cp.wait_all()
        mask = group_mask()
        for t, at in enumerate(row_tiles(rows, SEG)):
            qkv = nn(cs[t], w_s[0, :, : 3 * quarter]).astype(BF16)
            qkv_ref[at] = qkv
            cut = [
                [qkv[:, i * quarter + h * HEAD : i * quarter + (h + 1) * HEAD] for i in range(3)]
                for h in range(heads)
            ]
            probs = []
            for q, k, v in cut:
                s = jnp.where(mask, nt(q, k) * SCALE, -1e30)
                ex = jnp.exp(s - jnp.max(s, axis=-1, keepdims=True))
                probs.append((ex * (1.0 / jnp.sum(ex, axis=-1, keepdims=True))).astype(BF16))
            os = []
            for h in range(heads):
                p_ref[t, h] = probs[h]
                os.append(nn(probs[h], cut[h][2]).astype(BF16))
            o = jnp.concatenate(os, axis=1)
            o_ref[at] = o
            a_ref[at] = nt(o, w_s[0, :, 3 * quarter :]).astype(BF16)

    return call(
        body,
        (
            sds((rows, d), F32),
            sds((rows, 3 * quarter), BF16),
            sds((rows, quarter), BF16),
            sds((tiles, heads, SEG, SEG), BF16),
            sds((rows, d), BF16),
        ),
        (WHOLE,) * 5,
        [SMEM] + [WHOLE] * 3 + [ANY] * len(w),
        [VMEM((1, d, d), BF16), DMA((8,))],
        us=0.01,
    )(blk, zl, onehot, nv, *w)


def cross_mlp(blk, c, a0, a1, nv, w):
    rows, d = c.shape

    def body(blk_ref, c_ref, a0_ref, a1_ref, nv_ref, *refs):
        y_ref, n_ref, r_ref, gb_ref, gp_ref, m_ref, w_s, sems = refs[len(w) :]
        cp = Copies(sems)
        fetch_cross(cp, refs[: len(w)], blk_ref, w_s)
        n, r = norm_parts(c_ref[...] + (a0_ref[...].astype(F32) + a1_ref[...].astype(F32)))
        n_ref[...] = n
        r_ref[...] = r
        y = n * nv_ref[2:3] + nv_ref[6:7]
        y_ref[...] = y
        cp.wait_all()
        g, gd = gelu_both(nn(y.astype(BF16), w_s[0]))
        gb_ref[...] = g.astype(BF16)
        gp_ref[...] = gd.astype(BF16)
        m_ref[...] = nt(gb_ref[...], w_s[1]).astype(BF16)

    return call(
        body,
        (
            sds((rows, d), F32),
            sds((rows, d), F32),
            sds((rows, 1), F32),
            sds((rows, d), BF16),
            sds((rows, d), BF16),
            sds((rows, d), BF16),
        ),
        (WHOLE,) * 6,
        [SMEM] + [WHOLE] * 4 + [ANY] * len(w),
        [VMEM((2, d, d), BF16), DMA((16,))],
        us=4,
    )(blk, c, a0, a1, nv, *w)


def cross_mlp_back(slots, blocked, blk, y, m0, m1, cot, nv, gb, gp, w):
    rows, d = y.shape
    own = d // slots if blocked else d

    def body(blk_ref, y_ref, m0_ref, m1_ref, cot_ref, nv_ref, gb_ref, gp_ref, *refs):
        (e_ref, dh_ref, gd_out, gu_out, dy_ref, sums_ref, w_s, gd, gu, sems) = refs[len(w) :]
        cp = Copies(sems)
        got = fetch_cross(cp, refs[: len(w)], blk_ref, w_s)
        gain = nv_ref[3:4]
        n, r = norm_parts(y_ref[...] + (m0_ref[...].astype(F32) + m1_ref[...].astype(F32)))
        e_ref[...] = (n * gain + nv_ref[7:8]).astype(BF16)
        grad = cot_ref[...].astype(F32)
        sums_ref[...] = sums_of(grad, n)
        dh = norm_back(grad, n, r, gain)
        dh_ref[...] = dh
        dm = dh.astype(BF16)
        cp.wait(*got)
        du = (nn(dm, w_s[1]) * gp_ref[...].astype(F32)).astype(BF16)
        dy_ref[...] = nt(du, w_s[0]).astype(BF16)
        gd[...] = tn(dm, gb_ref[...])
        own_rows(cp, blocked, blk_ref, gd, gd_out)
        gu[...] = tn(y_ref[...].astype(BF16), du)
        own_rows(cp, blocked, blk_ref, gu, gu_out)
        cp.wait_all()

    return call(
        body,
        (
            sds((rows, d), BF16),
            sds((rows, d), F32),
            sds((own, d), F32),
            sds((own, d), F32),
            sds((rows, d), BF16),
            sds((8, d), F32),
        ),
        (WHOLE, WHOLE, ANY, ANY, WHOLE, WHOLE),
        [SMEM] + [WHOLE] * 7 + [ANY] * len(w),
        [VMEM((2, d, d), BF16), VMEM((d, d), F32), VMEM((d, d), F32), DMA((18,))],
        us=30,
    )(blk, y, m0, m1, cot, nv, gb, gp, *w)


def cross_attn_back(slots, blocked, blk, dh2, d0, d1, n1, r1, c, qkv, o, p, nv, w):
    rows, d = dh2.shape
    quarter = d // 4
    heads = quarter // HEAD
    own = d // slots if blocked else d

    def body(blk_ref, dh2_ref, d0_ref, d1_ref, n_ref, r_ref, c_ref, qkv_ref, o_ref, p_ref, nv_ref,
             *refs):
        dh_ref, dx_ref, g_out, sums_ref, da_s, dqkv_s, w_s, g, sems = refs[len(w) :]
        cp = Copies(sems)
        got = fetch_cross(cp, refs[: len(w)], blk_ref, w_s)
        grad = dh2_ref[...] + (d0_ref[...].astype(F32) + d1_ref[...].astype(F32))
        n = n_ref[...]
        sums_ref[...] = sums_of(grad, n)
        dh = norm_back(grad, n, r_ref[...], nv_ref[2:3])
        dh_ref[...] = dh
        da_s[...] = dh.astype(BF16)
        cp.wait(*got)
        for t, at in enumerate(row_tiles(rows, SEG)):
            do = nn(da_s[at], w_s[0, :, 3 * quarter :]).astype(BF16)
            qkv_t = qkv_ref[at]
            cut = [
                [qkv_t[:, i * quarter + h * HEAD : i * quarter + (h + 1) * HEAD] for i in range(3)]
                for h in range(heads)
            ]
            dos = [do[:, h * HEAD : (h + 1) * HEAD] for h in range(heads)]
            dss = []
            for h in range(heads):
                pf = p_ref[t, h].astype(F32)
                pd = pf * nt(dos[h], cut[h][2])
                dss.append((pd - pf * jnp.sum(pd, axis=-1, keepdims=True)).astype(BF16))
            dq, dk, dv = [], [], []
            for h in range(heads):
                dv.append(tn(p_ref[t, h], dos[h]).astype(BF16))
                dq.append((nn(dss[h], cut[h][1]) * SCALE).astype(BF16))
                dk.append((tn(dss[h], cut[h][0]) * SCALE).astype(BF16))
            dqkv_s[at] = jnp.concatenate(dq + dk + dv, axis=1)
        dx_ref[...] = nt(dqkv_s[...], w_s[0, :, : 3 * quarter]).astype(BF16)
        g[:, : 3 * quarter] = tn(c_ref[...].astype(BF16), dqkv_s[...])
        g[:, 3 * quarter :] = tn(da_s[...], o_ref[...])
        own_rows(cp, blocked, blk_ref, g, g_out)
        cp.wait_all()

    return call(
        body,
        (sds((rows, d), F32), sds((rows, d), BF16), sds((own, d), F32), sds((8, d), F32)),
        (WHOLE, WHOLE, ANY, WHOLE),
        [SMEM] + [WHOLE] * 10 + [ANY] * len(w),
        [
            VMEM((rows, d), BF16),
            VMEM((rows, 3 * quarter), BF16),
            VMEM((1, d, d), BF16),
            VMEM((d, d), F32),
            DMA((9,)),
        ],
        us=5,
    )(blk, dh2, d0, d1, n1, r1, c, qkv, o, p, nv, *w)


def swap(axis, size, bit, value):
    return lax.ppermute(value, axis, [(i, i ^ bit) for i in range(size)])


core_swap = functools.partial(swap, "tensor", 4, 1)
y_swap = functools.partial(swap, "tensor", 4, 2)
x_swap = functools.partial(swap, "dp", 8, 1)


def z_swap(k, value):
    return swap("dp", 8, 2 * k, value)


def tied(*trees):
    return lax.optimization_barrier(trees)


PLANES = ((0, 0), (0, 1), (1, 0))
ATTN_PIECES = (
    [(n, (), 0, y, x, 0) for n, (y, x) in enumerate(PLANES)]
    + [(3 + n, (k - 1,), 0, y, x, k) for n, (y, x) in enumerate(PLANES) for k in (1, 2, 3)]
    + [(6, (k,), 0, 1, 1, k) for k in (0, 1)]
    + [(7, (k - 2,), 0, 1, 1, k) for k in (2, 3)]
)
MLP_PIECES = (
    [(n, (), 1, y, x, 0) for n, (y, x) in enumerate(PLANES)]
    + [(3 + n, (k - 1,), 0, y, x, k) for n, (y, x) in enumerate(PLANES) for k in (1, 2, 3)]
    + [(6, (k,), 0, 1, 1, k) for k in (0, 1)]
    + [(7, (k - 2,), 0, 1, 1, k) for k in (2, 3)]
)


def both_cores(pieces, count):
    return [
        (count * c + which, lead, pack, 2 * c + y, 4 * x + z)
        for c in range(2)
        for which, lead, pack, y, x, z in pieces
    ]


PLAIN_PLAN = [(0, (j,), 0, j, None) for j in range(4)]


def xor_order(stacked, index, bits):
    shape = stacked.shape
    out = stacked.reshape((2,) * bits + shape[1:])
    for b in range(bits):
        out = jnp.where((index >> (bits - 1 - b)) & 1 == 1, jnp.flip(out, b), out)
    return out.reshape(shape)


def add(*parts):
    total = parts[0].astype(F32)
    for p in parts[1:]:
        total = total + p.astype(F32)
    return total


def low_add(*parts):
    return add(*parts).astype(BF16)


class Scatter:
    def __init__(self, g0, g1_swapped):
        self.g = (g0, g1_swapped)

    def own(self, y, x, zs):
        return tuple(g[y, x, zs] for g in self.g)

    def diagonal(self):
        return low_add(*self.own(1, 1, slice(0, 2))), low_add(*self.own(1, 1, slice(2, 4)))

    def columns(self, from_x, from_y):
        lo, hi = slice(0, 2), slice(2, 4)
        to_x = jnp.concatenate([low_add(*self.own(0, 1, lo)), low_add(*self.own(0, 1, hi), from_y)])
        to_y = jnp.concatenate([low_add(*self.own(1, 0, lo), from_x), low_add(*self.own(1, 0, hi))])
        return to_x, to_y

    def planes(self, from_x, from_y):
        self.mine = (*self.own(0, 0, 0), from_x[0], from_y[0])
        return [low_add(*self.own(0, 0, k), from_x[k], from_y[k]) for k in (1, 2, 3)]

    def last(self, back):
        return add(*self.mine, *back)


def body(tokens, w_qkv, w_out, w_up, w_down, norm_gain, norm_bias, seg_table, seg_ids, cotangent):
    nd, ntens = lax.axis_size("dp"), lax.axis_size("tensor")
    fast = nd == 8
    di, ti = lax.axis_index("dp"), lax.axis_index("tensor")
    seqs, toks, d = tokens.shape
    rows, dblk = seqs * toks, tokens.shape[2] // nd
    per_dev = toks // SEG
    x = tokens.reshape(rows, d)
    cot = cotangent.reshape(rows, d)

    def pack(b):
        return (
            jnp.concatenate([w_qkv[b].reshape(dblk, -1), w_out[b].T], axis=1),
            jnp.stack([w_up[b], w_down[b].T]),
        )

    attn0, mlp0 = pack(0)
    attn1, mlp1 = pack(1)
    small = jnp.concatenate(
        [norm_gain.reshape(4, dblk), norm_bias.reshape(4, dblk), seg_table], axis=0
    )
    onehot = (seg_ids.reshape(-1, 1) == jnp.arange(128, dtype=jnp.int32)).astype(BF16)

    p3 = jnp.concatenate([attn1[None], mlp1])

    def place(leaders):
        leaders = leaders.reshape(seqs, per_dev, -1)
        space = jnp.zeros((seqs, per_dev * ntens, leaders.shape[-1]), BF16)
        return lax.dynamic_update_slice(space, leaders, (0, per_dev * ti, 0)).reshape(
            -1, leaders.shape[-1]
        )

    early = jnp.pad(onehot, ((0, 0), (0, d - onehot.shape[1])))
    early = place(cot.reshape(-1, SEG, d)[:, 0])
    if fast:
        zi, xi = di // 2, di % 2
        blk = jnp.stack([(zi ^ k) * 2 + (xi ^ l) for l in range(2) for k in range(4)]).astype(jnp.int32)

        def z_all(p):
            return [z_swap(k, p) for k in (1, 2, 3)]

        tiny = jnp.pad(small, ((0, 0), (0, d - dblk)))
        p_all = jnp.concatenate([attn0, mlp0.reshape(-1, d), tiny])
        z1, x0, y0 = z_all(p_all[:dblk]), x_swap(p_all), y_swap(p_all)
        early = early + core_swap(early)
        z1, x0, y0, pm, early = tied(z1, x0, y0, p_all[dblk:], early)
        c1 = jnp.stack(z1)
        xc1, yc1 = x_swap(c1), y_swap(c1)
        zm = z_all(pm)
        xc1, yc1, early = tied(xc1, yc1, early)
        ex1, ey1 = x_swap(jnp.stack([y0[:dblk], yc1[0]])), y_swap(xc1[1:])
        early = early + y_swap(early)
        ex1, ey1, early = tied(ex1, ey1, early)
        p3a, p3u, p3d = p3[0], p3[1], jnp.concatenate([p3[2], early])
        z3a = z_all(tied(p3a, ex1)[0])
        base = [p_all, x0, y0]
        base_core = [core_swap(v) for v in base]
        mine1 = [c1, xc1, yc1, ex1, ey1]
        attn_pieces = base + mine1 + base_core + [core_swap(v) for v in mine1]
        attn_plan = both_cores(ATTN_PIECES, 8)
        cm = jnp.stack(zm)
        xcm, ycm = x_swap(cm), y_swap(cm)
    else:
        blk = jnp.zeros((8,), jnp.int32)

        def whole(p):
            g = lax.all_gather(p, ("tensor", "dp"), axis=0)
            g = g.reshape(ntens, nd, p.shape[0], dblk, d).transpose(0, 2, 1, 3, 4)
            g = g.reshape(ntens, p.shape[0] * d, d)
            return xor_order(g, ti, 2)

        attn_pieces, mlp_pieces = [whole(attn0[None])], [whole(mlp0)]
        attn_plan = mlp_plan = PLAIN_PLAN
        w1 = lax.all_gather(p3, "dp", axis=1, tiled=True)
        w1a, w1m = [w1[:1]], [w1[1:]]
        nv = lax.all_gather(small, "dp", axis=1, tiled=True).astype(F32)
    w_a, qkv, o, p, n1, r1, n_first = attn_forward(attn_plan, blk, x, attn_pieces)

    if fast:
        n_first, z3a = tied(n_first, z3a)
    pay = place(jnp.concatenate([n_first[:, 0], onehot], axis=1))
    if fast:
        pay = pay + core_swap(pay)
        pay = pay + y_swap(pay)
        xcm, ycm, pay = tied(xcm, ycm, pay)
        to_x, to_y, p3u = tied(jnp.stack([y0[dblk:], ycm[0]]), xcm[1:], p3u)
        ex2, ey2 = x_swap(to_x), y_swap(to_y)
        z3u = z_all(p3u)
        pay = jnp.stack([pay, x_swap(pay)])
        at = 3 * dblk
        tiny = jnp.stack(
            [jnp.stack([p_all[at:], x0[at:]])]
            + [jnp.stack([a[2 * dblk :], b[2 * dblk :]]) for a, b in zip(zm, xcm)]
        )[..., :dblk]
        nv = xor_order(tiny.reshape(nd, 16, dblk), di, 3)
        nv = nv.transpose(1, 0, 2).reshape(16, d).astype(F32)
        w1a = jnp.stack([p3a] + z3a)
        ex2, ey2, pay, z3u, p3d, w1a, nv = tied(ex2, ey2, pay, z3u, p3d, w1a, nv)
        mine2 = [cm, xcm, ycm, ex2, ey2]
        mlp_pieces = base + mine2 + base_core + [core_swap(v) for v in mine2]
        mlp_plan = both_cores(MLP_PIECES, 8)
        pay = jnp.stack([pay] + z_all(pay))
        first = 0
        z3d = z_all(p3d)
        w1a = [w1a, x_swap(w1a)]
    else:
        pay = lax.all_gather(lax.psum(pay, "tensor"), "dp", axis=0)
        lead_cot = lax.all_gather(lax.psum(early, "tensor"), "dp", axis=0).reshape(-1, d)
        first = di * seqs * per_dev * ntens
    pay = pay.reshape(-1, d + onehot.shape[1])
    lead_n, lead_hot = pay[:, :d], pay[:, d:]

    wu, wd, ybl, gbl, gpl, zl, nl, rl = lead_forward(mlp_plan, blk, lead_n, nv, mlp_pieces)
    if fast:
        z3d, zl, w1a = tied(z3d, zl, w1a)
        w1m = jnp.stack([jnp.concatenate(v) for v in zip([p3u] + z3u, [p3d] + z3d)])
        w1m = [w1m, x_swap(w1m)]
        lead_cot = jnp.stack(w1m, axis=1)[:, :, 2 * dblk :].reshape(-1, d)

    def near_sum(part):
        if fast:
            return low_add(part, core_swap(part))
        return lax.psum(part.astype(F32), "tensor")

    def far_sum(half):
        return y_swap(half) if fast else jnp.zeros_like(half)

    c, cqkv, co, cp, ca = cross_attn(blk, zl, lead_hot, nv, w1a)
    s1 = near_sum(ca)
    t1 = far_sum(s1)
    n2, s1 = tied(n1, s1)
    gb, gp, yb, dm, g1, dy, result, sums2 = mlp_forward(nd, fast, blk, n2, cot, nv, wu, wd)
    t1, sums2, w1m = tied(t1, sums2, w1m)
    cy, cn, cr, cgb, cgp, cm = cross_mlp(blk, c, s1, t1, nv, w1m)
    s2 = near_sum(cm)
    t2 = far_sum(s2)
    dm, s2 = tied(dm, s2)
    g0, dy = mlp_backward(nd, fast, blk, dm, yb, gb, gp, wu, wd, dy)
    t2, dy = tied(t2, dy)
    e, cdh2, cgd, cgu, cdy, csum2 = cross_mlp_back(
        nd, fast, blk, cy, s2, t2, lead_cot, nv, cgb, cgp, w1m
    )
    if fast:

        def shards(g):
            return g.reshape(2, 2, 4, *g.shape[2:])

        other_m, cdy = tied(core_swap(shards(g1)), cdy)
    s3 = near_sum(cdy)
    t3 = far_sum(s3)
    if fast:
        sm_ = Scatter(shards(g0), other_m)
        ops = sm_.diagonal()
        t3, ops = tied(t3, ops)
        diag = x_swap(ops[0]), y_swap(ops[1])
    t3, dy = tied(t3, dy)
    cdh, cdx, cga, csum1 = cross_attn_back(
        nd, fast, blk, cdh2, s3, t3, cn, cr, c, cqkv, co, cp, nv, w1a
    )
    s4 = near_sum(cdx)
    t4 = far_sum(s4)
    if fast:
        diag, s4 = tied(diag, s4)
        ops = sm_.columns(*diag)
        t4, ops = tied(t4, ops)
        cols = x_swap(ops[0]), y_swap(ops[1])
    def own_leaders(full):
        part = lax.dynamic_slice_in_dim(full, first, seqs * per_dev * ntens, 0)
        part = part.reshape(seqs, per_dev * ntens, d)
        return lax.dynamic_slice_in_dim(part, per_dev * ti, per_dev, 1).reshape(-1, d)

    lead = (cdh, s4, t4, lead_hot, nl, rl, ybl, gbl, gpl, wu, wd)
    if fast:
        spot = jnp.stack([s * per_dev * ntens + per_dev * ti + i for s in range(seqs) for i in range(per_dev)])
        first_in = (dy, spot.astype(jnp.int32), n1, r1, nv, sums2)
        a1, dx, da, sums, lgd, lgu, lsum = attn_backward(
            1, nd, fast, blk, x, qkv, o, p, w_a, first_in, None, lead
        )
    else:
        dyl, lgd, lgu, lsum = lead_backward(nd, fast, blk, nv, lead)
        first_in = (dy, own_leaders(dyl), n1, r1, nv, sums2)
        a1, dx, da, sums = attn_backward(1, nd, fast, blk, x, qkv, o, p, w_a, first_in, None)
    if fast:
        cols, dx = tied(cols, dx)
        ops = sm_.planes(*cols)
        dx, ops = tied(dx, ops)
        planes = [z_swap(kk, op) for kk, op in zip((1, 2, 3), ops)]
        other = core_swap(shards(a1))
    a0, dx = attn_backward(0, nd, fast, blk, x, qkv, o, p, w_a, None, (da, dx, sums))

    if fast:
        sa = Scatter(shards(a0), other)
        ops = sa.diagonal()
        ops, e, csum1, csum2, cga, cgu, cgd, lsum, lgd, lgu = tied(
            ops, e, csum1, csum2, cga, cgu, cgd, lsum, lgd, lgu
        )
        diag = x_swap(ops[0]), y_swap(ops[1])
        planes, diag = tied(planes, diag)
        ops = sa.columns(*diag)
        cols = x_swap(ops[0]), y_swap(ops[1])
        ops = sa.planes(*cols)
        gm = sm_.last(planes)
        ga = sa.last([z_swap(kk, op) for kk, op in zip((1, 2, 3), ops)])[0]
        norm_sums = ga[dblk : dblk + 8, :dblk]
        ga = ga[:dblk]
    else:

        def owned(lo, hi):
            g = jnp.concatenate([lo, hi])
            g = xor_order(g, ti, 2).astype(F32)
            g = lax.psum_scatter(g, "tensor", scatter_dimension=0)
            return lax.psum_scatter(g, "dp", scatter_dimension=1, tiled=True)

        gm, ga = owned(g0, g1), owned(a0, a1)[0]
        norm_sums = lax.psum_scatter(
            lax.psum(sums, "tensor"), "dp", scatter_dimension=1, tiled=True
        )

    def rows_of(full):
        if fast:
            return full
        return lax.dynamic_slice_in_dim(full, di * dblk, dblk, 0)

    def cols_of(full):
        return lax.dynamic_slice_in_dim(full, di * dblk, dblk, 1)

    gu0, gd0 = gm[0] + rows_of(lgu), gm[1] + rows_of(lgd)
    ga1, gu1, gd1 = rows_of(cga), rows_of(cgu), rows_of(cgd)
    wide = w_qkv.shape[3] * 3
    grad_qkv = jnp.stack([ga[:, :wide], ga1[:, :wide]]).reshape(w_qkv.shape)
    grad_out = jnp.stack([ga[:, wide:].T, ga1[:, wide:].T])
    grad_up = jnp.stack([gu0, gu1])
    grad_down = jnp.stack([gd0.T, gd1.T])
    lsum, csum1, csum2 = cols_of(lsum), cols_of(csum1), cols_of(csum2)
    grad_gain = jnp.stack(
        [
            jnp.stack([norm_sums[0], norm_sums[2] + lsum[0]]),
            jnp.stack([csum1[0], csum2[0]]),
        ]
    )
    grad_bias = jnp.stack(
        [
            jnp.stack([norm_sums[1], norm_sums[3] + lsum[1]]),
            jnp.stack([csum1[1], csum2[1]]),
        ]
    )
    result = result.reshape(-1, SEG, d).at[:, 0].set(own_leaders(e)).reshape(tokens.shape)
    return (
        result,
        dx.reshape(tokens.shape),
        grad_qkv,
        grad_out,
        grad_up,
        grad_down,
        grad_gain,
        grad_bias,
        lsum[8:16],
    )


def solution(mesh):
    return jax.shard_map(
        body,
        mesh=mesh,
        in_specs=(
            P("dp", "tensor", None),
            P(None, "dp", None, "tensor"),
            P(None, "tensor", "dp"),
            P(None, "dp", "tensor"),
            P(None, "tensor", "dp"),
            P(None, None, "dp"),
            P(None, None, "dp"),
            P(None, "dp"),
            P("dp", "tensor"),
            P("dp", "tensor", None),
        ),
        out_specs=(
            P("dp", "tensor", None),
            P("dp", "tensor", None),
            P(None, "dp", None, "tensor"),
            P(None, "tensor", "dp"),
            P(None, "dp", "tensor"),
            P(None, "tensor", "dp"),
            P(None, None, "dp"),
            P(None, None, "dp"),
            P(None, "dp"),
        ),
        check_vma=False,
    )
```

```python
import functools
import math

import jax
import jax.numpy as jnp
from jax import lax
from jax.experimental import pallas as pl
from jax.experimental.pallas import tpu as pltpu
from jax.sharding import PartitionSpec as P

HEAD = 64
SEG = 128
GROUP = 8
F32, BF16 = jnp.float32, jnp.bfloat16
VMEM = pltpu.VMEM
ANY = pl.BlockSpec(memory_space=pl.ANY)
WHOLE = pl.BlockSpec(memory_space=pltpu.VMEM)
SMEM = pl.BlockSpec(memory_space=pltpu.SMEM)
PARAMS = pltpu.CompilerParams(vmem_limit_bytes=60 << 20)
EPS = 1e-05
SCALE = HEAD ** (-0.5)
RSQRT2 = 1.0 / math.sqrt(2.0)
RSQRT2PI = 1.0 / math.sqrt(2.0 * math.pi)


def nn(a, b):
    return lax.dot_general(a, b, (((1,), (0,)), ((), ())), preferred_element_type=F32)


def nt(a, b):
    return lax.dot_general(a, b, (((1,), (1,)), ((), ())), preferred_element_type=F32)


def tn(a, b):
    return lax.dot_general(a, b, (((0,), (0,)), ((), ())), preferred_element_type=F32)


def norm_parts(h):
    center = h - jnp.mean(h, axis=-1, keepdims=True)
    rstd = lax.rsqrt(jnp.mean(center * center, axis=-1, keepdims=True) + EPS)
    return center * rstd, rstd


def norm_back(grad, normed, rstd, gain):
    dn = grad * gain
    return rstd * (
        dn
        - jnp.mean(dn, axis=-1, keepdims=True)
        - normed * jnp.mean(dn * normed, axis=-1, keepdims=True)
    )


def gelu_both(u):
    cdf = 0.5 + 0.5 * lax.erf(u * RSQRT2)
    return u * cdf, cdf + u * (jnp.exp(-0.5 * u * u) * RSQRT2PI)


def halves(pair):
    lane = lax.broadcasted_iota(jnp.int32, pair.shape, 1)
    zero = jnp.zeros_like(pair)
    return jnp.concatenate(
        [jnp.where(lane < HEAD, pair, zero), jnp.where(lane < HEAD, zero, pair)], axis=0
    )


def unhalve(stacked):
    lane = lax.broadcasted_iota(jnp.int32, (SEG, 2 * HEAD), 1)
    return jnp.where(lane < HEAD, stacked[:SEG], stacked[SEG:])


def half_softmax(s):
    top = jnp.concatenate(
        [
            jnp.broadcast_to(jnp.max(s[:, :SEG], axis=-1, keepdims=True), (SEG, SEG)),
            jnp.broadcast_to(jnp.max(s[:, SEG:], axis=-1, keepdims=True), (SEG, SEG)),
        ],
        axis=1,
    )
    ex = jnp.exp(s - top)
    inv = jnp.concatenate(
        [
            jnp.broadcast_to(1.0 / jnp.sum(ex[:, :SEG], axis=-1, keepdims=True), (SEG, SEG)),
            jnp.broadcast_to(1.0 / jnp.sum(ex[:, SEG:], axis=-1, keepdims=True), (SEG, SEG)),
        ],
        axis=1,
    )
    return ex * inv


def call(body, outs, out_specs, in_specs, scratch=(), us=10):
    return pl.pallas_call(
        body,
        out_shape=outs,
        in_specs=in_specs,
        out_specs=out_specs,
        scratch_shapes=list(scratch),
        compiler_params=PARAMS,
        cost_estimate=pl.CostEstimate(flops=int(us * 2e9), bytes_accessed=1, transcendentals=0),
    )


def sds(shape, dtype):
    return jax.ShapeDtypeStruct(shape, dtype)


DMA = pltpu.SemaphoreType.DMA


class Copies:
    def __init__(self, sems):
        self.sems, self.used, self.open = sems, 0, []

    def start(self, src, dst):
        copy = pltpu.make_async_copy(src, dst, self.sems.at[self.used])
        self.used += 1
        copy.start()
        self.open.append(copy)
        return copy

    def wait(self, *copies):
        for c in copies:
            if any(c is other for other in self.open):
                self.open = [other for other in self.open if other is not c]
                c.wait()

    def wait_all(self):
        for c in self.open:
            c.wait()
        self.open = []


def fetch(cp, plan, pieces, pack, blk_ref, dst, d):
    out = []
    for which, lead, start, j, slot in plan:
        rows = d if slot is None else d // 8
        src = pieces[which].at[(*lead, pl.ds((start + pack) * rows, rows))]
        at = pl.ds(0 if slot is None else pl.multiple_of(blk_ref[slot] * rows, 16), rows)
        out.append(cp.start(src, dst.at[at, pl.ds(j * d, d)]))
    return out


def row_tiles(rows, tile):
    return [slice(i, min(i + tile, rows)) for i in range(0, rows, tile)]


def attn_forward(plan, blk, x, pieces):
    rows, d = x.shape
    segs, quarter = rows // SEG, d // 4
    pairs = d // SEG
    np_ = len(pieces)

    def body(blk_ref, x_hbm, *refs):
        ins, refs = refs[:np_], refs[np_:]
        w_out, qkv_out, o_out, p_out, n_out, r_ref, nl_ref = refs[:7]
        raw, w, x_s, qkv, o_s, p_s, n_s, sems = refs[7:]
        cp = Copies(sems)
        got = fetch(cp, plan, ins, 0, blk_ref, raw, d)
        got_x = cp.start(x_hbm, x_s)
        cp.wait(*got)
        for t in range(4):
            for half in range(2):
                j = 2 * half
                at = slice(t * d + j * quarter, t * d + (j + 2) * quarter)
                w[:, at] = jnp.concatenate(
                    [
                        raw[:, j * d + t * quarter : j * d + (t + 1) * quarter],
                        raw[:, (j + 1) * d + t * quarter : (j + 1) * d + (t + 1) * quarter],
                    ],
                    axis=1,
                )
        cp.start(w, w_out)
        cp.wait(got_x)
        qkv[...] = nn(x_s[...], w[:, : 3 * d]).astype(BF16)
        cp.start(qkv, qkv_out)
        for t in range(segs):
            at = slice(t * SEG, (t + 1) * SEG)
            probs = []
            for pair in range(pairs):
                lo = pair * SEG
                s = nt(qkv[at, lo : lo + SEG], halves(qkv[at, d + lo : d + lo + SEG])) * SCALE
                probs.append(half_softmax(s).astype(BF16))
            for pair in range(pairs):
                lo = pair * SEG
                p_s[t, pair] = probs[pair]
                o_s[at, lo : lo + SEG] = nn(
                    probs[pair], halves(qkv[at, 2 * d + lo : 2 * d + lo + SEG])
                ).astype(BF16)
            cp.start(p_s.at[t], p_out.at[t])
        cp.start(o_s, o_out)
        n_s[...] = nt(o_s[...], w[:, 3 * d :])
        for t in range(segs):
            at = slice(t * SEG, (t + 1) * SEG)
            n, r = norm_parts(x_s[at].astype(F32) + n_s[at])
            n_s[at] = n
            r_ref[at] = r
            nl_ref[t] = n[0:8].astype(BF16)
            cp.start(n_s.at[at], n_out.at[at])
        cp.wait_all()

    return call(
        body,
        (
            sds((d, 4 * d), BF16),
            sds((rows, 3 * d), BF16),
            sds((rows, d), BF16),
            sds((segs, pairs, SEG, 2 * SEG), BF16),
            sds((rows, d), F32),
            sds((rows, 1), F32),
            sds((segs, 8, d), BF16),
        ),
        (ANY,) * 5 + (WHOLE,) * 2,
        [SMEM, ANY] + [ANY] * np_,
        [
            VMEM((d, 4 * d), BF16),
            VMEM((d, 4 * d), BF16),
            VMEM((rows, d), BF16),
            VMEM((rows, 3 * d), BF16),
            VMEM((rows, d), BF16),
            VMEM((segs, pairs, SEG, 2 * SEG), BF16),
            VMEM((rows, d), F32),
            DMA((len(plan) + 4 + 2 * segs,)),
        ],
        us=30,
    )(blk, x, *pieces)


def lead_forward(plan, blk, lead_n, nv, pieces):
    leads, d = lead_n.shape
    np_ = len(pieces)

    def body(blk_ref, ln_ref, nv_ref, *refs):
        ins, refs = refs[:np_], refs[np_:]
        wu_out, wd_out, yb_ref, gb_ref, gp_ref, zl_ref, nl_ref, rl_ref, wu, wd, sems = refs

        def lead_y(at):
            return ln_ref[at].astype(F32) * nv_ref[0:1] + nv_ref[4:5]

        cp = Copies(sems)
        got_u = fetch(cp, plan, ins, 0, blk_ref, wu, d)
        got_d = fetch(cp, plan, ins, 1, blk_ref, wd, d)
        cp.wait(*got_u)
        cp.start(wu, wu_out)
        for at in row_tiles(leads, SEG):
            yb_ref[at] = lead_y(at).astype(BF16)
            g, gd = gelu_both(nn(yb_ref[at], wu[...]))
            gb_ref[at] = g.astype(BF16)
            gp_ref[at] = gd.astype(BF16)
        cp.wait(*got_d)
        cp.start(wd, wd_out)
        for at in row_tiles(leads, SEG):
            n, r = norm_parts(lead_y(at) + nt(gb_ref[at], wd[...]))
            zl_ref[at] = n * nv_ref[1:2] + nv_ref[5:6]
            nl_ref[at] = n
            rl_ref[at] = r
        cp.wait_all()

    return call(
        body,
        (
            sds((d, 4 * d), BF16),
            sds((d, 4 * d), BF16),
            sds((leads, d), BF16),
            sds((leads, 4 * d), BF16),
            sds((leads, 4 * d), BF16),
            sds((leads, d), F32),
            sds((leads, d), F32),
            sds((leads, 1), F32),
        ),
        (ANY, ANY) + (WHOLE,) * 6,
        [SMEM, WHOLE, WHOLE] + [ANY] * np_,
        [VMEM((d, 4 * d), BF16), VMEM((d, 4 * d), BF16), DMA((2 * len(plan) + 2,))],
        us=20,
    )(blk, lead_n, nv, *pieces)


def put_blocks(cp, blocked, blk_ref, src, out, y, pack, slots):
    if not blocked:
        cp.start(src, out.at[y, pack])
        return
    rows = src.shape[0] // slots
    for s in range(slots):
        at = pl.ds(pl.multiple_of(blk_ref[s] * rows, 16), rows)
        cp.start(src.at[at], out.at[y, s, pack, pl.ds(0, rows)])


def mlp_forward(slots, blocked, blk, n1, cot, nv, wu_, wd_):
    rows, d = n1.shape
    half, dblk = 2 * d, d // slots
    per = slots if blocked else 1

    def body(blk_ref, y_hbm, cot_hbm, nv_ref, wu_hbm, wd_hbm, *refs):
        gb_out, gp_out, yb_out, dm_out, g_out, dy_out, res_out, sums_ref = refs[:8]
        y_s, cot_s, wu, wd, yb, gb, gp, dm, dh_s, res, du, gd, gu, sems = refs[8:]
        cp = Copies(sems)
        got_y = cp.start(y_hbm, y_s)
        up, down = [], []
        for j in range(4):
            cols = pl.ds(j * d, d)
            up.append(cp.start(wu_hbm.at[:, cols], wu.at[:, cols]))
        down.append(cp.start(wd_hbm, wd))
        got_cot = cp.start(cot_hbm, cot_s)
        cp.wait(got_y)
        y_s[...] = y_s[...] * nv_ref[0:1] + nv_ref[4:5]
        yb[...] = y_s[...].astype(BF16)
        cp.start(yb, yb_out)
        for j in range(4):
            cols = slice(j * d, (j + 1) * d)
            cp.wait(up[j])
            act, slope = gelu_both(nn(yb[...], wu[:, cols]))
            gb[:, cols] = act.astype(BF16)
            gp[:, cols] = slope.astype(BF16)
            if j < 2:
                cp.start(gb.at[:, pl.ds(j * d, d)], gb_out.at[:, pl.ds(j * d, d)])
                cp.start(gp.at[:, pl.ds(j * d, d)], gp_out.at[:, pl.ds(j * d, d)])
        cp.wait(*down)
        cp.wait(got_cot)
        gain, bias = nv_ref[1:2], nv_ref[5:6]
        top, bottom = jnp.zeros((1, d), F32), jnp.zeros((1, d), F32)
        dh_s[...] = nt(gb[...], wd[...])
        for at in row_tiles(rows, SEG):
            n, r = norm_parts(y_s[at] + dh_s[at])
            res[at] = (n * gain + bias).astype(BF16)
            row = lax.broadcasted_iota(jnp.int32, (SEG, d), 0)
            grad = jnp.where(row == 0, 0.0, cot_s[at].astype(F32))
            top += jnp.sum(grad * n, axis=0, keepdims=True)
            bottom += jnp.sum(grad, axis=0, keepdims=True)
            dh = norm_back(grad, n, r, gain)
            dh_s[at] = dh
            dm[at] = dh.astype(BF16)
            for s, out in ((res, res_out), (dm, dm_out)):
                cp.start(s.at[at], out.at[at])
        sums_ref[...] = jnp.concatenate([top, bottom, jnp.zeros((6, d), F32)], axis=0)
        for y in range(2):
            mine = slice(y * d, (y + 1) * d)
            wide = slice(half + y * d, half + (y + 1) * d)
            gd[:, mine] = tn(dm[...], gb[:, wide]).astype(BF16)
            put_blocks(cp, blocked, blk_ref, gd.at[:, pl.ds(y * d, d)], g_out, y, 1, slots)
            du[:, mine] = (nn(dm[...], wd[:, wide]) * gp[:, wide].astype(F32)).astype(BF16)
        for y in range(2):
            mine = slice(y * d, (y + 1) * d)
            gu[:, mine] = tn(yb[...], du[:, mine]).astype(BF16)
            put_blocks(cp, blocked, blk_ref, gu.at[:, pl.ds(y * d, d)], g_out, y, 0, slots)
        y_s[...] = dh_s[...] + nt(du[...], wu[:, half:])
        cp.start(y_s, dy_out)
        cp.wait_all()

    g_shape = (2, slots, 2, dblk, d) if blocked else (2, 2, d, d)

    return call(
        body,
        (
            sds((rows, half), BF16),
            sds((rows, half), BF16),
            sds((rows, d), BF16),
            sds((rows, d), BF16),
            sds(g_shape, BF16),
            sds((rows, d), F32),
            sds((rows, d), BF16),
            sds((8, d), F32),
        ),
        (ANY,) * 7 + (WHOLE,),
        [SMEM, ANY, ANY, WHOLE, ANY, ANY],
        [
            VMEM((rows, d), F32),
            VMEM((rows, d), BF16),
            VMEM((d, 4 * d), BF16),
            VMEM((d, 4 * d), BF16),
            VMEM((rows, d), BF16),
            VMEM((rows, 4 * d), BF16),
            VMEM((rows, 4 * d), BF16),
            VMEM((rows, d), BF16),
            VMEM((rows, d), F32),
            VMEM((rows, d), BF16),
            VMEM((rows, half), BF16),
            VMEM((d, half), BF16),
            VMEM((d, half), BF16),
            DMA((14 + 2 * (rows // SEG) + 4 * per,)),
        ],
        us=0.01,
    )(blk, n1, cot, nv, wu_, wd_)


def mlp_backward(slots, blocked, blk, dm_, yb_, gb_, gp_, wu_, wd_, start_):
    rows, d = dm_.shape
    dblk = d // slots
    per = slots if blocked else 1
    half = 2 * d

    def body(blk_ref, dm_hbm, yb_hbm, gb_hbm, gp_hbm, wu_hbm, wd_hbm, st_hbm, g_out, dy_out, *scr):
        dm, yb, gb, gp, wu, wd, st, du, gd, gu, dy, sems = scr
        cp = Copies(sems)
        cols = pl.ds(0, half)
        got_dm = cp.start(dm_hbm, dm)
        got_gb = cp.start(gb_hbm, gb)
        got_wd = cp.start(wd_hbm.at[:, cols], wd)
        got_gp = cp.start(gp_hbm, gp)
        got_yb = cp.start(yb_hbm, yb)
        got_wu = cp.start(wu_hbm.at[:, cols], wu)
        got_st = cp.start(st_hbm, st)
        cp.wait(got_dm, got_gb)
        for y in range(2):
            mine = slice(y * d, (y + 1) * d)
            gd[:, mine] = tn(dm[...], gb[:, mine]).astype(BF16)
            put_blocks(cp, blocked, blk_ref, gd.at[:, pl.ds(y * d, d)], g_out, y, 1, slots)
        cp.wait(got_wd, got_gp)
        for y in range(2):
            mine = slice(y * d, (y + 1) * d)
            du[:, mine] = (nn(dm[...], wd[:, mine]) * gp[:, mine].astype(F32)).astype(BF16)
        cp.wait(got_yb)
        for y in range(2):
            mine = slice(y * d, (y + 1) * d)
            gu[:, mine] = tn(yb[...], du[:, mine]).astype(BF16)
            put_blocks(cp, blocked, blk_ref, gu.at[:, pl.ds(y * d, d)], g_out, y, 0, slots)
        cp.wait(got_wu, got_st)
        dy[...] = st[...] + nt(du[...], wu[...])
        cp.start(dy, dy_out)
        cp.wait_all()

    g_shape = (2, slots, 2, dblk, d) if blocked else (2, 2, d, d)
    return call(
        body,
        (sds(g_shape, BF16), sds((rows, d), F32)),
        (ANY, ANY),
        [SMEM] + [ANY] * 7,
        [
            VMEM((rows, d), BF16),
            VMEM((rows, d), BF16),
            VMEM((rows, half), BF16),
            VMEM((rows, half), BF16),
            VMEM((d, half), BF16),
            VMEM((d, half), BF16),
            VMEM((rows, d), F32),
            VMEM((rows, half), BF16),
            VMEM((d, half), BF16),
            VMEM((d, half), BF16),
            VMEM((rows, d), F32),
            DMA((7 + 4 * per + rows // (2 * SEG),)),
        ],
        us=8,
    )(blk, dm_, yb_, gb_, gp_, wu_, wd_, start_)


def own_rows(cp, blocked, blk_ref, src, out):
    if blocked:
        rows = out.shape[0]
        src = src.at[pl.ds(pl.multiple_of(blk_ref[0] * rows, 8), rows)]
    cp.start(src, out)


def sums_of(grad, n):
    d = grad.shape[1]
    return jnp.concatenate(
        [
            jnp.sum(grad * n, axis=0, keepdims=True),
            jnp.sum(grad, axis=0, keepdims=True),
            jnp.zeros((6, d), F32),
        ],
        axis=0,
    )


LEAD_INS = [WHOLE] * 7 + [ANY] * 4


def lead_scratch(rows, d):
    return [
        VMEM((rows, d), BF16),
        VMEM((rows, 4 * d), BF16),
        VMEM((d, 4 * d), BF16),
        VMEM((d, 4 * d), BF16),
        VMEM((d, d), F32),
        VMEM((d, d), F32),
    ]


def lead_fetch(cp, ins, scr):
    gb_hbm, gp_hbm, wu_hbm, wd_hbm = ins[7:]
    gb, gp, wu, wd, _, _ = scr
    d = gb.shape[1]
    got = [cp.start(wd_hbm, wd), cp.start(gp_hbm, gp), cp.start(wu_hbm, wu)]
    return got + [cp.start(gb_hbm.at[:, pl.ds(0, d)], gb)]


def lead_grads(cp, blocked, blk_ref, nv_ref, ins, scr, got, dy_ref, gd_out, gu_out, sums_ref):
    dh_ref, d0_ref, d1_ref, oh_ref, n_ref, r_ref, yb_ref = ins[:7]
    gb, gp, wu, wd, gd, gu = scr
    d = gb.shape[1]
    grad = dh_ref[...] + (d0_ref[...].astype(F32) + d1_ref[...].astype(F32))
    n = n_ref[...]
    tops = [sums_of(grad, n)]
    for i in range(8):
        tops.append(jnp.sum(oh_ref[:, i : i + 1].astype(F32) * grad, axis=0, keepdims=True))
    sums_ref[...] = jnp.concatenate(tops, axis=0)
    dh2 = norm_back(grad, n, r_ref[...], nv_ref[1:2])
    dm = dh2.astype(BF16)
    cp.wait(*got[:2])
    du = (nn(dm, wd[...]) * gp[...].astype(F32)).astype(BF16)
    cp.wait(got[2])
    dy_ref[...] = dh2 + nt(du, wu[...])
    cp.wait(got[3])
    gd[...] = tn(dm, gb[...])
    own_rows(cp, blocked, blk_ref, gd, gd_out)
    gu[...] = tn(yb_ref[...], du[:, :d])
    own_rows(cp, blocked, blk_ref, gu, gu_out)


def lead_backward(slots, blocked, blk, nv, lead):
    rows, d = lead[0].shape
    own = d // slots if blocked else d
    n_in = len(lead)

    def body(blk_ref, nv_ref, *refs):
        ins, refs = refs[:n_in], refs[n_in:]
        dy_ref, gd_out, gu_out, sums_ref, *scr, sems = refs
        cp = Copies(sems)
        got = lead_fetch(cp, ins, scr)
        lead_grads(cp, blocked, blk_ref, nv_ref, ins, scr, got, dy_ref, gd_out, gu_out, sums_ref)
        cp.wait_all()

    return call(
        body,
        (sds((rows, d), F32), sds((own, d), F32), sds((own, d), F32), sds((16, d), F32)),
        (WHOLE, ANY, ANY, WHOLE),
        [SMEM, WHOLE] + LEAD_INS,
        lead_scratch(rows, d) + [DMA((6,))],
        us=7,
    )(blk, nv, *lead)


def attn_backward(core, slots, blocked, blk, x_, qkv_, o_, p_, w_, first, rest, lead=None):
    rows, d = x_.shape
    segs, half, quarter = rows // SEG, d // 2, d // 4
    dblk = d // slots
    per = slots if blocked else 1
    pairs = half // SEG
    opening = first is not None
    extra = first if opening else rest
    inside = lead is not None
    leads = lead[0].shape[0] if inside else 0
    lead = tuple(lead) if inside else ()

    def body(blk_ref, x_hbm, qkv_hbm, o_hbm, p_hbm, w_hbm, *refs):
        more, refs = refs[: len(extra)], refs[len(extra) :]
        lead_ins, refs = refs[: len(lead)], refs[len(lead) :]
        n_out = (4 if opening else 2) + (3 if inside else 0)
        outs, scr = refs[:n_out], refs[n_out:]
        g_out, dx_out = outs[:2]
        x, qkv, o, p, w, st, da, do, dqkv, gr, ex, dx, sems = scr[:13]
        cp = Copies(sems)
        if opening:
            dy_hbm, ld_ref, n_hbm, r_ref, nv_ref, s2_ref = more
            da_out, sums_ref = outs[2:4]
            nb = scr[13]
            if inside:
                got_lead = lead_fetch(cp, lead_ins, scr[15:])
            got_dy = cp.start(dy_hbm, st)
            got_n = cp.start(n_hbm, nb)
        else:
            da_hbm, st_hbm, sums_ref = more
            got_da = cp.start(da_hbm, da)
        got_w = [
            cp.start(w_hbm.at[:, pl.ds(t * d + core * half, half)], w.at[:, pl.ds(t * half, half)])
            for t in (3, 0, 1, 2)
        ]
        got_qkv = [
            cp.start(
                qkv_hbm.at[:, pl.ds(t * d + core * half, half)], qkv.at[:, pl.ds(t * half, half)]
            )
            for t in (2, 0, 1)
        ]
        got_p = cp.start(p_hbm.at[:, pl.ds(core * pairs, pairs)], p)
        got_o = cp.start(o_hbm.at[:, pl.ds(core * half, half)], o)
        got_x = cp.start(x_hbm, x)
        if inside:
            lead_grads(
                cp, blocked, blk_ref, nv_ref, lead_ins, scr[15:], got_lead, scr[14], *outs[4:]
            )
        if opening:
            cp.wait(got_dy, got_n)
            top, bottom = jnp.zeros((1, d), F32), jnp.zeros((1, d), F32)
            for t in range(segs):
                at = slice(t * SEG, (t + 1) * SEG)
                row = lax.broadcasted_iota(jnp.int32, (SEG, d), 0)
                mine = scr[14][pl.ds(ld_ref[t], 1)] if inside else ld_ref[t : t + 1]
                grad = st[at] + jnp.where(row == 0, mine, 0.0)
                n = nb[at]
                top += jnp.sum(grad * n, axis=0, keepdims=True)
                bottom += jnp.sum(grad, axis=0, keepdims=True)
                dh = norm_back(grad, n, r_ref[at], nv_ref[0:1])
                st[at] = dh
                da[at] = dh.astype(BF16)
            cp.start(da, da_out)
            sums_ref[...] = jnp.concatenate(
                [top, bottom, s2_ref[0:2], jnp.zeros((4, d), F32)], axis=0
            )
        else:
            got_st = cp.start(st_hbm, st)
            cp.wait(got_da)
        if blocked:
            for b in range(slots):
                ex[b] = jnp.zeros((16, d), BF16)
                ex[b, 0:8, 0:dblk] = sums_ref[:, b * dblk : (b + 1) * dblk].astype(BF16)
            for y in range(2):
                for s in range(slots):
                    cp.start(ex.at[blk_ref[s]], g_out.at[y, s, 0, pl.ds(dblk, 16)])
        cp.wait(got_w[0])
        do[...] = nn(da[...], w[:, 3 * half :]).astype(BF16)
        cp.wait(got_p, *got_qkv)
        for t in range(segs):
            at = slice(t * SEG, (t + 1) * SEG)
            dss = []
            for pair in range(pairs):
                mine = slice(pair * SEG, (pair + 1) * SEG)
                pf = p[t, pair].astype(F32)
                v = qkv[at, 2 * half + pair * SEG : 2 * half + (pair + 1) * SEG]
                pd = pf * nt(do[at, mine], halves(v))
                parts = [
                    pd[:, c] - pf[:, c] * jnp.sum(pd[:, c], axis=-1, keepdims=True)
                    for c in (slice(0, SEG), slice(SEG, 2 * SEG))
                ]
                dss.append(jnp.concatenate(parts, axis=1).astype(BF16))
            for pair in range(pairs):
                mine = slice(pair * SEG, (pair + 1) * SEG)
                q, k = (qkv[at, i * half + pair * SEG : i * half + (pair + 1) * SEG] for i in (0, 1))
                ds = dss[pair]
                dv = unhalve(tn(p[t, pair], do[at, mine]))
                dk = unhalve(tn(ds, q)) * SCALE
                dq = nn(ds, halves(k)) * SCALE
                for i, g in enumerate((dq, dk, dv)):
                    dqkv[at, i * half + pair * SEG : i * half + (pair + 1) * SEG] = g.astype(BF16)
        cp.wait(got_x, got_o)
        gf = tn(x[...], dqkv[...]).astype(BF16)
        go = tn(da[...], o[...]).astype(BF16)
        for y in range(2):
            at = slice(y * quarter, (y + 1) * quarter)
            cut = [gf[:, i * half + y * quarter : i * half + (y + 1) * quarter] for i in range(3)]
            cut.append(go[:, at])
            gr[y, :, :half] = jnp.concatenate(cut[:2], axis=1)
            gr[y, :, half:] = jnp.concatenate(cut[2:], axis=1)
            put_blocks(cp, blocked, blk_ref, gr.at[y], g_out, y, 0, slots)
        if not opening:
            cp.wait(got_st)
        cp.wait(*got_w)
        dx[...] = st[...] + nt(dqkv[...], w[:, : 3 * half])
        cp.start(dx, dx_out)
        cp.wait_all()

    g_shape = (2, slots, 1, dblk + 16, d) if blocked else (2, 1, d, d)
    outs = [sds(g_shape, BF16), sds((rows, d), F32)]
    specs = [ANY, ANY]
    in_more = [ANY, ANY, WHOLE]
    if opening:
        outs += [sds((rows, d), BF16), sds((8, d), F32)]
        specs += [ANY, WHOLE]
        in_more = [ANY, SMEM if inside else WHOLE, ANY, WHOLE, WHOLE, WHOLE]
    if inside:
        own = d // slots if blocked else d
        outs += [sds((own, d), F32), sds((own, d), F32), sds((16, d), F32)]
        specs += [ANY, ANY, WHOLE]
        in_more += LEAD_INS
    scratch = [
        VMEM((rows, d), BF16),
        VMEM((rows, 3 * half), BF16),
        VMEM((rows, half), BF16),
        VMEM((segs, pairs, SEG, 2 * SEG), BF16),
        VMEM((d, 4 * half), BF16),
        VMEM((rows, d), F32),
        VMEM((rows, d), BF16),
        VMEM((rows, half), BF16),
        VMEM((rows, 3 * half), BF16),
        VMEM((2, d, d), BF16),
        VMEM((slots if blocked else 1, 16, d), BF16),
        VMEM((rows, d), F32),
        DMA((24 + 4 * per,)),
    ]
    if opening:
        scratch.append(VMEM((rows, d), F32))
    if inside:
        scratch += [VMEM((leads, d), F32)] + lead_scratch(leads, d)
    return call(
        body,
        tuple(outs),
        tuple(specs),
        [SMEM] + [ANY] * 5 + in_more,
        scratch,
        us=30,
    )(blk, x_, qkv_, o_, p_, w_, *extra, *lead)


def fetch_cross(cp, pieces, blk_ref, dst):
    if len(pieces) == 1:
        return [cp.start(pieces[0], dst)]
    packs, d, _ = dst.shape
    rows = d // 8
    out = []
    for slot in range(8):
        at = pl.ds(pl.multiple_of(blk_ref[slot] * rows, 16), rows)
        for p in range(packs):
            src = pieces[slot // 4].at[slot % 4, pl.ds(p * rows, rows)]
            out.append(cp.start(src, dst.at[p, at]))
    return out


def group_mask():
    a = lax.broadcasted_iota(jnp.int32, (SEG, SEG), 0) // GROUP
    b = lax.broadcasted_iota(jnp.int32, (SEG, SEG), 1) // GROUP
    return a == b


def cross_attn(blk, zl, onehot, nv, w):
    rows, d = zl.shape
    quarter = d // 4
    heads = quarter // HEAD
    tiles = rows // SEG

    def body(blk_ref, z_ref, oh_ref, nv_ref, *refs):
        c_ref, qkv_ref, o_ref, p_ref, a_ref, w_s, sems = refs[len(w) :]
        cp = Copies(sems)
        fetch_cross(cp, refs[: len(w)], blk_ref, w_s)
        cs = []
        for at in row_tiles(rows, SEG):
            c = z_ref[at]
            for i in range(8):
                c += oh_ref[at, i : i + 1].astype(F32) * nv_ref[8 + i : 9 + i]
            c_ref[at] = c
            cs.append(c.astype(BF16))
        cp.wait_all()
        mask = group_mask()
        for t, at in enumerate(row_tiles(rows, SEG)):
            qkv = nn(cs[t], w_s[0, :, : 3 * quarter]).astype(BF16)
            qkv_ref[at] = qkv
            cut = [
                [qkv[:, i * quarter + h * HEAD : i * quarter + (h + 1) * HEAD] for i in range(3)]
                for h in range(heads)
            ]
            probs = []
            for q, k, v in cut:
                s = jnp.where(mask, nt(q, k) * SCALE, -1e30)
                ex = jnp.exp(s - jnp.max(s, axis=-1, keepdims=True))
                probs.append((ex * (1.0 / jnp.sum(ex, axis=-1, keepdims=True))).astype(BF16))
            os = []
            for h in range(heads):
                p_ref[t, h] = probs[h]
                os.append(nn(probs[h], cut[h][2]).astype(BF16))
            o = jnp.concatenate(os, axis=1)
            o_ref[at] = o
            a_ref[at] = nt(o, w_s[0, :, 3 * quarter :]).astype(BF16)

    return call(
        body,
        (
            sds((rows, d), F32),
            sds((rows, 3 * quarter), BF16),
            sds((rows, quarter), BF16),
            sds((tiles, heads, SEG, SEG), BF16),
            sds((rows, d), BF16),
        ),
        (WHOLE,) * 5,
        [SMEM] + [WHOLE] * 3 + [ANY] * len(w),
        [VMEM((1, d, d), BF16), DMA((8,))],
        us=0.01,
    )(blk, zl, onehot, nv, *w)


def cross_mlp(blk, c, a0, a1, nv, w):
    rows, d = c.shape

    def body(blk_ref, c_ref, a0_ref, a1_ref, nv_ref, *refs):
        y_ref, n_ref, r_ref, gb_ref, gp_ref, m_ref, w_s, sems = refs[len(w) :]
        cp = Copies(sems)
        fetch_cross(cp, refs[: len(w)], blk_ref, w_s)
        n, r = norm_parts(c_ref[...] + (a0_ref[...].astype(F32) + a1_ref[...].astype(F32)))
        n_ref[...] = n
        r_ref[...] = r
        y = n * nv_ref[2:3] + nv_ref[6:7]
        y_ref[...] = y
        cp.wait_all()
        g, gd = gelu_both(nn(y.astype(BF16), w_s[0]))
        gb_ref[...] = g.astype(BF16)
        gp_ref[...] = gd.astype(BF16)
        m_ref[...] = nt(gb_ref[...], w_s[1]).astype(BF16)

    return call(
        body,
        (
            sds((rows, d), F32),
            sds((rows, d), F32),
            sds((rows, 1), F32),
            sds((rows, d), BF16),
            sds((rows, d), BF16),
            sds((rows, d), BF16),
        ),
        (WHOLE,) * 6,
        [SMEM] + [WHOLE] * 4 + [ANY] * len(w),
        [VMEM((2, d, d), BF16), DMA((16,))],
        us=4,
    )(blk, c, a0, a1, nv, *w)


def cross_mlp_back(slots, blocked, blk, y, m0, m1, cot, nv, gb, gp, w):
    rows, d = y.shape
    own = d // slots if blocked else d

    def body(blk_ref, y_ref, m0_ref, m1_ref, cot_ref, nv_ref, gb_ref, gp_ref, *refs):
        (e_ref, dh_ref, gd_out, gu_out, dy_ref, sums_ref, w_s, gd, gu, sems) = refs[len(w) :]
        cp = Copies(sems)
        got = fetch_cross(cp, refs[: len(w)], blk_ref, w_s)
        gain = nv_ref[3:4]
        n, r = norm_parts(y_ref[...] + (m0_ref[...].astype(F32) + m1_ref[...].astype(F32)))
        e_ref[...] = (n * gain + nv_ref[7:8]).astype(BF16)
        grad = cot_ref[...].astype(F32)
        sums_ref[...] = sums_of(grad, n)
        dh = norm_back(grad, n, r, gain)
        dh_ref[...] = dh
        dm = dh.astype(BF16)
        cp.wait(*got)
        du = (nn(dm, w_s[1]) * gp_ref[...].astype(F32)).astype(BF16)
        dy_ref[...] = nt(du, w_s[0]).astype(BF16)
        gd[...] = tn(dm, gb_ref[...])
        own_rows(cp, blocked, blk_ref, gd, gd_out)
        gu[...] = tn(y_ref[...].astype(BF16), du)
        own_rows(cp, blocked, blk_ref, gu, gu_out)
        cp.wait_all()

    return call(
        body,
        (
            sds((rows, d), BF16),
            sds((rows, d), F32),
            sds((own, d), F32),
            sds((own, d), F32),
            sds((rows, d), BF16),
            sds((8, d), F32),
        ),
        (WHOLE, WHOLE, ANY, ANY, WHOLE, WHOLE),
        [SMEM] + [WHOLE] * 7 + [ANY] * len(w),
        [VMEM((2, d, d), BF16), VMEM((d, d), F32), VMEM((d, d), F32), DMA((18,))],
        us=30,
    )(blk, y, m0, m1, cot, nv, gb, gp, *w)


def cross_attn_back(slots, blocked, blk, dh2, d0, d1, n1, r1, c, qkv, o, p, nv, w):
    rows, d = dh2.shape
    quarter = d // 4
    heads = quarter // HEAD
    own = d // slots if blocked else d

    def body(blk_ref, dh2_ref, d0_ref, d1_ref, n_ref, r_ref, c_ref, qkv_ref, o_ref, p_ref, nv_ref,
             *refs):
        dh_ref, dx_ref, g_out, sums_ref, da_s, dqkv_s, w_s, g, sems = refs[len(w) :]
        cp = Copies(sems)
        got = fetch_cross(cp, refs[: len(w)], blk_ref, w_s)
        grad = dh2_ref[...] + (d0_ref[...].astype(F32) + d1_ref[...].astype(F32))
        n = n_ref[...]
        sums_ref[...] = sums_of(grad, n)
        dh = norm_back(grad, n, r_ref[...], nv_ref[2:3])
        dh_ref[...] = dh
        da_s[...] = dh.astype(BF16)
        cp.wait(*got)
        for t, at in enumerate(row_tiles(rows, SEG)):
            do = nn(da_s[at], w_s[0, :, 3 * quarter :]).astype(BF16)
            qkv_t = qkv_ref[at]
            cut = [
                [qkv_t[:, i * quarter + h * HEAD : i * quarter + (h + 1) * HEAD] for i in range(3)]
                for h in range(heads)
            ]
            dos = [do[:, h * HEAD : (h + 1) * HEAD] for h in range(heads)]
            dss = []
            for h in range(heads):
                pf = p_ref[t, h].astype(F32)
                pd = pf * nt(dos[h], cut[h][2])
                dss.append((pd - pf * jnp.sum(pd, axis=-1, keepdims=True)).astype(BF16))
            dq, dk, dv = [], [], []
            for h in range(heads):
                dv.append(tn(p_ref[t, h], dos[h]).astype(BF16))
                dq.append((nn(dss[h], cut[h][1]) * SCALE).astype(BF16))
                dk.append((tn(dss[h], cut[h][0]) * SCALE).astype(BF16))
            dqkv_s[at] = jnp.concatenate(dq + dk + dv, axis=1)
        dx_ref[...] = nt(dqkv_s[...], w_s[0, :, : 3 * quarter]).astype(BF16)
        g[:, : 3 * quarter] = tn(c_ref[...].astype(BF16), dqkv_s[...])
        g[:, 3 * quarter :] = tn(da_s[...], o_ref[...])
        own_rows(cp, blocked, blk_ref, g, g_out)
        cp.wait_all()

    return call(
        body,
        (sds((rows, d), F32), sds((rows, d), BF16), sds((own, d), F32), sds((8, d), F32)),
        (WHOLE, WHOLE, ANY, WHOLE),
        [SMEM] + [WHOLE] * 10 + [ANY] * len(w),
        [
            VMEM((rows, d), BF16),
            VMEM((rows, 3 * quarter), BF16),
            VMEM((1, d, d), BF16),
            VMEM((d, d), F32),
            DMA((9,)),
        ],
        us=5,
    )(blk, dh2, d0, d1, n1, r1, c, qkv, o, p, nv, *w)


def swap(axis, size, bit, value):
    return lax.ppermute(value, axis, [(i, i ^ bit) for i in range(size)])


core_swap = functools.partial(swap, "tensor", 4, 1)
y_swap = functools.partial(swap, "tensor", 4, 2)
x_swap = functools.partial(swap, "dp", 8, 1)


def z_swap(k, value):
    return swap("dp", 8, 2 * k, value)


def tied(*trees):
    return lax.optimization_barrier(trees)


PLANES = ((0, 0), (0, 1), (1, 0))
ATTN_PIECES = (
    [(n, (), 0, y, x, 0) for n, (y, x) in enumerate(PLANES)]
    + [(3 + n, (k - 1,), 0, y, x, k) for n, (y, x) in enumerate(PLANES) for k in (1, 2, 3)]
    + [(6, (k,), 0, 1, 1, k) for k in (0, 1)]
    + [(7, (k - 2,), 0, 1, 1, k) for k in (2, 3)]
)
MLP_PIECES = (
    [(n, (), 1, y, x, 0) for n, (y, x) in enumerate(PLANES)]
    + [(3 + n, (k - 1,), 0, y, x, k) for n, (y, x) in enumerate(PLANES) for k in (1, 2, 3)]
    + [(6, (k,), 0, 1, 1, k) for k in (0, 1)]
    + [(7, (k - 2,), 0, 1, 1, k) for k in (2, 3)]
)


def both_cores(pieces, count):
    return [
        (count * c + which, lead, pack, 2 * c + y, 4 * x + z)
        for c in range(2)
        for which, lead, pack, y, x, z in pieces
    ]


PLAIN_PLAN = [(0, (j,), 0, j, None) for j in range(4)]


def xor_order(stacked, index, bits):
    shape = stacked.shape
    out = stacked.reshape((2,) * bits + shape[1:])
    for b in range(bits):
        out = jnp.where((index >> (bits - 1 - b)) & 1 == 1, jnp.flip(out, b), out)
    return out.reshape(shape)


def add(*parts):
    total = parts[0].astype(F32)
    for p in parts[1:]:
        total = total + p.astype(F32)
    return total


def low_add(*parts):
    return add(*parts).astype(BF16)


class Scatter:
    def __init__(self, g0, g1_swapped):
        self.g = (g0, g1_swapped)

    def own(self, y, x, zs):
        return tuple(g[y, x, zs] for g in self.g)

    def diagonal(self):
        return low_add(*self.own(1, 1, slice(0, 2))), low_add(*self.own(1, 1, slice(2, 4)))

    def columns(self, from_x, from_y):
        lo, hi = slice(0, 2), slice(2, 4)
        to_x = jnp.concatenate([low_add(*self.own(0, 1, lo)), low_add(*self.own(0, 1, hi), from_y)])
        to_y = jnp.concatenate([low_add(*self.own(1, 0, lo), from_x), low_add(*self.own(1, 0, hi))])
        return to_x, to_y

    def planes(self, from_x, from_y):
        self.mine = (*self.own(0, 0, 0), from_x[0], from_y[0])
        return [low_add(*self.own(0, 0, k), from_x[k], from_y[k]) for k in (1, 2, 3)]

    def last(self, back):
        return add(*self.mine, *back)


def body(tokens, w_qkv, w_out, w_up, w_down, norm_gain, norm_bias, seg_table, seg_ids, cotangent):
    nd, ntens = lax.axis_size("dp"), lax.axis_size("tensor")
    fast = nd == 8
    di, ti = lax.axis_index("dp"), lax.axis_index("tensor")
    seqs, toks, d = tokens.shape
    rows, dblk = seqs * toks, tokens.shape[2] // nd
    per_dev = toks // SEG
    x = tokens.reshape(rows, d)
    cot = cotangent.reshape(rows, d)

    def pack(b):
        return (
            jnp.concatenate([w_qkv[b].reshape(dblk, -1), w_out[b].T], axis=1),
            jnp.stack([w_up[b], w_down[b].T]),
        )

    attn0, mlp0 = pack(0)
    attn1, mlp1 = pack(1)
    small = jnp.concatenate(
        [norm_gain.reshape(4, dblk), norm_bias.reshape(4, dblk), seg_table], axis=0
    )
    onehot = (seg_ids.reshape(-1, 1) == jnp.arange(128, dtype=jnp.int32)).astype(BF16)

    p3 = jnp.concatenate([attn1[None], mlp1])

    def place(leaders):
        leaders = leaders.reshape(seqs, per_dev, -1)
        space = jnp.zeros((seqs, per_dev * ntens, leaders.shape[-1]), BF16)
        return lax.dynamic_update_slice(space, leaders, (0, per_dev * ti, 0)).reshape(
            -1, leaders.shape[-1]
        )

    if fast:
        zi, xi = di // 2, di % 2
        blk = jnp.stack([(zi ^ k) * 2 + (xi ^ l) for l in range(2) for k in range(4)]).astype(jnp.int32)

        def z_all(p):
            return [z_swap(k, p) for k in (1, 2, 3)]

        tiny = jnp.pad(small, ((0, 0), (0, d - dblk)))
        p_all = jnp.concatenate([attn0, mlp0.reshape(-1, d), tiny])
        z1, x0, y0 = z_all(p_all[:dblk]), x_swap(p_all), y_swap(p_all)
        z1, x0, y0, pm = tied(z1, x0, y0, p_all[dblk:])
        c1 = jnp.stack(z1)
        xc1, yc1 = x_swap(c1), y_swap(c1)
        zm = z_all(pm)
        xc1, yc1 = tied(xc1, yc1)
        ex1, ey1 = x_swap(jnp.stack([y0[:dblk], yc1[0]])), y_swap(xc1[1:])
        ex1, ey1, p3a = tied(ex1, ey1, p3[0])
        z3a = z_all(p3a)
        base = [p_all, x0, y0]
        base_core = [core_swap(v) for v in base]
        mine1 = [c1, xc1, yc1, ex1, ey1]
        attn_pieces = base + mine1 + base_core + [core_swap(v) for v in mine1]
        attn_plan = both_cores(ATTN_PIECES, 8)
        cm = jnp.stack(zm)
        xcm, ycm = x_swap(cm), y_swap(cm)
    else:
        blk = jnp.zeros((8,), jnp.int32)

        def whole(p):
            g = lax.all_gather(p, ("tensor", "dp"), axis=0)
            g = g.reshape(ntens, nd, p.shape[0], dblk, d).transpose(0, 2, 1, 3, 4)
            g = g.reshape(ntens, p.shape[0] * d, d)
            return xor_order(g, ti, 2)

        attn_pieces, mlp_pieces = [whole(attn0[None])], [whole(mlp0)]
        attn_plan = mlp_plan = PLAIN_PLAN
        w1 = lax.all_gather(p3, "dp", axis=1, tiled=True)
        w1a, w1m = [w1[:1]], [w1[1:]]
        nv = lax.all_gather(small, "dp", axis=1, tiled=True).astype(F32)
    w_a, qkv, o, p, n1, r1, n_first = attn_forward(attn_plan, blk, x, attn_pieces)

    if fast:
        n_first, z3a = tied(n_first, z3a)
    narrow = d + onehot.shape[1]
    pay = place(jnp.concatenate([n_first[:, 0], onehot, cot.reshape(-1, SEG, d)[:, 0]], axis=1))
    if fast:
        pay = pay + core_swap(pay)
        pay = pay + y_swap(pay)
        xcm, ycm, pay = tied(xcm, ycm, pay)
        p3u, p3d, pay = p3[1], jnp.concatenate([p3[2], pay[:, narrow:]]), pay[:, :narrow]
        to_x, to_y, p3u = tied(jnp.stack([y0[dblk:], ycm[0]]), xcm[1:], p3u)
        ex2, ey2 = x_swap(to_x), y_swap(to_y)
        z3u = z_all(p3u)
        pay = jnp.stack([pay, x_swap(pay)])
        at = 3 * dblk
        tiny = jnp.stack(
            [jnp.stack([p_all[at:], x0[at:]])]
            + [jnp.stack([a[2 * dblk :], b[2 * dblk :]]) for a, b in zip(zm, xcm)]
        )[..., :dblk]
        nv = xor_order(tiny.reshape(nd, 16, dblk), di, 3)
        nv = nv.transpose(1, 0, 2).reshape(16, d).astype(F32)
        w1a = jnp.stack([p3a] + z3a)
        ex2, ey2 = tied(ex2, ey2)
        ex2, ey2, pay, z3u, p3d, w1a, nv = tied(ex2, ey2, pay, z3u, p3d, w1a, nv)
        mine2 = [cm, xcm, ycm, ex2, ey2]
        mlp_pieces = base + mine2 + base_core + [core_swap(v) for v in mine2]
        mlp_plan = both_cores(MLP_PIECES, 8)
        pay = jnp.stack([pay] + z_all(pay))
        first = 0
        z3d = z_all(p3d)
        w1a = [w1a, x_swap(w1a)]
    else:
        pay = lax.all_gather(lax.psum(pay, "tensor"), "dp", axis=0)
        first = di * seqs * per_dev * ntens
    pay = pay.reshape(-1, pay.shape[-1])
    lead_n, lead_hot = pay[:, :d], pay[:, d:narrow]
    if not fast:
        lead_cot = pay[:, narrow:]

    wu, wd, ybl, gbl, gpl, zl, nl, rl = lead_forward(mlp_plan, blk, lead_n, nv, mlp_pieces)
    if fast:
        z3d, zl, w1a = tied(z3d, zl, w1a)
        w1m = jnp.stack([jnp.concatenate(v) for v in zip([p3u] + z3u, [p3d] + z3d)])
        w1m = [w1m, x_swap(w1m)]
        lead_cot = jnp.stack(w1m, axis=1)[:, :, 2 * dblk :].reshape(-1, d)

    def near_sum(part):
        if fast:
            return low_add(part, core_swap(part))
        return lax.psum(part.astype(F32), "tensor")

    def far_sum(half):
        return y_swap(half) if fast else jnp.zeros_like(half)

    c, cqkv, co, cp, ca = cross_attn(blk, zl, lead_hot, nv, w1a)
    s1 = near_sum(ca)
    t1 = far_sum(s1)
    n2, s1 = tied(n1, s1)
    gb, gp, yb, dm, g1, dy, result, sums2 = mlp_forward(nd, fast, blk, n2, cot, nv, wu, wd)
    t1, sums2, w1m = tied(t1, sums2, w1m)
    cy, cn, cr, cgb, cgp, cm = cross_mlp(blk, c, s1, t1, nv, w1m)
    s2 = near_sum(cm)
    t2 = far_sum(s2)
    dm, s2 = tied(dm, s2)
    g0, dy = mlp_backward(nd, fast, blk, dm, yb, gb, gp, wu, wd, dy)
    t2, dy = tied(t2, dy)
    e, cdh2, cgd, cgu, cdy, csum2 = cross_mlp_back(
        nd, fast, blk, cy, s2, t2, lead_cot, nv, cgb, cgp, w1m
    )
    if fast:

        def shards(g):
            return g.reshape(2, 2, 4, *g.shape[2:])

        other_m, cdy = tied(core_swap(shards(g1)), cdy)
    s3 = near_sum(cdy)
    t3 = far_sum(s3)
    if fast:
        sm_ = Scatter(shards(g0), other_m)
        ops = sm_.diagonal()
        t3, ops = tied(t3, ops)
        diag = x_swap(ops[0]), y_swap(ops[1])
    t3, dy = tied(t3, dy)
    cdh, cdx, cga, csum1 = cross_attn_back(
        nd, fast, blk, cdh2, s3, t3, cn, cr, c, cqkv, co, cp, nv, w1a
    )
    s4 = near_sum(cdx)
    t4 = far_sum(s4)
    if fast:
        diag, s4 = tied(diag, s4)
        ops = sm_.columns(*diag)
        t4, ops = tied(t4, ops)
        cols = x_swap(ops[0]), y_swap(ops[1])
    def own_leaders(full):
        part = lax.dynamic_slice_in_dim(full, first, seqs * per_dev * ntens, 0)
        part = part.reshape(seqs, per_dev * ntens, d)
        return lax.dynamic_slice_in_dim(part, per_dev * ti, per_dev, 1).reshape(-1, d)

    lead = (cdh, s4, t4, lead_hot, nl, rl, ybl, gbl, gpl, wu, wd)
    if fast:
        spot = jnp.stack([s * per_dev * ntens + per_dev * ti + i for s in range(seqs) for i in range(per_dev)])
        first_in = (dy, spot.astype(jnp.int32), n1, r1, nv, sums2)
        a1, dx, da, sums, lgd, lgu, lsum = attn_backward(
            1, nd, fast, blk, x, qkv, o, p, w_a, first_in, None, lead
        )
    else:
        dyl, lgd, lgu, lsum = lead_backward(nd, fast, blk, nv, lead)
        first_in = (dy, own_leaders(dyl), n1, r1, nv, sums2)
        a1, dx, da, sums = attn_backward(1, nd, fast, blk, x, qkv, o, p, w_a, first_in, None)
    if fast:
        cols, dx = tied(cols, dx)
        ops = sm_.planes(*cols)
        dx, ops = tied(dx, ops)
        planes = [z_swap(kk, op) for kk, op in zip((1, 2, 3), ops)]
        other = core_swap(shards(a1))
    a0, dx = attn_backward(0, nd, fast, blk, x, qkv, o, p, w_a, None, (da, dx, sums))

    if fast:
        sa = Scatter(shards(a0), other)
        ops = sa.diagonal()
        ops, e, csum1, csum2, cga, cgu, cgd, lsum, lgd, lgu = tied(
            ops, e, csum1, csum2, cga, cgu, cgd, lsum, lgd, lgu
        )
        diag = x_swap(ops[0]), y_swap(ops[1])
        planes, diag = tied(planes, diag)
        ops = sa.columns(*diag)
        cols = x_swap(ops[0]), y_swap(ops[1])
        ops = sa.planes(*cols)
        gm = sm_.last(planes)
        ga = sa.last([z_swap(kk, op) for kk, op in zip((1, 2, 3), ops)])[0]
        norm_sums = ga[dblk : dblk + 8, :dblk]
        ga = ga[:dblk]
    else:

        def owned(lo, hi):
            g = jnp.concatenate([lo, hi])
            g = xor_order(g, ti, 2).astype(F32)
            g = lax.psum_scatter(g, "tensor", scatter_dimension=0)
            return lax.psum_scatter(g, "dp", scatter_dimension=1, tiled=True)

        gm, ga = owned(g0, g1), owned(a0, a1)[0]
        norm_sums = lax.psum_scatter(
            lax.psum(sums, "tensor"), "dp", scatter_dimension=1, tiled=True
        )

    def rows_of(full):
        if fast:
            return full
        return lax.dynamic_slice_in_dim(full, di * dblk, dblk, 0)

    def cols_of(full):
        return lax.dynamic_slice_in_dim(full, di * dblk, dblk, 1)

    gu0, gd0 = gm[0] + rows_of(lgu), gm[1] + rows_of(lgd)
    ga1, gu1, gd1 = rows_of(cga), rows_of(cgu), rows_of(cgd)
    wide = w_qkv.shape[3] * 3
    grad_qkv = jnp.stack([ga[:, :wide], ga1[:, :wide]]).reshape(w_qkv.shape)
    grad_out = jnp.stack([ga[:, wide:].T, ga1[:, wide:].T])
    grad_up = jnp.stack([gu0, gu1])
    grad_down = jnp.stack([gd0.T, gd1.T])
    lsum, csum1, csum2 = cols_of(lsum), cols_of(csum1), cols_of(csum2)
    grad_gain = jnp.stack(
        [
            jnp.stack([norm_sums[0], norm_sums[2] + lsum[0]]),
            jnp.stack([csum1[0], csum2[0]]),
        ]
    )
    grad_bias = jnp.stack(
        [
            jnp.stack([norm_sums[1], norm_sums[3] + lsum[1]]),
            jnp.stack([csum1[1], csum2[1]]),
        ]
    )
    result = result.reshape(-1, SEG, d).at[:, 0].set(own_leaders(e)).reshape(tokens.shape)
    return (
        result,
        dx.reshape(tokens.shape),
        grad_qkv,
        grad_out,
        grad_up,
        grad_down,
        grad_gain,
        grad_bias,
        lsum[8:16],
    )


def solution(mesh):
    return jax.shard_map(
        body,
        mesh=mesh,
        in_specs=(
            P("dp", "tensor", None),
            P(None, "dp", None, "tensor"),
            P(None, "tensor", "dp"),
            P(None, "dp", "tensor"),
            P(None, "tensor", "dp"),
            P(None, None, "dp"),
            P(None, None, "dp"),
            P(None, "dp"),
            P("dp", "tensor"),
            P("dp", "tensor", None),
        ),
        out_specs=(
            P("dp", "tensor", None),
            P("dp", "tensor", None),
            P(None, "dp", None, "tensor"),
            P(None, "tensor", "dp"),
            P(None, "dp", "tensor"),
            P(None, "tensor", "dp"),
            P(None, None, "dp"),
            P(None, None, "dp"),
            P(None, "dp"),
        ),
        check_vma=False,
    )
```

```python
import functools
import math

import jax
import jax.numpy as jnp
from jax import lax
from jax.experimental import pallas as pl
from jax.experimental.pallas import tpu as pltpu
from jax.sharding import PartitionSpec as P

HEAD = 64
SEG = 128
GROUP = 8
F32, BF16 = jnp.float32, jnp.bfloat16
VMEM = pltpu.VMEM
ANY = pl.BlockSpec(memory_space=pl.ANY)
WHOLE = pl.BlockSpec(memory_space=pltpu.VMEM)
SMEM = pl.BlockSpec(memory_space=pltpu.SMEM)
PARAMS = pltpu.CompilerParams(vmem_limit_bytes=60 << 20)
EPS = 1e-05
SCALE = HEAD ** (-0.5)
RSQRT2 = 1.0 / math.sqrt(2.0)
RSQRT2PI = 1.0 / math.sqrt(2.0 * math.pi)


def nn(a, b):
    return lax.dot_general(a, b, (((1,), (0,)), ((), ())), preferred_element_type=F32)


def nt(a, b):
    return lax.dot_general(a, b, (((1,), (1,)), ((), ())), preferred_element_type=F32)


def tn(a, b):
    return lax.dot_general(a, b, (((0,), (0,)), ((), ())), preferred_element_type=F32)


def norm_parts(h):
    center = h - jnp.mean(h, axis=-1, keepdims=True)
    rstd = lax.rsqrt(jnp.mean(center * center, axis=-1, keepdims=True) + EPS)
    return center * rstd, rstd


def norm_back(grad, normed, rstd, gain):
    dn = grad * gain
    return rstd * (
        dn
        - jnp.mean(dn, axis=-1, keepdims=True)
        - normed * jnp.mean(dn * normed, axis=-1, keepdims=True)
    )


def gelu_both(u):
    cdf = 0.5 + 0.5 * lax.erf(u * RSQRT2)
    return u * cdf, cdf + u * (jnp.exp(-0.5 * u * u) * RSQRT2PI)


def halves(pair):
    lane = lax.broadcasted_iota(jnp.int32, pair.shape, 1)
    zero = jnp.zeros_like(pair)
    return jnp.concatenate(
        [jnp.where(lane < HEAD, pair, zero), jnp.where(lane < HEAD, zero, pair)], axis=0
    )


def unhalve(stacked):
    lane = lax.broadcasted_iota(jnp.int32, (SEG, 2 * HEAD), 1)
    return jnp.where(lane < HEAD, stacked[:SEG], stacked[SEG:])


def half_softmax(s):
    top = jnp.concatenate(
        [
            jnp.broadcast_to(jnp.max(s[:, :SEG], axis=-1, keepdims=True), (SEG, SEG)),
            jnp.broadcast_to(jnp.max(s[:, SEG:], axis=-1, keepdims=True), (SEG, SEG)),
        ],
        axis=1,
    )
    ex = jnp.exp(s - top)
    inv = jnp.concatenate(
        [
            jnp.broadcast_to(1.0 / jnp.sum(ex[:, :SEG], axis=-1, keepdims=True), (SEG, SEG)),
            jnp.broadcast_to(1.0 / jnp.sum(ex[:, SEG:], axis=-1, keepdims=True), (SEG, SEG)),
        ],
        axis=1,
    )
    return ex * inv


def call(body, outs, out_specs, in_specs, scratch=(), us=10):
    return pl.pallas_call(
        body,
        out_shape=outs,
        in_specs=in_specs,
        out_specs=out_specs,
        scratch_shapes=list(scratch),
        compiler_params=PARAMS,
        cost_estimate=pl.CostEstimate(flops=int(us * 2e9), bytes_accessed=1, transcendentals=0),
    )


def sds(shape, dtype):
    return jax.ShapeDtypeStruct(shape, dtype)


DMA = pltpu.SemaphoreType.DMA


class Copies:
    def __init__(self, sems):
        self.sems, self.used, self.open = sems, 0, []

    def start(self, src, dst):
        copy = pltpu.make_async_copy(src, dst, self.sems.at[self.used])
        self.used += 1
        copy.start()
        self.open.append(copy)
        return copy

    def wait(self, *copies):
        for c in copies:
            if any(c is other for other in self.open):
                self.open = [other for other in self.open if other is not c]
                c.wait()

    def wait_all(self):
        for c in self.open:
            c.wait()
        self.open = []


def fetch(cp, plan, pieces, pack, blk_ref, dst, d):
    out = []
    for which, lead, start, j, slot in plan:
        rows = d if slot is None else d // 8
        src = pieces[which].at[(*lead, pl.ds((start + pack) * rows, rows))]
        at = pl.ds(0 if slot is None else pl.multiple_of(blk_ref[slot] * rows, 16), rows)
        out.append(cp.start(src, dst.at[at, pl.ds(j * d, d)]))
    return out


def row_tiles(rows, tile):
    return [slice(i, min(i + tile, rows)) for i in range(0, rows, tile)]


def attn_forward(plan, blk, x, pieces):
    rows, d = x.shape
    segs, quarter = rows // SEG, d // 4
    pairs = d // SEG
    np_ = len(pieces)

    def body(blk_ref, x_hbm, *refs):
        ins, refs = refs[:np_], refs[np_:]
        w_out, qkv_out, o_out, p_out, n_out, r_ref, nl_ref = refs[:7]
        raw, w, x_s, qkv, o_s, p_s, n_s, sems = refs[7:]
        cp = Copies(sems)
        got = fetch(cp, plan, ins, 0, blk_ref, raw, d)
        got_x = cp.start(x_hbm, x_s)
        cp.wait(*got)
        for t in range(4):
            for half in range(2):
                j = 2 * half
                at = slice(t * d + j * quarter, t * d + (j + 2) * quarter)
                w[:, at] = jnp.concatenate(
                    [
                        raw[:, j * d + t * quarter : j * d + (t + 1) * quarter],
                        raw[:, (j + 1) * d + t * quarter : (j + 1) * d + (t + 1) * quarter],
                    ],
                    axis=1,
                )
        cp.start(w, w_out)
        cp.wait(got_x)
        qkv[...] = nn(x_s[...], w[:, : 3 * d]).astype(BF16)
        cp.start(qkv, qkv_out)
        for t in range(segs):
            at = slice(t * SEG, (t + 1) * SEG)
            probs = []
            for pair in range(pairs):
                lo = pair * SEG
                s = nt(qkv[at, lo : lo + SEG], halves(qkv[at, d + lo : d + lo + SEG])) * SCALE
                probs.append(half_softmax(s).astype(BF16))
            for pair in range(pairs):
                lo = pair * SEG
                p_s[t, pair] = probs[pair]
                o_s[at, lo : lo + SEG] = nn(
                    probs[pair], halves(qkv[at, 2 * d + lo : 2 * d + lo + SEG])
                ).astype(BF16)
            cp.start(p_s.at[t], p_out.at[t])
        cp.start(o_s, o_out)
        n_s[...] = nt(o_s[...], w[:, 3 * d :])
        for t in range(segs):
            at = slice(t * SEG, (t + 1) * SEG)
            n, r = norm_parts(x_s[at].astype(F32) + n_s[at])
            n_s[at] = n
            r_ref[at] = r
            nl_ref[t] = n[0:8].astype(BF16)
            cp.start(n_s.at[at], n_out.at[at])
        cp.wait_all()

    return call(
        body,
        (
            sds((d, 4 * d), BF16),
            sds((rows, 3 * d), BF16),
            sds((rows, d), BF16),
            sds((segs, pairs, SEG, 2 * SEG), BF16),
            sds((rows, d), F32),
            sds((rows, 1), F32),
            sds((segs, 8, d), BF16),
        ),
        (ANY,) * 5 + (WHOLE,) * 2,
        [SMEM, ANY] + [ANY] * np_,
        [
            VMEM((d, 4 * d), BF16),
            VMEM((d, 4 * d), BF16),
            VMEM((rows, d), BF16),
            VMEM((rows, 3 * d), BF16),
            VMEM((rows, d), BF16),
            VMEM((segs, pairs, SEG, 2 * SEG), BF16),
            VMEM((rows, d), F32),
            DMA((len(plan) + 4 + 2 * segs,)),
        ],
        us=30,
    )(blk, x, *pieces)


def lead_forward(plan, blk, lead_n, nv, pieces):
    leads, d = lead_n.shape
    np_ = len(pieces)

    def body(blk_ref, ln_ref, nv_ref, *refs):
        ins, refs = refs[:np_], refs[np_:]
        wu_out, wd_out, yb_ref, gb_ref, gp_ref, zl_ref, nl_ref, rl_ref, wu, wd, sems = refs

        def lead_y(at):
            return ln_ref[at].astype(F32) * nv_ref[0:1] + nv_ref[4:5]

        cp = Copies(sems)
        got_u = fetch(cp, plan, ins, 0, blk_ref, wu, d)
        got_d = fetch(cp, plan, ins, 1, blk_ref, wd, d)
        cp.wait(*got_u)
        cp.start(wu, wu_out)
        for at in row_tiles(leads, SEG):
            yb_ref[at] = lead_y(at).astype(BF16)
            g, gd = gelu_both(nn(yb_ref[at], wu[...]))
            gb_ref[at] = g.astype(BF16)
            gp_ref[at] = gd.astype(BF16)
        cp.wait(*got_d)
        cp.start(wd, wd_out)
        for at in row_tiles(leads, SEG):
            n, r = norm_parts(lead_y(at) + nt(gb_ref[at], wd[...]))
            zl_ref[at] = n * nv_ref[1:2] + nv_ref[5:6]
            nl_ref[at] = n
            rl_ref[at] = r
        cp.wait_all()

    return call(
        body,
        (
            sds((d, 4 * d), BF16),
            sds((d, 4 * d), BF16),
            sds((leads, d), BF16),
            sds((leads, 4 * d), BF16),
            sds((leads, 4 * d), BF16),
            sds((leads, d), F32),
            sds((leads, d), F32),
            sds((leads, 1), F32),
        ),
        (ANY, ANY) + (WHOLE,) * 6,
        [SMEM, WHOLE, WHOLE] + [ANY] * np_,
        [VMEM((d, 4 * d), BF16), VMEM((d, 4 * d), BF16), DMA((2 * len(plan) + 2,))],
        us=20,
    )(blk, lead_n, nv, *pieces)


def put_blocks(cp, blocked, blk_ref, src, out, y, pack, slots):
    if not blocked:
        cp.start(src, out.at[y, pack])
        return
    rows = src.shape[0] // slots
    for s in range(slots):
        at = pl.ds(pl.multiple_of(blk_ref[s] * rows, 16), rows)
        cp.start(src.at[at], out.at[y, s, pack, pl.ds(0, rows)])


def mlp_forward(slots, blocked, blk, n1, cot, nv, wu_, wd_):
    rows, d = n1.shape
    half, dblk = 2 * d, d // slots
    per = slots if blocked else 1

    def body(blk_ref, y_hbm, cot_hbm, nv_ref, wu_hbm, wd_hbm, *refs):
        gb_out, gp_out, yb_out, dm_out, g_out, dy_out, res_out, sums_ref = refs[:8]
        y_s, cot_s, wu, wd, yb, gb, gp, dm, dh_s, res, du, gd, gu, sems = refs[8:]
        cp = Copies(sems)
        got_y = cp.start(y_hbm, y_s)
        up, down = [], []
        for j in range(4):
            cols = pl.ds(j * d, d)
            up.append(cp.start(wu_hbm.at[:, cols], wu.at[:, cols]))
        down.append(cp.start(wd_hbm, wd))
        got_cot = cp.start(cot_hbm, cot_s)
        cp.wait(got_y)
        y_s[...] = y_s[...] * nv_ref[0:1] + nv_ref[4:5]
        yb[...] = y_s[...].astype(BF16)
        cp.start(yb, yb_out)
        for j in range(4):
            cols = slice(j * d, (j + 1) * d)
            cp.wait(up[j])
            act, slope = gelu_both(nn(yb[...], wu[:, cols]))
            gb[:, cols] = act.astype(BF16)
            gp[:, cols] = slope.astype(BF16)
            if j < 2:
                cp.start(gb.at[:, pl.ds(j * d, d)], gb_out.at[:, pl.ds(j * d, d)])
                cp.start(gp.at[:, pl.ds(j * d, d)], gp_out.at[:, pl.ds(j * d, d)])
        cp.wait(*down)
        cp.wait(got_cot)
        gain, bias = nv_ref[1:2], nv_ref[5:6]
        top, bottom = jnp.zeros((1, d), F32), jnp.zeros((1, d), F32)
        dh_s[...] = nt(gb[...], wd[...])
        for at in row_tiles(rows, SEG):
            n, r = norm_parts(y_s[at] + dh_s[at])
            res[at] = (n * gain + bias).astype(BF16)
            row = lax.broadcasted_iota(jnp.int32, (SEG, d), 0)
            grad = jnp.where(row == 0, 0.0, cot_s[at].astype(F32))
            top += jnp.sum(grad * n, axis=0, keepdims=True)
            bottom += jnp.sum(grad, axis=0, keepdims=True)
            dh = norm_back(grad, n, r, gain)
            dh_s[at] = dh
            dm[at] = dh.astype(BF16)
            for s, out in ((res, res_out), (dm, dm_out)):
                cp.start(s.at[at], out.at[at])
        sums_ref[...] = jnp.concatenate([top, bottom, jnp.zeros((6, d), F32)], axis=0)
        for y in range(2):
            mine = slice(y * d, (y + 1) * d)
            wide = slice(half + y * d, half + (y + 1) * d)
            gd[:, mine] = tn(dm[...], gb[:, wide]).astype(BF16)
            put_blocks(cp, blocked, blk_ref, gd.at[:, pl.ds(y * d, d)], g_out, y, 1, slots)
            du[:, mine] = (nn(dm[...], wd[:, wide]) * gp[:, wide].astype(F32)).astype(BF16)
        for y in range(2):
            mine = slice(y * d, (y + 1) * d)
            gu[:, mine] = tn(yb[...], du[:, mine]).astype(BF16)
            put_blocks(cp, blocked, blk_ref, gu.at[:, pl.ds(y * d, d)], g_out, y, 0, slots)
        y_s[...] = dh_s[...] + nt(du[...], wu[:, half:])
        cp.start(y_s, dy_out)
        cp.wait_all()

    g_shape = (2, slots, 2, dblk, d) if blocked else (2, 2, d, d)

    return call(
        body,
        (
            sds((rows, half), BF16),
            sds((rows, half), BF16),
            sds((rows, d), BF16),
            sds((rows, d), BF16),
            sds(g_shape, BF16),
            sds((rows, d), F32),
            sds((rows, d), BF16),
            sds((8, d), F32),
        ),
        (ANY,) * 7 + (WHOLE,),
        [SMEM, ANY, ANY, WHOLE, ANY, ANY],
        [
            VMEM((rows, d), F32),
            VMEM((rows, d), BF16),
            VMEM((d, 4 * d), BF16),
            VMEM((d, 4 * d), BF16),
            VMEM((rows, d), BF16),
            VMEM((rows, 4 * d), BF16),
            VMEM((rows, 4 * d), BF16),
            VMEM((rows, d), BF16),
            VMEM((rows, d), F32),
            VMEM((rows, d), BF16),
            VMEM((rows, half), BF16),
            VMEM((d, half), BF16),
            VMEM((d, half), BF16),
            DMA((14 + 2 * (rows // SEG) + 4 * per,)),
        ],
        us=0.01,
    )(blk, n1, cot, nv, wu_, wd_)


def mlp_backward(slots, blocked, blk, dm_, yb_, gb_, gp_, wu_, wd_, start_):
    rows, d = dm_.shape
    dblk = d // slots
    per = slots if blocked else 1
    half = 2 * d

    def body(blk_ref, dm_hbm, yb_hbm, gb_hbm, gp_hbm, wu_hbm, wd_hbm, st_hbm, g_out, dy_out, *scr):
        dm, yb, gb, gp, wu, wd, st, du, gd, gu, dy, sems = scr
        cp = Copies(sems)
        cols = pl.ds(0, half)
        got_dm = cp.start(dm_hbm, dm)
        got_gb = cp.start(gb_hbm, gb)
        got_wd = cp.start(wd_hbm.at[:, cols], wd)
        got_gp = cp.start(gp_hbm, gp)
        got_yb = cp.start(yb_hbm, yb)
        got_wu = cp.start(wu_hbm.at[:, cols], wu)
        got_st = cp.start(st_hbm, st)
        cp.wait(got_dm, got_gb)
        for y in range(2):
            mine = slice(y * d, (y + 1) * d)
            gd[:, mine] = tn(dm[...], gb[:, mine]).astype(BF16)
            put_blocks(cp, blocked, blk_ref, gd.at[:, pl.ds(y * d, d)], g_out, y, 1, slots)
        cp.wait(got_wd, got_gp)
        for y in range(2):
            mine = slice(y * d, (y + 1) * d)
            du[:, mine] = (nn(dm[...], wd[:, mine]) * gp[:, mine].astype(F32)).astype(BF16)
        cp.wait(got_yb)
        for y in range(2):
            mine = slice(y * d, (y + 1) * d)
            gu[:, mine] = tn(yb[...], du[:, mine]).astype(BF16)
            put_blocks(cp, blocked, blk_ref, gu.at[:, pl.ds(y * d, d)], g_out, y, 0, slots)
        cp.wait(got_wu, got_st)
        dy[...] = st[...] + nt(du[...], wu[...])
        cp.start(dy, dy_out)
        cp.wait_all()

    g_shape = (2, slots, 2, dblk, d) if blocked else (2, 2, d, d)
    return call(
        body,
        (sds(g_shape, BF16), sds((rows, d), F32)),
        (ANY, ANY),
        [SMEM] + [ANY] * 7,
        [
            VMEM((rows, d), BF16),
            VMEM((rows, d), BF16),
            VMEM((rows, half), BF16),
            VMEM((rows, half), BF16),
            VMEM((d, half), BF16),
            VMEM((d, half), BF16),
            VMEM((rows, d), F32),
            VMEM((rows, half), BF16),
            VMEM((d, half), BF16),
            VMEM((d, half), BF16),
            VMEM((rows, d), F32),
            DMA((7 + 4 * per + rows // (2 * SEG),)),
        ],
        us=8,
    )(blk, dm_, yb_, gb_, gp_, wu_, wd_, start_)


def own_rows(cp, blocked, blk_ref, src, out):
    if blocked:
        rows = out.shape[0]
        src = src.at[pl.ds(pl.multiple_of(blk_ref[0] * rows, 8), rows)]
    cp.start(src, out)


def sums_of(grad, n):
    d = grad.shape[1]
    return jnp.concatenate(
        [
            jnp.sum(grad * n, axis=0, keepdims=True),
            jnp.sum(grad, axis=0, keepdims=True),
            jnp.zeros((6, d), F32),
        ],
        axis=0,
    )


LEAD_INS = [WHOLE] * 7 + [ANY] * 4


def lead_scratch(rows, d):
    return [
        VMEM((rows, d), BF16),
        VMEM((rows, 4 * d), BF16),
        VMEM((d, 4 * d), BF16),
        VMEM((d, 4 * d), BF16),
        VMEM((d, d), F32),
        VMEM((d, d), F32),
    ]


def lead_fetch(cp, ins, scr):
    gb_hbm, gp_hbm, wu_hbm, wd_hbm = ins[7:]
    gb, gp, wu, wd, _, _ = scr
    d = gb.shape[1]
    got = [cp.start(wd_hbm, wd), cp.start(gp_hbm, gp), cp.start(wu_hbm, wu)]
    return got + [cp.start(gb_hbm.at[:, pl.ds(0, d)], gb)]


def lead_grads(cp, blocked, blk_ref, nv_ref, ins, scr, got, dy_ref, gd_out, gu_out, sums_ref):
    dh_ref, d0_ref, d1_ref, oh_ref, n_ref, r_ref, yb_ref = ins[:7]
    gb, gp, wu, wd, gd, gu = scr
    d = gb.shape[1]
    grad = dh_ref[...] + (d0_ref[...].astype(F32) + d1_ref[...].astype(F32))
    n = n_ref[...]
    tops = [sums_of(grad, n)]
    for i in range(8):
        tops.append(jnp.sum(oh_ref[:, i : i + 1].astype(F32) * grad, axis=0, keepdims=True))
    sums_ref[...] = jnp.concatenate(tops, axis=0)
    dh2 = norm_back(grad, n, r_ref[...], nv_ref[1:2])
    dm = dh2.astype(BF16)
    cp.wait(*got[:2])
    du = (nn(dm, wd[...]) * gp[...].astype(F32)).astype(BF16)
    cp.wait(got[2])
    dy_ref[...] = dh2 + nt(du, wu[...])
    cp.wait(got[3])
    gd[...] = tn(dm, gb[...])
    own_rows(cp, blocked, blk_ref, gd, gd_out)
    gu[...] = tn(yb_ref[...], du[:, :d])
    own_rows(cp, blocked, blk_ref, gu, gu_out)


def lead_backward(slots, blocked, blk, nv, lead):
    rows, d = lead[0].shape
    own = d // slots if blocked else d
    n_in = len(lead)

    def body(blk_ref, nv_ref, *refs):
        ins, refs = refs[:n_in], refs[n_in:]
        dy_ref, gd_out, gu_out, sums_ref, *scr, sems = refs
        cp = Copies(sems)
        got = lead_fetch(cp, ins, scr)
        lead_grads(cp, blocked, blk_ref, nv_ref, ins, scr, got, dy_ref, gd_out, gu_out, sums_ref)
        cp.wait_all()

    return call(
        body,
        (sds((rows, d), F32), sds((own, d), F32), sds((own, d), F32), sds((16, d), F32)),
        (WHOLE, ANY, ANY, WHOLE),
        [SMEM, WHOLE] + LEAD_INS,
        lead_scratch(rows, d) + [DMA((6,))],
        us=7,
    )(blk, nv, *lead)


def attn_backward(core, slots, blocked, blk, x_, qkv_, o_, p_, w_, first, rest, lead=None):
    rows, d = x_.shape
    segs, half, quarter = rows // SEG, d // 2, d // 4
    dblk = d // slots
    per = slots if blocked else 1
    pairs = half // SEG
    opening = first is not None
    extra = first if opening else rest
    inside = lead is not None
    leads = lead[0].shape[0] if inside else 0
    lead = tuple(lead) if inside else ()

    def body(blk_ref, x_hbm, qkv_hbm, o_hbm, p_hbm, w_hbm, *refs):
        more, refs = refs[: len(extra)], refs[len(extra) :]
        lead_ins, refs = refs[: len(lead)], refs[len(lead) :]
        n_out = (4 if opening else 2) + (3 if inside else 0)
        outs, scr = refs[:n_out], refs[n_out:]
        g_out, dx_out = outs[:2]
        x, qkv, o, p, w, st, da, do, dqkv, gr, ex, dx, sems = scr[:13]
        cp = Copies(sems)
        if opening:
            dy_hbm, ld_ref, n_hbm, r_ref, nv_ref, s2_ref = more
            da_out, sums_ref = outs[2:4]
            nb = scr[13]
            if inside:
                got_lead = lead_fetch(cp, lead_ins, scr[15:])
            got_dy = cp.start(dy_hbm, st)
            got_n = cp.start(n_hbm, nb)
        else:
            da_hbm, st_hbm, sums_ref = more
            got_da = cp.start(da_hbm, da)
        got_w = [
            cp.start(w_hbm.at[:, pl.ds(t * d + core * half, half)], w.at[:, pl.ds(t * half, half)])
            for t in (3, 0, 1, 2)
        ]
        got_qkv = [
            cp.start(
                qkv_hbm.at[:, pl.ds(t * d + core * half, half)], qkv.at[:, pl.ds(t * half, half)]
            )
            for t in (2, 0, 1)
        ]
        got_p = cp.start(p_hbm.at[:, pl.ds(core * pairs, pairs)], p)
        got_o = cp.start(o_hbm.at[:, pl.ds(core * half, half)], o)
        got_x = cp.start(x_hbm, x)
        if inside:
            lead_grads(
                cp, blocked, blk_ref, nv_ref, lead_ins, scr[15:], got_lead, scr[14], *outs[4:]
            )
        if opening:
            cp.wait(got_dy, got_n)
            top, bottom = jnp.zeros((1, d), F32), jnp.zeros((1, d), F32)
            for t in range(segs):
                at = slice(t * SEG, (t + 1) * SEG)
                row = lax.broadcasted_iota(jnp.int32, (SEG, d), 0)
                mine = scr[14][pl.ds(ld_ref[t], 1)] if inside else ld_ref[t : t + 1]
                grad = st[at] + jnp.where(row == 0, mine, 0.0)
                n = nb[at]
                top += jnp.sum(grad * n, axis=0, keepdims=True)
                bottom += jnp.sum(grad, axis=0, keepdims=True)
                dh = norm_back(grad, n, r_ref[at], nv_ref[0:1])
                st[at] = dh
                da[at] = dh.astype(BF16)
            cp.start(da, da_out)
            sums_ref[...] = jnp.concatenate(
                [top, bottom, s2_ref[0:2], jnp.zeros((4, d), F32)], axis=0
            )
        else:
            got_st = cp.start(st_hbm, st)
            cp.wait(got_da)
        if blocked:
            for b in range(slots):
                ex[b] = jnp.zeros((16, d), BF16)
                ex[b, 0:8, 0:dblk] = sums_ref[:, b * dblk : (b + 1) * dblk].astype(BF16)
            for y in range(2):
                for s in range(slots):
                    cp.start(ex.at[blk_ref[s]], g_out.at[y, s, 0, pl.ds(dblk, 16)])
        cp.wait(got_w[0])
        do[...] = nn(da[...], w[:, 3 * half :]).astype(BF16)
        cp.wait(got_p, *got_qkv)
        for t in range(segs):
            at = slice(t * SEG, (t + 1) * SEG)
            dss = []
            for pair in range(pairs):
                mine = slice(pair * SEG, (pair + 1) * SEG)
                pf = p[t, pair].astype(F32)
                v = qkv[at, 2 * half + pair * SEG : 2 * half + (pair + 1) * SEG]
                pd = pf * nt(do[at, mine], halves(v))
                parts = [
                    pd[:, c] - pf[:, c] * jnp.sum(pd[:, c], axis=-1, keepdims=True)
                    for c in (slice(0, SEG), slice(SEG, 2 * SEG))
                ]
                dss.append(jnp.concatenate(parts, axis=1).astype(BF16))
            for pair in range(pairs):
                mine = slice(pair * SEG, (pair + 1) * SEG)
                q, k = (qkv[at, i * half + pair * SEG : i * half + (pair + 1) * SEG] for i in (0, 1))
                ds = dss[pair]
                dv = unhalve(tn(p[t, pair], do[at, mine]))
                dk = unhalve(tn(ds, q)) * SCALE
                dq = nn(ds, halves(k)) * SCALE
                for i, g in enumerate((dq, dk, dv)):
                    dqkv[at, i * half + pair * SEG : i * half + (pair + 1) * SEG] = g.astype(BF16)
        cp.wait(got_x, got_o)
        gf = tn(x[...], dqkv[...]).astype(BF16)
        go = tn(da[...], o[...]).astype(BF16)
        for y in range(2):
            at = slice(y * quarter, (y + 1) * quarter)
            cut = [gf[:, i * half + y * quarter : i * half + (y + 1) * quarter] for i in range(3)]
            cut.append(go[:, at])
            gr[y, :, :half] = jnp.concatenate(cut[:2], axis=1)
            gr[y, :, half:] = jnp.concatenate(cut[2:], axis=1)
            put_blocks(cp, blocked, blk_ref, gr.at[y], g_out, y, 0, slots)
        if not opening:
            cp.wait(got_st)
        cp.wait(*got_w)
        dx[...] = st[...] + nt(dqkv[...], w[:, : 3 * half])
        cp.start(dx, dx_out)
        cp.wait_all()

    g_shape = (2, slots, 1, dblk + 16, d) if blocked else (2, 1, d, d)
    outs = [sds(g_shape, BF16), sds((rows, d), F32)]
    specs = [ANY, ANY]
    in_more = [ANY, ANY, WHOLE]
    if opening:
        outs += [sds((rows, d), BF16), sds((8, d), F32)]
        specs += [ANY, WHOLE]
        in_more = [ANY, SMEM if inside else WHOLE, ANY, WHOLE, WHOLE, WHOLE]
    if inside:
        own = d // slots if blocked else d
        outs += [sds((own, d), F32), sds((own, d), F32), sds((16, d), F32)]
        specs += [ANY, ANY, WHOLE]
        in_more += LEAD_INS
    scratch = [
        VMEM((rows, d), BF16),
        VMEM((rows, 3 * half), BF16),
        VMEM((rows, half), BF16),
        VMEM((segs, pairs, SEG, 2 * SEG), BF16),
        VMEM((d, 4 * half), BF16),
        VMEM((rows, d), F32),
        VMEM((rows, d), BF16),
        VMEM((rows, half), BF16),
        VMEM((rows, 3 * half), BF16),
        VMEM((2, d, d), BF16),
        VMEM((slots if blocked else 1, 16, d), BF16),
        VMEM((rows, d), F32),
        DMA((24 + 4 * per,)),
    ]
    if opening:
        scratch.append(VMEM((rows, d), F32))
    if inside:
        scratch += [VMEM((leads, d), F32)] + lead_scratch(leads, d)
    return call(
        body,
        tuple(outs),
        tuple(specs),
        [SMEM] + [ANY] * 5 + in_more,
        scratch,
        us=30,
    )(blk, x_, qkv_, o_, p_, w_, *extra, *lead)


def fetch_cross(cp, pieces, blk_ref, dst):
    if len(pieces) == 1:
        return [cp.start(pieces[0], dst)]
    packs, d, _ = dst.shape
    rows = d // 8
    out = []
    for slot in range(8):
        at = pl.ds(pl.multiple_of(blk_ref[slot] * rows, 16), rows)
        for p in range(packs):
            src = pieces[slot // 4].at[slot % 4, pl.ds(p * rows, rows)]
            out.append(cp.start(src, dst.at[p, at]))
    return out


def group_mask():
    a = lax.broadcasted_iota(jnp.int32, (SEG, SEG), 0) // GROUP
    b = lax.broadcasted_iota(jnp.int32, (SEG, SEG), 1) // GROUP
    return a == b


def cross_attn(blk, zl, onehot, nv, w):
    rows, d = zl.shape
    quarter = d // 4
    heads = quarter // HEAD
    tiles = rows // SEG

    def body(blk_ref, z_ref, oh_ref, nv_ref, *refs):
        c_ref, qkv_ref, o_ref, p_ref, a_ref, w_s, sems = refs[len(w) :]
        cp = Copies(sems)
        fetch_cross(cp, refs[: len(w)], blk_ref, w_s)
        cs = []
        for at in row_tiles(rows, SEG):
            c = z_ref[at]
            for i in range(8):
                c += oh_ref[at, i : i + 1].astype(F32) * nv_ref[8 + i : 9 + i]
            c_ref[at] = c
            cs.append(c.astype(BF16))
        cp.wait_all()
        mask = group_mask()
        for t, at in enumerate(row_tiles(rows, SEG)):
            qkv = nn(cs[t], w_s[0, :, : 3 * quarter]).astype(BF16)
            qkv_ref[at] = qkv
            cut = [
                [qkv[:, i * quarter + h * HEAD : i * quarter + (h + 1) * HEAD] for i in range(3)]
                for h in range(heads)
            ]
            probs = []
            for q, k, v in cut:
                s = jnp.where(mask, nt(q, k) * SCALE, -1e30)
                ex = jnp.exp(s - jnp.max(s, axis=-1, keepdims=True))
                probs.append((ex * (1.0 / jnp.sum(ex, axis=-1, keepdims=True))).astype(BF16))
            os = []
            for h in range(heads):
                p_ref[t, h] = probs[h]
                os.append(nn(probs[h], cut[h][2]).astype(BF16))
            o = jnp.concatenate(os, axis=1)
            o_ref[at] = o
            a_ref[at] = nt(o, w_s[0, :, 3 * quarter :]).astype(BF16)

    return call(
        body,
        (
            sds((rows, d), F32),
            sds((rows, 3 * quarter), BF16),
            sds((rows, quarter), BF16),
            sds((tiles, heads, SEG, SEG), BF16),
            sds((rows, d), BF16),
        ),
        (WHOLE,) * 5,
        [SMEM] + [WHOLE] * 3 + [ANY] * len(w),
        [VMEM((1, d, d), BF16), DMA((8,))],
        us=0.01,
    )(blk, zl, onehot, nv, *w)


def cross_mlp(blk, c, a0, a1, nv, w):
    rows, d = c.shape

    def body(blk_ref, c_ref, a0_ref, a1_ref, nv_ref, *refs):
        y_ref, n_ref, r_ref, gb_ref, gp_ref, m_ref, w_s, sems = refs[len(w) :]
        cp = Copies(sems)
        fetch_cross(cp, refs[: len(w)], blk_ref, w_s)
        n, r = norm_parts(c_ref[...] + (a0_ref[...].astype(F32) + a1_ref[...].astype(F32)))
        n_ref[...] = n
        r_ref[...] = r
        y = n * nv_ref[2:3] + nv_ref[6:7]
        y_ref[...] = y
        cp.wait_all()
        g, gd = gelu_both(nn(y.astype(BF16), w_s[0]))
        gb_ref[...] = g.astype(BF16)
        gp_ref[...] = gd.astype(BF16)
        m_ref[...] = nt(gb_ref[...], w_s[1]).astype(BF16)

    return call(
        body,
        (
            sds((rows, d), F32),
            sds((rows, d), F32),
            sds((rows, 1), F32),
            sds((rows, d), BF16),
            sds((rows, d), BF16),
            sds((rows, d), BF16),
        ),
        (WHOLE,) * 6,
        [SMEM] + [WHOLE] * 4 + [ANY] * len(w),
        [VMEM((2, d, d), BF16), DMA((16,))],
        us=4,
    )(blk, c, a0, a1, nv, *w)


def cross_mlp_back(slots, blocked, blk, y, m0, m1, cot, nv, gb, gp, w):
    rows, d = y.shape
    own = d // slots if blocked else d

    def body(blk_ref, y_ref, m0_ref, m1_ref, cot_ref, nv_ref, gb_ref, gp_ref, *refs):
        (e_ref, dh_ref, gd_out, gu_out, dy_ref, sums_ref, w_s, gd, gu, sems) = refs[len(w) :]
        cp = Copies(sems)
        got = fetch_cross(cp, refs[: len(w)], blk_ref, w_s)
        gain = nv_ref[3:4]
        n, r = norm_parts(y_ref[...] + (m0_ref[...].astype(F32) + m1_ref[...].astype(F32)))
        e_ref[...] = (n * gain + nv_ref[7:8]).astype(BF16)
        grad = cot_ref[...].astype(F32)
        sums_ref[...] = sums_of(grad, n)
        dh = norm_back(grad, n, r, gain)
        dh_ref[...] = dh
        dm = dh.astype(BF16)
        cp.wait(*got)
        du = (nn(dm, w_s[1]) * gp_ref[...].astype(F32)).astype(BF16)
        dy_ref[...] = nt(du, w_s[0]).astype(BF16)
        gd[...] = tn(dm, gb_ref[...])
        own_rows(cp, blocked, blk_ref, gd, gd_out)
        gu[...] = tn(y_ref[...].astype(BF16), du)
        own_rows(cp, blocked, blk_ref, gu, gu_out)
        cp.wait_all()

    return call(
        body,
        (
            sds((rows, d), BF16),
            sds((rows, d), F32),
            sds((own, d), F32),
            sds((own, d), F32),
            sds((rows, d), BF16),
            sds((8, d), F32),
        ),
        (WHOLE, WHOLE, ANY, ANY, WHOLE, WHOLE),
        [SMEM] + [WHOLE] * 7 + [ANY] * len(w),
        [VMEM((2, d, d), BF16), VMEM((d, d), F32), VMEM((d, d), F32), DMA((18,))],
        us=30,
    )(blk, y, m0, m1, cot, nv, gb, gp, *w)


def cross_attn_back(slots, blocked, blk, dh2, d0, d1, n1, r1, c, qkv, o, p, nv, w):
    rows, d = dh2.shape
    quarter = d // 4
    heads = quarter // HEAD
    own = d // slots if blocked else d

    def body(blk_ref, dh2_ref, d0_ref, d1_ref, n_ref, r_ref, c_ref, qkv_ref, o_ref, p_ref, nv_ref,
             *refs):
        dh_ref, dx_ref, g_out, sums_ref, da_s, dqkv_s, w_s, g, sems = refs[len(w) :]
        cp = Copies(sems)
        got = fetch_cross(cp, refs[: len(w)], blk_ref, w_s)
        grad = dh2_ref[...] + (d0_ref[...].astype(F32) + d1_ref[...].astype(F32))
        n = n_ref[...]
        sums_ref[...] = sums_of(grad, n)
        dh = norm_back(grad, n, r_ref[...], nv_ref[2:3])
        dh_ref[...] = dh
        da_s[...] = dh.astype(BF16)
        cp.wait(*got)
        for t, at in enumerate(row_tiles(rows, SEG)):
            do = nn(da_s[at], w_s[0, :, 3 * quarter :]).astype(BF16)
            qkv_t = qkv_ref[at]
            cut = [
                [qkv_t[:, i * quarter + h * HEAD : i * quarter + (h + 1) * HEAD] for i in range(3)]
                for h in range(heads)
            ]
            dos = [do[:, h * HEAD : (h + 1) * HEAD] for h in range(heads)]
            dss = []
            for h in range(heads):
                pf = p_ref[t, h].astype(F32)
                pd = pf * nt(dos[h], cut[h][2])
                dss.append((pd - pf * jnp.sum(pd, axis=-1, keepdims=True)).astype(BF16))
            dq, dk, dv = [], [], []
            for h in range(heads):
                dv.append(tn(p_ref[t, h], dos[h]).astype(BF16))
                dq.append((nn(dss[h], cut[h][1]) * SCALE).astype(BF16))
                dk.append((tn(dss[h], cut[h][0]) * SCALE).astype(BF16))
            dqkv_s[at] = jnp.concatenate(dq + dk + dv, axis=1)
        dx_ref[...] = nt(dqkv_s[...], w_s[0, :, : 3 * quarter]).astype(BF16)
        g[:, : 3 * quarter] = tn(c_ref[...].astype(BF16), dqkv_s[...])
        g[:, 3 * quarter :] = tn(da_s[...], o_ref[...])
        own_rows(cp, blocked, blk_ref, g, g_out)
        cp.wait_all()

    return call(
        body,
        (sds((rows, d), F32), sds((rows, d), BF16), sds((own, d), F32), sds((8, d), F32)),
        (WHOLE, WHOLE, ANY, WHOLE),
        [SMEM] + [WHOLE] * 10 + [ANY] * len(w),
        [
            VMEM((rows, d), BF16),
            VMEM((rows, 3 * quarter), BF16),
            VMEM((1, d, d), BF16),
            VMEM((d, d), F32),
            DMA((9,)),
        ],
        us=5,
    )(blk, dh2, d0, d1, n1, r1, c, qkv, o, p, nv, *w)


def swap(axis, size, bit, value):
    return lax.ppermute(value, axis, [(i, i ^ bit) for i in range(size)])


core_swap = functools.partial(swap, "tensor", 4, 1)
y_swap = functools.partial(swap, "tensor", 4, 2)
x_swap = functools.partial(swap, "dp", 8, 1)


def z_swap(k, value):
    return swap("dp", 8, 2 * k, value)


def tied(*trees):
    return lax.optimization_barrier(trees)


PLANES = ((0, 0), (0, 1), (1, 0))
ATTN_PIECES = (
    [(n, (), 0, y, x, 0) for n, (y, x) in enumerate(PLANES)]
    + [(3 + n, (k - 1,), 0, y, x, k) for n, (y, x) in enumerate(PLANES) for k in (1, 2, 3)]
    + [(6, (k,), 0, 1, 1, k) for k in (0, 1)]
    + [(7, (k - 2,), 0, 1, 1, k) for k in (2, 3)]
)
MLP_PIECES = (
    [(n, (), 1, y, x, 0) for n, (y, x) in enumerate(PLANES)]
    + [(3 + n, (k - 1,), 0, y, x, k) for n, (y, x) in enumerate(PLANES) for k in (1, 2, 3)]
    + [(6, (k,), 0, 1, 1, k) for k in (0, 1)]
    + [(7, (k - 2,), 0, 1, 1, k) for k in (2, 3)]
)


def both_cores(pieces, count):
    return [
        (count * c + which, lead, pack, 2 * c + y, 4 * x + z)
        for c in range(2)
        for which, lead, pack, y, x, z in pieces
    ]


PLAIN_PLAN = [(0, (j,), 0, j, None) for j in range(4)]


def xor_order(stacked, index, bits):
    shape = stacked.shape
    out = stacked.reshape((2,) * bits + shape[1:])
    for b in range(bits):
        out = jnp.where((index >> (bits - 1 - b)) & 1 == 1, jnp.flip(out, b), out)
    return out.reshape(shape)


def add(*parts):
    total = parts[0].astype(F32)
    for p in parts[1:]:
        total = total + p.astype(F32)
    return total


def low_add(*parts):
    return add(*parts).astype(BF16)


class Scatter:
    def __init__(self, g0, g1_swapped):
        self.g = (g0, g1_swapped)

    def own(self, y, x, zs):
        return tuple(g[y, x, zs] for g in self.g)

    def diagonal(self):
        return low_add(*self.own(1, 1, slice(0, 2))), low_add(*self.own(1, 1, slice(2, 4)))

    def columns(self, from_x, from_y):
        lo, hi = slice(0, 2), slice(2, 4)
        to_x = jnp.concatenate([low_add(*self.own(0, 1, lo)), low_add(*self.own(0, 1, hi), from_y)])
        to_y = jnp.concatenate([low_add(*self.own(1, 0, lo), from_x), low_add(*self.own(1, 0, hi))])
        return to_x, to_y

    def planes(self, from_x, from_y):
        self.mine = (*self.own(0, 0, 0), from_x[0], from_y[0])
        return [low_add(*self.own(0, 0, k), from_x[k], from_y[k]) for k in (1, 2, 3)]

    def last(self, back):
        return add(*self.mine, *back)


def body(tokens, w_qkv, w_out, w_up, w_down, norm_gain, norm_bias, seg_table, seg_ids, cotangent):
    nd, ntens = lax.axis_size("dp"), lax.axis_size("tensor")
    fast = nd == 8
    di, ti = lax.axis_index("dp"), lax.axis_index("tensor")
    seqs, toks, d = tokens.shape
    rows, dblk = seqs * toks, tokens.shape[2] // nd
    per_dev = toks // SEG
    x = tokens.reshape(rows, d)
    cot = cotangent.reshape(rows, d)

    def pack(b):
        return (
            jnp.concatenate([w_qkv[b].reshape(dblk, -1), w_out[b].T], axis=1),
            jnp.stack([w_up[b], w_down[b].T]),
        )

    attn0, mlp0 = pack(0)
    attn1, mlp1 = pack(1)
    small = jnp.concatenate(
        [norm_gain.reshape(4, dblk), norm_bias.reshape(4, dblk), seg_table], axis=0
    )
    onehot = (seg_ids.reshape(-1, 1) == jnp.arange(128, dtype=jnp.int32)).astype(BF16)

    p3 = jnp.concatenate([attn1[None], mlp1])

    def place(leaders):
        leaders = leaders.reshape(seqs, per_dev, -1)
        space = jnp.zeros((seqs, per_dev * ntens, leaders.shape[-1]), BF16)
        return lax.dynamic_update_slice(space, leaders, (0, per_dev * ti, 0)).reshape(
            -1, leaders.shape[-1]
        )

    if fast:
        zi, xi = di // 2, di % 2
        blk = jnp.stack([(zi ^ k) * 2 + (xi ^ l) for l in range(2) for k in range(4)]).astype(jnp.int32)

        def z_all(p):
            return [z_swap(k, p) for k in (1, 2, 3)]

        tiny = jnp.pad(small, ((0, 0), (0, d - dblk)))
        p_all = jnp.concatenate([attn0, mlp0.reshape(-1, d), tiny])
        z1, x0, y0 = z_all(p_all[:dblk]), x_swap(p_all), y_swap(p_all)
        z1, x0, y0, pm = tied(z1, x0, y0, p_all[dblk:])
        c1 = jnp.stack(z1)
        xc1, yc1 = x_swap(c1), y_swap(c1)
        zm = z_all(pm)
        xc1, yc1 = tied(xc1, yc1)
        ex1, ey1 = x_swap(jnp.stack([y0[:dblk], yc1[0]])), y_swap(xc1[1:])
        ex1, ey1, p3a = tied(ex1, ey1, p3[0])
        z3a = z_all(p3a)
        base = [p_all, x0, y0]
        base_core = [core_swap(v) for v in base]
        mine1 = [c1, xc1, yc1, ex1, ey1]
        attn_pieces = base + mine1 + base_core + [core_swap(v) for v in mine1]
        attn_plan = both_cores(ATTN_PIECES, 8)
        cm = jnp.stack(zm)
        xcm, ycm = x_swap(cm), y_swap(cm)
    else:
        blk = jnp.zeros((8,), jnp.int32)

        def whole(p):
            g = lax.all_gather(p, ("tensor", "dp"), axis=0)
            g = g.reshape(ntens, nd, p.shape[0], dblk, d).transpose(0, 2, 1, 3, 4)
            g = g.reshape(ntens, p.shape[0] * d, d)
            return xor_order(g, ti, 2)

        attn_pieces, mlp_pieces = [whole(attn0[None])], [whole(mlp0)]
        attn_plan = mlp_plan = PLAIN_PLAN
        w1 = lax.all_gather(p3, "dp", axis=1, tiled=True)
        w1a, w1m = [w1[:1]], [w1[1:]]
        nv = lax.all_gather(small, "dp", axis=1, tiled=True).astype(F32)
    w_a, qkv, o, p, n1, r1, n_first = attn_forward(attn_plan, blk, x, attn_pieces)

    if fast:
        n_first, z3a = tied(n_first, z3a)
    narrow = d + onehot.shape[1]
    pay = place(jnp.concatenate([n_first[:, 0], onehot, cot.reshape(-1, SEG, d)[:, 0]], axis=1))
    if fast:
        pay = pay + core_swap(pay)
        pay = pay + y_swap(pay)
        xcm, ycm, pay = tied(xcm, ycm, pay)
        p3u, p3d, pay = p3[1], jnp.concatenate([p3[2], pay[:, narrow:]]), pay[:, :narrow]
        to_x, to_y, p3u = tied(jnp.stack([y0[dblk:], ycm[0]]), xcm[1:], p3u)
        ex2, ey2 = x_swap(to_x), y_swap(to_y)
        z3u = z_all(p3u)
        pay = jnp.stack([pay, x_swap(pay)])
        at = 3 * dblk
        tiny = jnp.stack(
            [jnp.stack([p_all[at:], x0[at:]])]
            + [jnp.stack([a[2 * dblk :], b[2 * dblk :]]) for a, b in zip(zm, xcm)]
        )[..., :dblk]
        nv = xor_order(tiny.reshape(nd, 16, dblk), di, 3)
        nv = nv.transpose(1, 0, 2).reshape(16, d).astype(F32)
        w1a = jnp.stack([p3a] + z3a)
        ex2, ey2 = tied(ex2, ey2)
        ex2, ey2, pay, z3u, p3d, w1a, nv = tied(ex2, ey2, pay, z3u, p3d, w1a, nv)
        mine2 = [cm, xcm, ycm, ex2, ey2]
        mlp_pieces = base + mine2 + base_core + [core_swap(v) for v in mine2]
        mlp_plan = both_cores(MLP_PIECES, 8)
        pay = jnp.stack([pay] + z_all(pay))
        first = 0
        z3d = z_all(p3d)
        w1a = [w1a, x_swap(w1a)]
    else:
        pay = lax.all_gather(lax.psum(pay, "tensor"), "dp", axis=0)
        first = di * seqs * per_dev * ntens
    pay = pay.reshape(-1, pay.shape[-1])
    lead_n, lead_hot = pay[:, :d], pay[:, d:narrow]
    if not fast:
        lead_cot = pay[:, narrow:]

    wu, wd, ybl, gbl, gpl, zl, nl, rl = lead_forward(mlp_plan, blk, lead_n, nv, mlp_pieces)
    if fast:
        z3d, zl, w1a = tied(z3d, zl, w1a)
        w1m = jnp.stack([jnp.concatenate(v) for v in zip([p3u] + z3u, [p3d] + z3d)])
        w1m = [w1m, x_swap(w1m)]
        lead_cot = jnp.stack(w1m, axis=1)[:, :, 2 * dblk :].reshape(-1, d)

    def near_sum(part):
        if fast:
            return low_add(part, core_swap(part))
        return lax.psum(part.astype(F32), "tensor")

    def far_sum(half):
        return y_swap(half) if fast else jnp.zeros_like(half)

    c, cqkv, co, cp, ca = cross_attn(blk, zl, lead_hot, nv, w1a)
    s1 = near_sum(ca)
    t1 = far_sum(s1)
    n2, s1 = tied(n1, s1)
    gb, gp, yb, dm, g1, dy, result, sums2 = mlp_forward(nd, fast, blk, n2, cot, nv, wu, wd)
    t1, sums2, w1m = tied(t1, sums2, w1m)
    cy, cn, cr, cgb, cgp, cm = cross_mlp(blk, c, s1, t1, nv, w1m)
    s2 = near_sum(cm)
    t2 = far_sum(s2)
    dm, s2 = tied(dm, s2)
    g0, dy = mlp_backward(nd, fast, blk, dm, yb, gb, gp, wu, wd, dy)
    t2, dy = tied(t2, dy)
    e, cdh2, cgd, cgu, cdy, csum2 = cross_mlp_back(
        nd, fast, blk, cy, s2, t2, lead_cot, nv, cgb, cgp, w1m
    )
    if fast:

        def shards(g):
            return g.reshape(2, 2, 4, *g.shape[2:])

        other_m, cdy = tied(core_swap(shards(g1)), cdy)
    s3 = near_sum(cdy)
    t3 = far_sum(s3)
    if fast:
        sm_ = Scatter(shards(g0), other_m)
        ops = sm_.diagonal()
        diag = x_swap(ops[0]), y_swap(ops[1])
        t3 = tied(t3, ops)[0]
    t3, dy = tied(t3, dy)
    cdh, cdx, cga, csum1 = cross_attn_back(
        nd, fast, blk, cdh2, s3, t3, cn, cr, c, cqkv, co, cp, nv, w1a
    )
    s4 = near_sum(cdx)
    t4 = far_sum(s4)
    if fast:
        diag, s4 = tied(diag, s4)
        ops = sm_.columns(*diag)
        t4, ops = tied(t4, ops)
        cols = x_swap(ops[0]), y_swap(ops[1])
    def own_leaders(full):
        part = lax.dynamic_slice_in_dim(full, first, seqs * per_dev * ntens, 0)
        part = part.reshape(seqs, per_dev * ntens, d)
        return lax.dynamic_slice_in_dim(part, per_dev * ti, per_dev, 1).reshape(-1, d)

    lead = (cdh, s4, t4, lead_hot, nl, rl, ybl, gbl, gpl, wu, wd)
    if fast:
        spot = jnp.stack([s * per_dev * ntens + per_dev * ti + i for s in range(seqs) for i in range(per_dev)])
        first_in = (dy, spot.astype(jnp.int32), n1, r1, nv, sums2)
        a1, dx, da, sums, lgd, lgu, lsum = attn_backward(
            1, nd, fast, blk, x, qkv, o, p, w_a, first_in, None, lead
        )
    else:
        dyl, lgd, lgu, lsum = lead_backward(nd, fast, blk, nv, lead)
        first_in = (dy, own_leaders(dyl), n1, r1, nv, sums2)
        a1, dx, da, sums = attn_backward(1, nd, fast, blk, x, qkv, o, p, w_a, first_in, None)
    if fast:
        cols, dx = tied(cols, dx)
        ops = sm_.planes(*cols)
        dx, ops = tied(dx, ops)
        planes = [z_swap(kk, op) for kk, op in zip((1, 2, 3), ops)]
        other = core_swap(shards(a1))
    a0, dx = attn_backward(0, nd, fast, blk, x, qkv, o, p, w_a, None, (da, dx, sums))

    if fast:
        sa = Scatter(shards(a0), other)
        ops = sa.diagonal()
        ops, e, csum1, csum2, cga, cgu, cgd, lsum, lgd, lgu = tied(
            ops, e, csum1, csum2, cga, cgu, cgd, lsum, lgd, lgu
        )
        diag = x_swap(ops[0]), y_swap(ops[1])
        planes, diag = tied(planes, diag)
        ops = sa.columns(*diag)
        cols = x_swap(ops[0]), y_swap(ops[1])
        ops = sa.planes(*cols)
        gm = sm_.last(planes)
        ga = sa.last([z_swap(kk, op) for kk, op in zip((1, 2, 3), ops)])[0]
        norm_sums = ga[dblk : dblk + 8, :dblk]
        ga = ga[:dblk]
    else:

        def owned(lo, hi):
            g = jnp.concatenate([lo, hi])
            g = xor_order(g, ti, 2).astype(F32)
            g = lax.psum_scatter(g, "tensor", scatter_dimension=0)
            return lax.psum_scatter(g, "dp", scatter_dimension=1, tiled=True)

        gm, ga = owned(g0, g1), owned(a0, a1)[0]
        norm_sums = lax.psum_scatter(
            lax.psum(sums, "tensor"), "dp", scatter_dimension=1, tiled=True
        )

    def rows_of(full):
        if fast:
            return full
        return lax.dynamic_slice_in_dim(full, di * dblk, dblk, 0)

    def cols_of(full):
        return lax.dynamic_slice_in_dim(full, di * dblk, dblk, 1)

    gu0, gd0 = gm[0] + rows_of(lgu), gm[1] + rows_of(lgd)
    ga1, gu1, gd1 = rows_of(cga), rows_of(cgu), rows_of(cgd)
    wide = w_qkv.shape[3] * 3
    grad_qkv = jnp.stack([ga[:, :wide], ga1[:, :wide]]).reshape(w_qkv.shape)
    grad_out = jnp.stack([ga[:, wide:].T, ga1[:, wide:].T])
    grad_up = jnp.stack([gu0, gu1])
    grad_down = jnp.stack([gd0.T, gd1.T])
    lsum, csum1, csum2 = cols_of(lsum), cols_of(csum1), cols_of(csum2)
    grad_gain = jnp.stack(
        [
            jnp.stack([norm_sums[0], norm_sums[2] + lsum[0]]),
            jnp.stack([csum1[0], csum2[0]]),
        ]
    )
    grad_bias = jnp.stack(
        [
            jnp.stack([norm_sums[1], norm_sums[3] + lsum[1]]),
            jnp.stack([csum1[1], csum2[1]]),
        ]
    )
    result = result.reshape(-1, SEG, d).at[:, 0].set(own_leaders(e)).reshape(tokens.shape)
    return (
        result,
        dx.reshape(tokens.shape),
        grad_qkv,
        grad_out,
        grad_up,
        grad_down,
        grad_gain,
        grad_bias,
        lsum[8:16],
    )


def solution(mesh):
    return jax.shard_map(
        body,
        mesh=mesh,
        in_specs=(
            P("dp", "tensor", None),
            P(None, "dp", None, "tensor"),
            P(None, "tensor", "dp"),
            P(None, "dp", "tensor"),
            P(None, "tensor", "dp"),
            P(None, None, "dp"),
            P(None, None, "dp"),
            P(None, "dp"),
            P("dp", "tensor"),
            P("dp", "tensor", None),
        ),
        out_specs=(
            P("dp", "tensor", None),
            P("dp", "tensor", None),
            P(None, "dp", None, "tensor"),
            P(None, "tensor", "dp"),
            P(None, "dp", "tensor"),
            P(None, "tensor", "dp"),
            P(None, None, "dp"),
            P(None, None, "dp"),
            P(None, "dp"),
        ),
        check_vma=False,
    )
```
